32 devices in a mesh: batch: 8 (over z, y), proto: 4 (over x, core).
Axes of the slice: x: 2, y: 2, z: 4, core: 2. Of those that a mesh axis runs over, the one named last changes fastest.
Arguments:
- embeddings: bfloat16 [8192, 1024], P('batch'), may hold values from -6 to 6
- pairing: int32 [8192], P('batch'), may hold values from 0 to 1023, as said below
- w_in: bfloat16 [1024, 512], replicated, may hold values from -0.1875 to 0.1875
- w_out: bfloat16 [512, 128], replicated, may hold values from -0.25 to 0.25
- prototypes: bfloat16 [32768, 128], P('proto'), may hold values from -1.8 to 1.8
Outputs:
- grad_in: float32 [1024, 512], replicated
- grad_out: float32 [512, 128], replicated
- grad_proto: float32 [32768, 128], P('proto')
The draws below stay inside these ranges and needn't reach their ends.
Inputs may be any that keep to these rules, and one draw needn't show every extreme that they name: Within every aligned block of 1024 rows the views come in pairs: pairing[pairing[i]] = i and pairing[i] != i, both counted within the block.
All inputs are finite; a program needn't handle non-finite values.
Results may differ from the reference program's by a relative error of at most 0.007.
Values may be sent and summed in bfloat16 or wider, within the bound.
No kernel may reach another device: no remote copies, remote signals or barrier semaphores. Data moves between devices by JAX's collectives and lax.ppermute only.
A program may use at most 64 MiB of HBM per device.

```python
import math
import jax
import jax.numpy as jnp
from jax import lax

E = 1024
H = 512
Z = 128
K = 32768
R_DEV = 1024
ITERS = 3
ROWS = 8192


def draw_pairing(key, part):

    def one_block(block_key):
        order = jax.random.permutation(block_key, R_DEV).astype(jnp.int32)
        partners = order.reshape(R_DEV // 2, 2)[:, ::-1].reshape(R_DEV)
        return jnp.zeros((R_DEV,), jnp.int32).at[order].set(partners)
    keys = jax.random.split(jax.random.fold_in(key, 11), ROWS // R_DEV)
    return jax.vmap(one_block)(keys).reshape(ROWS).astype(jnp.int32)


def draw_prototypes(key, part):
    base_key = jax.random.fold_in(key, 23)
    first, second = jax.random.split(base_key)
    values = jnp.clip(jax.random.normal(first, (K, Z), jnp.float32), -6.0, 6.0)
    scale = jnp.exp(jax.random.uniform(second, (K, 1), jnp.float32, math.log(0.03), math.log(0.3)))
    return (values * scale).astype(jnp.bfloat16)


def block_levels(rng, dims, pieces, smallest, largest):
    def one(position, blocks):
        heights = jax.random.uniform(jax.random.fold_in(jax.random.fold_in(rng, 6), position), (blocks,), jnp.float32, smallest / len(pieces), largest / len(pieces))
        return jnp.repeat(jnp.exp(heights), dims[position] // blocks).reshape((-1,) + (1,) * (len(dims) - position - 1))

    gain = one(*pieces[0])
    for cut in pieces[1:]:
        gain = gain * one(*cut)
    return gain


def scatter_about(stream_key, extent, deviation, bound, cuts=(), kind=jnp.bfloat16):
    loudness = block_levels(stream_key, extent, cuts, -0.22, 0.18) if cuts else 1.0
    result = jax.random.normal(stream_key, extent, jnp.float32) * deviation * loudness
    return jnp.minimum(jnp.maximum(result, -bound), bound).astype(kind)


def setup_inputs(seed: int = 0) -> dict:
    seeds = jax.random.split(jax.random.key(seed), 6)
    return {
        "embeddings": scatter_about(seeds[0], (ROWS, E), 1.0, 6.0, ((0, 8),)),
        "pairing": draw_pairing(jax.random.fold_in(seeds[5], 71), 0),
        "w_in": scatter_about(seeds[2], (E, H), E ** -0.5, 0.1875),
        "w_out": scatter_about(seeds[3], (H, Z), H ** -0.5, 0.25),
        "prototypes": draw_prototypes(jax.random.fold_in(seeds[5], 71), 0),
    }


norm_eps = 1e-06
code_temp = 0.05
pred_temp = 0.1
loss_scale = 64.0

def head_forward(rows_in, w_in, w_out):
    pre_act = jnp.dot(rows_in, w_in, preferred_element_type=jnp.float32)
    hidden = jax.nn.gelu(pre_act).astype(jnp.bfloat16)
    raw_out = jnp.dot(hidden, w_out, preferred_element_type=jnp.float32)
    inv_norm = lax.rsqrt(lax.optimization_barrier(jnp.sum(raw_out * raw_out, axis=1, keepdims=True)) + norm_eps)
    return (pre_act, hidden, raw_out, inv_norm, (raw_out * inv_norm).astype(jnp.bfloat16))

def head_backward(rows_in, w_out, pre_act, hidden, raw_out, inv_norm, view_grad):
    along = lax.optimization_barrier(jnp.sum(raw_out * view_grad, axis=1, keepdims=True))
    d_raw = (inv_norm * view_grad - raw_out * (inv_norm * inv_norm * inv_norm) * along).astype(jnp.bfloat16)
    grad_out = lax.dot_general(hidden, d_raw, (((0,), (0,)), ((), ())), preferred_element_type=jnp.float32)
    d_hidden = lax.dot_general(d_raw, w_out, (((1,), (1,)), ((), ())), preferred_element_type=jnp.float32)
    _, pullback = jax.vjp(jax.nn.gelu, pre_act)
    d_pre = pullback(d_hidden)[0].astype(jnp.bfloat16)
    grad_in = lax.dot_general(rows_in, d_pre, (((0,), (0,)), ((), ())), preferred_element_type=jnp.float32)
    return (grad_in, grad_out)

def unit_rows(prototypes):
    proto_f = prototypes.astype(jnp.float32)
    proto_inv = lax.rsqrt(lax.optimization_barrier(jnp.sum(proto_f * proto_f, axis=1, keepdims=True)) + norm_eps)
    return (proto_f, proto_inv, (proto_f * proto_inv).astype(jnp.bfloat16))

def scores_of(rows_in, unit):
    return lax.dot_general(rows_in, unit, (((1,), (1,)), ((), ())), preferred_element_type=jnp.float32)

def reference(embeddings, pairing, w_in, w_out, prototypes):
    pre_act, hidden, raw_out, inv_norm, views = head_forward(embeddings, w_in, w_out)
    proto_f, proto_inv, unit = unit_rows(prototypes)
    block_rows = min(R_DEV, 512)
    count = ROWS // block_rows
    offsets = jnp.arange(ROWS, dtype=jnp.int32) // R_DEV * R_DEV
    mate_index = (offsets + pairing).astype(jnp.int32)
    mates = views[mate_index]
    view_blocks = views.reshape(count, block_rows, Z)
    row_scale = jnp.ones((ROWS,), jnp.float32)
    col_scale = jnp.ones((K,), jnp.float32)
    for sweep in range(ITERS):

        def add_columns(running, pair):
            block, scale = pair
            found = lax.optimization_barrier(jnp.sum(scale[:, None] * jnp.exp(scores_of(block, unit) / code_temp), axis=0))
            return (running + found, None)
        col_total, _ = lax.scan(add_columns, jnp.zeros((K,), jnp.float32), (view_blocks, row_scale.reshape(count, block_rows)))
        col_scale = 1.0 / col_total

        def add_rows(block, col_scale=col_scale):
            return lax.optimization_barrier(jnp.sum(jnp.exp(scores_of(block, unit) / code_temp) * col_scale[None, :], axis=1))
        row_scale = (1.0 / lax.map(add_rows, view_blocks)).reshape(ROWS)

    def add_totals(block):
        return lax.optimization_barrier(jnp.sum(jnp.exp(scores_of(block, unit) / pred_temp), axis=1))
    totals = lax.map(add_totals, view_blocks).reshape(ROWS)
    mate_scale = row_scale[mate_index]

    def finish(running, pair):
        block, mate_block, mate_row, total = pair
        scores = scores_of(block, unit)
        mate_scores = scores_of(mate_block, unit)
        predicted = jnp.exp(scores / pred_temp) / total[:, None]
        codes = mate_row[:, None] * jnp.exp(mate_scores / code_temp) * col_scale[None, :]
        d_scores = ((predicted - codes) * (loss_scale / pred_temp)).astype(jnp.bfloat16)
        view_part = jnp.dot(d_scores, unit, preferred_element_type=jnp.float32)
        running = running + lax.dot_general(d_scores, block, (((0,), (0,)), ((), ())), preferred_element_type=jnp.float32)
        return (running, view_part)
    unit_grad, view_parts = lax.scan(finish, jnp.zeros((K, Z), jnp.float32), (view_blocks, mates.reshape(count, block_rows, Z), mate_scale.reshape(count, block_rows), totals.reshape(count, block_rows)))
    view_grad = view_parts.reshape(ROWS, Z)
    along = lax.optimization_barrier(jnp.sum(proto_f * unit_grad, axis=1, keepdims=True))
    grad_proto = proto_inv * unit_grad - proto_f * (proto_inv * proto_inv * proto_inv) * along
    grad_in, grad_out = head_backward(embeddings, w_out, pre_act, hidden, raw_out, inv_norm, view_grad)
    return (grad_in, grad_out, grad_proto)
```

```python
import functools
import math

import jax
import jax.numpy as jnp
from jax import lax
from jax.experimental import pallas as pl
from jax.experimental.pallas import tpu as pltpu
from jax.sharding import PartitionSpec as P

ITERS = 3
norm_eps = 1e-06
code_temp = 0.05
pred_temp = 0.1
loss_scale = 64.0
GRAD_SCALE = loss_scale / pred_temp
EXP2_SCALE = math.log2(math.e) / pred_temp
GELU_K = math.sqrt(2.0 / math.pi)
GELU_A = 0.044715

f32 = jnp.float32
bf16 = jnp.bfloat16
NN = (((1,), (0,)), ((), ()))
NT = (((1,), (1,)), ((), ()))
TN = (((0,), (0,)), ((), ()))
VMEM_LIMIT = 56 * 1024 * 1024


def dot(a, b, dims=NN):
    return lax.dot_general(a, b, dims, preferred_element_type=f32)


def params(*semantics):
    return pltpu.CompilerParams(
        dimension_semantics=semantics or None, vmem_limit_bytes=VMEM_LIMIT
    )


def split_rows(vec):
    hi = vec.astype(bf16)
    lo = (vec - hi.astype(f32)).astype(bf16)
    n = vec.shape[1]
    row = lax.broadcasted_iota(jnp.int32, (8, n), 0)
    hi8 = jnp.broadcast_to(hi.astype(f32), (8, n))
    lo8 = jnp.broadcast_to(lo.astype(f32), (8, n))
    return jnp.where(row == 0, hi8, jnp.where(row == 1, lo8, 0.0)).astype(bf16)


def to_column(vec):
    n = vec.shape[1]
    return jnp.broadcast_to(vec, (8, n)).T[:, :1]


def swap_lanes(x):
    half = x.shape[1] // 2
    return jnp.concatenate([x[:, half:], x[:, :half]], axis=1)


def swap_rows(x):
    half = x.shape[0] // 2
    return jnp.concatenate([x[half:], x[:half]], axis=0)


def full(shape):
    return pl.BlockSpec(shape, lambda *_: (0,) * len(shape))


def head_kernel(emb, pairing, w_in, w_out, pre, hid, raw, views, views_t, pos, scratch):
    step = pl.program_id(0)
    rows = emb.shape[0]
    pre_act = dot(emb[...], w_in[...])
    pre[...] = pre_act
    t = jnp.tanh(GELU_K * (pre_act + GELU_A * (pre_act * pre_act * pre_act)))
    hidden = (0.5 * pre_act * (1.0 + t)).astype(bf16)
    hid[...] = hidden
    raw_out = dot(hidden, w_out[...])
    raw[...] = raw_out
    inv = lax.rsqrt(jnp.sum(raw_out * raw_out, axis=1, keepdims=True) + norm_eps)
    scratch[pl.ds(pl.multiple_of(step * rows, rows), rows), :] = (raw_out * inv).astype(bf16)

    @pl.when(step == pl.num_programs(0) - 1)
    def _():
        mate = pairing[...]
        n = mate.shape[1]
        lane = lax.broadcasted_iota(jnp.int32, (1, n), 1)
        first = lane < mate
        low = jnp.minimum(lane, mate)
        sub = lax.broadcasted_iota(jnp.int32, (n, n), 0)
        before = jnp.where(sub < low, 1.0, 0.0).astype(bf16)
        first8 = jnp.broadcast_to(jnp.where(first, 1.0, 0.0), (8, n)).astype(bf16)
        rank = dot(first8, before)[:1].astype(jnp.int32)
        place = jnp.where(first, rank, rank + n // 2)
        pos[...] = place
        move = jnp.where(sub == place, 1.0, 0.0).astype(bf16)
        ordered = dot(move, scratch[...])
        views[...] = ordered.astype(bf16)
        views_t[...] = ordered.T.astype(bf16)


def head(embeddings, pairing, w_in, w_out):
    rows, wide = embeddings.shape
    hidden = w_in.shape[1]
    depth = w_out.shape[1]
    steps = 4
    block = rows // steps
    return pl.pallas_call(
        head_kernel,
        grid=(steps,),
        in_specs=[
            pl.BlockSpec((block, wide), lambda i: (i, 0)),
            full((1, rows)),
            full((wide, hidden)),
            full((hidden, depth)),
        ],
        out_specs=[
            pl.BlockSpec((block, hidden), lambda i: (i, 0)),
            pl.BlockSpec((block, hidden), lambda i: (i, 0)),
            pl.BlockSpec((block, depth), lambda i: (i, 0)),
            full((rows, depth)),
            full((depth, rows)),
            full((1, rows)),
        ],
        out_shape=[
            jax.ShapeDtypeStruct((rows, hidden), f32),
            jax.ShapeDtypeStruct((rows, hidden), bf16),
            jax.ShapeDtypeStruct((rows, depth), f32),
            jax.ShapeDtypeStruct((rows, depth), bf16),
            jax.ShapeDtypeStruct((depth, rows), bf16),
            jax.ShapeDtypeStruct((1, rows), jnp.int32),
        ],
        scratch_shapes=[pltpu.VMEM((rows, depth), bf16)],
        compiler_params=params("arbitrary"),
        name="head",
    )(embeddings, pairing.reshape(1, rows), w_in, w_out)


def unit_of(protos):
    proto_f = protos.astype(f32)
    inv = lax.rsqrt(jnp.sum(proto_f * proto_f, axis=1, keepdims=True) + norm_eps)
    return proto_f, inv, proto_f * inv


def first_kernel(chunk, views, protos, expo, unit_t, col, tot, along, tot_acc, along_acc):
    step = pl.program_id(0)
    rows, depth = views.shape

    @pl.when(step == 0)
    def _():
        tot_acc[...] = jnp.zeros_like(tot_acc)
        along_acc[...] = jnp.zeros_like(along_acc)

    _, _, unit = unit_of(protos[...])
    unit16 = unit.astype(bf16)
    unit_tr = unit.T.astype(bf16)
    unit_t[...] = unit_tr
    width = unit.shape[0]
    running = jnp.zeros((8, width), f32)
    for start in range(0, rows, chunk):
        part = pl.ds(start, chunk)
        scores = dot(views[part, :], unit_tr)
        soft = jnp.exp2(scores * EXP2_SCALE)
        hard = soft * soft
        expo[part, :] = hard.astype(bf16)
        running = running + jnp.sum(hard.reshape(chunk // 8, 8, width), axis=0)
        lanes = soft[:, :128]
        for k in range(1, width // 128):
            lanes = lanes + soft[:, k * 128 : (k + 1) * 128]
        tot_acc[part, :] += lanes
        along_acc[part, :] += dot(soft.astype(bf16), unit16)
    col[...] = jnp.sum(running, axis=0, keepdims=True)

    @pl.when(step == pl.num_programs(0) - 1)
    def _():
        tot[...] = jnp.sum(tot_acc[...].T, axis=0, keepdims=True)
        along[...] = along_acc[...]


def first_pass(views, protos):
    rows, depth = views.shape
    width = protos.shape[0]
    block = min(512, width)
    chunk = min(256, rows)
    return pl.pallas_call(
        functools.partial(first_kernel, chunk),
        grid=(width // block,),
        in_specs=[full((rows, depth)), pl.BlockSpec((block, depth), lambda j: (j, 0))],
        out_specs=[
            pl.BlockSpec((rows, block), lambda j: (0, j)),
            pl.BlockSpec((depth, block), lambda j: (0, j)),
            pl.BlockSpec((1, block), lambda j: (0, j)),
            full((1, rows)),
            full((rows, depth)),
        ],
        out_shape=[
            jax.ShapeDtypeStruct((rows, width), bf16),
            jax.ShapeDtypeStruct((depth, width), bf16),
            jax.ShapeDtypeStruct((1, width), f32),
            jax.ShapeDtypeStruct((1, rows), f32),
            jax.ShapeDtypeStruct((rows, depth), f32),
        ],
        scratch_shapes=[pltpu.VMEM((rows, 128), f32), pltpu.VMEM((rows, depth), f32)],
        compiler_params=params("arbitrary"),
        name="first_pass",
    )(views, protos)


def rowsum_kernel(count, last, *refs):
    expo = refs[0]
    parts = refs[1 : 1 + count]
    if last:
        unit_t, scale, out, code, acc = refs[1 + count :]
    else:
        scale, out, acc = refs[1 + count :]
    step = pl.program_id(0)

    @pl.when(step == 0)
    def _():
        acc[...] = jnp.zeros_like(acc)

    total = parts[0][...]
    for other in parts[1:]:
        total = total + other[...]
    inverse = 1.0 / total
    scale[...] = inverse
    weights = split_rows(inverse)
    if last:
        scaled = (unit_t[...].astype(f32) * inverse).astype(bf16)
        pad = jnp.zeros((128 - 8, weights.shape[1]), bf16)
        weights = jnp.concatenate([scaled, weights, pad], axis=0)
    acc[...] += dot(expo[...], weights, NT)

    @pl.when(step == pl.num_programs(0) - 1)
    def _():
        depth = acc.shape[1] - 128 if last else 0
        sums = acc[:, depth:] if last else acc[...]
        sums = sums.T
        out[...] = sums[0:1] + sums[1:2]
        if last:
            code[...] = acc[:, :depth]


def rowsum(expo, parts, unit_t=None):
    rows, width = expo.shape
    block = min(1024, width)
    last = unit_t is not None
    vec = pl.BlockSpec((1, block), lambda j: (0, j))
    in_specs = [pl.BlockSpec((rows, block), lambda j: (0, j))] + [vec] * len(parts)
    out_specs = [vec, full((1, rows))]
    out_shape = [jax.ShapeDtypeStruct((1, width), f32), jax.ShapeDtypeStruct((1, rows), f32)]
    operands = [expo, *parts]
    lanes = 8
    if last:
        depth = unit_t.shape[0]
        in_specs.append(pl.BlockSpec((depth, block), lambda j: (0, j)))
        operands.append(unit_t)
        out_specs.append(full((rows, depth)))
        out_shape.append(jax.ShapeDtypeStruct((rows, depth), f32))
        lanes = depth + 128
    return pl.pallas_call(
        functools.partial(rowsum_kernel, len(parts), last),
        grid=(width // block,),
        in_specs=in_specs,
        out_specs=out_specs,
        out_shape=out_shape,
        scratch_shapes=[pltpu.VMEM((rows, lanes), f32)],
        compiler_params=params("arbitrary"),
        name="rowsum_last" if last else "rowsum",
    )(*operands)


def colsum_kernel(expo, total, out):
    weights = split_rows(1.0 / total[...])
    sums = dot(weights, expo[...])
    out[...] = sums[0:1] + sums[1:2]


def colsum(expo, total):
    rows, width = expo.shape
    block = min(1024, width)
    return pl.pallas_call(
        colsum_kernel,
        grid=(width // block,),
        in_specs=[pl.BlockSpec((rows, block), lambda j: (0, j)), full((1, rows))],
        out_specs=pl.BlockSpec((1, block), lambda j: (0, j)),
        out_shape=jax.ShapeDtypeStruct((1, width), f32),
        compiler_params=params("arbitrary"),
        name="colsum",
    )(expo, total)


def proto_first_kernel(count, *refs):
    protos = refs[0]
    views = refs[1 : 1 + count]
    totals = refs[1 + count : 1 + 2 * count]
    expo, grad, weights = refs[1 + 2 * count :]
    rows = views[0].shape[1]

    @pl.when(pl.program_id(0) == 0)
    def _():
        for k in range(count):
            scale = GRAD_SCALE / totals[k][...]
            weights[:, k * rows : (k + 1) * rows] = (views[k][...].astype(f32) * scale).astype(bf16)

    _, _, unit = unit_of(protos[...])
    unit16 = unit.astype(bf16)
    running = jnp.zeros(grad.shape, f32)
    for k in range(count):
        part = pl.ds(k * rows, rows)
        soft = jnp.exp2(dot(unit16, views[k][...]) * EXP2_SCALE)
        expo[:, part] = (soft * soft).astype(bf16)
        running = running + dot(soft.astype(bf16), weights[:, part], NT)
    grad[...] = running


def proto_first(protos, views_t, totals):
    width, depth = protos.shape
    count = len(views_t)
    rows = views_t[0].shape[1]
    block = min(256, width)
    return pl.pallas_call(
        functools.partial(proto_first_kernel, count),
        grid=(width // block,),
        in_specs=[pl.BlockSpec((block, depth), lambda j: (j, 0))]
        + [full((depth, rows))] * count
        + [full((1, rows))] * count,
        out_specs=[
            pl.BlockSpec((block, count * rows), lambda j: (j, 0)),
            pl.BlockSpec((block, depth), lambda j: (j, 0)),
        ],
        out_shape=[
            jax.ShapeDtypeStruct((width, count * rows), bf16),
            jax.ShapeDtypeStruct((width, depth), f32),
        ],
        scratch_shapes=[pltpu.VMEM((depth, count * rows), bf16)],
        compiler_params=params("arbitrary"),
        name="proto_first",
    )(protos, *views_t, *totals)


def proto_last_kernel(count, *refs):
    expo, grad, scale, protos = refs[:4]
    views = refs[4 : 4 + count]
    totals = refs[4 + count : 4 + 2 * count]
    out, weights = refs[4 + 2 * count :]
    rows = views[0].shape[1]

    @pl.when(pl.program_id(0) == 0)
    def _():
        for k in range(count):
            mates = swap_lanes(views[k][...])
            weights[:, k * rows : (k + 1) * rows] = (
                mates.astype(f32) * (GRAD_SCALE / totals[k][...])
            ).astype(bf16)

    unit_grad = grad[...] - to_column(scale[...]) * dot(expo[...], weights[...], NT)
    proto_f, inv, _ = unit_of(protos[...])
    inner = jnp.sum(proto_f * unit_grad, axis=1, keepdims=True)
    out[...] = (inv * unit_grad - proto_f * (inv * inv * inv) * inner).astype(bf16)


def proto_last(expo, grad, scale, protos, views_t, totals):
    width, depth = protos.shape
    count = len(views_t)
    rows = views_t[0].shape[1]
    block = min(256, width)
    return pl.pallas_call(
        functools.partial(proto_last_kernel, count),
        grid=(width // block,),
        in_specs=[
            pl.BlockSpec((block, count * rows), lambda j: (j, 0)),
            pl.BlockSpec((block, depth), lambda j: (j, 0)),
            pl.BlockSpec((1, block), lambda j: (0, j)),
            pl.BlockSpec((block, depth), lambda j: (j, 0)),
        ]
        + [full((depth, rows))] * count
        + [full((1, rows))] * count,
        out_specs=pl.BlockSpec((block, depth), lambda j: (j, 0)),
        out_shape=jax.ShapeDtypeStruct((width, depth), bf16),
        scratch_shapes=[pltpu.VMEM((depth, count * rows), bf16)],
        compiler_params=params("arbitrary"),
        name="proto_last",
    )(expo, grad, scale, protos, *views_t, *totals)


def view_grad_kernel(along, code, tot, total, out):
    soft = along[...] * to_column(GRAD_SCALE / tot[...])
    hard = swap_rows(code[...] * to_column(GRAD_SCALE / total[...]))
    out[...] = (soft - hard).astype(out.dtype)


def view_grad_part(along, code, tot, total):
    return pl.pallas_call(
        view_grad_kernel,
        out_shape=jax.ShapeDtypeStruct(along.shape, bf16),
        compiler_params=params(),
        name="view_grad",
    )(along, code, tot, total)


def backward_kernel(count, grad_a, grad_b, pos, raw, hid, pre, emb, hid_part, w_out, g_in, g_out):
    total = grad_a[...].astype(f32) + grad_b[...].astype(f32)
    n, depth = raw.shape
    place = jnp.broadcast_to(pos[...].astype(f32), (8, n)).T[:, :1].astype(jnp.int32)
    lane = lax.broadcasted_iota(jnp.int32, (n, n), 1)
    move = jnp.where(lane == place, 1.0, 0.0).astype(bf16)
    hi = total.astype(bf16)
    lo = (total - hi.astype(f32)).astype(bf16)
    moved = dot(move, jnp.concatenate([hi, lo], axis=1))
    grad = moved[:, :depth] + moved[:, depth:]
    raw_out = raw[...]
    inv = lax.rsqrt(jnp.sum(raw_out * raw_out, axis=1, keepdims=True) + norm_eps)
    inner = jnp.sum(raw_out * grad, axis=1, keepdims=True)
    d_raw = (inv * grad - raw_out * (inv * inv * inv) * inner).astype(bf16)
    g_out[...] = dot(hid_part[...], d_raw, TN)
    d_hidden = dot(d_raw, w_out[...], NT)
    v = pre[...]
    t = jnp.tanh(GELU_K * (v + GELU_A * (v * v * v)))
    slope = 0.5 * (1.0 + t) + (0.5 * GELU_K) * v * (1.0 - t * t) * (1.0 + (3.0 * GELU_A) * (v * v))
    d_pre = (slope * d_hidden).astype(bf16)
    g_in[...] = dot(emb[...], d_pre, TN)


def backward(grad_a, grad_b, pos, raw, hid, pre, emb, hid_part, w_out):
    return pl.pallas_call(
        functools.partial(backward_kernel, 1),
        out_shape=[
            jax.ShapeDtypeStruct((emb.shape[1], pre.shape[1]), f32),
            jax.ShapeDtypeStruct((hid_part.shape[1], raw.shape[1]), f32),
        ],
        compiler_params=params(),
        name="backward",
    )(grad_a, grad_b, pos, raw, hid, pre, emb, hid_part, w_out)


def body(nb, npr, embeddings, pairing, w_in, w_out, prototypes):
    b = lax.axis_index("batch")
    p = lax.axis_index("proto")
    rows, wide = embeddings.shape
    width, depth = prototypes.shape
    hidden_n = w_in.shape[1]
    own = width // nb

    def shifted(x, s):
        return lax.ppermute(x, "batch", [(i, (i + s) % nb) for i in range(nb)])

    def everyone(x):
        return [x] + [shifted(x, s) for s in range(1, nb)]

    pre, hid, raw, views, views_t, pos = head(embeddings, pairing, w_in, w_out)
    views_all = everyone(views_t)
    expo, unit_t, col, tot, along = first_pass(views, prototypes)
    protos_own = lax.dynamic_slice_in_dim(prototypes, b * own, own, 0)

    scale, row = rowsum(expo, everyone(col))
    summed = lax.psum(jnp.concatenate([row, tot], axis=0), "proto")
    total, tot = summed[:1], summed[1:]
    expo_own, grad_own = proto_first(protos_own, views_all, everyone(tot))
    for sweep in range(1, ITERS):
        col = colsum(expo, total)
        if sweep < ITERS - 1:
            scale, row = rowsum(expo, everyone(col))
        else:
            scale, row, code = rowsum(expo, everyone(col), unit_t)
        total = lax.psum(row, "proto")

    scale_own = lax.dynamic_slice_in_dim(scale, b * own, own, 1)
    proto_part = proto_last(
        expo_own, grad_own, scale_own, protos_own, views_all, everyone(total)
    )
    grad_proto = lax.all_gather(proto_part, "batch", axis=0, tiled=True).astype(f32)

    part = view_grad_part(along, code, tot, total)
    step = 1
    other = jnp.zeros_like(part)
    while step < npr:
        other = lax.ppermute(part, "proto", [(i, i ^ step) for i in range(npr)])
        if step * 2 < npr:
            part = (part.astype(f32) + other.astype(f32)).astype(bf16)
        step *= 2
    emb_part = lax.dynamic_slice_in_dim(embeddings, p * (wide // npr), wide // npr, 1)
    hid_part = lax.dynamic_slice_in_dim(hid, p * (hidden_n // npr), hidden_n // npr, 1)
    g_in, g_out = backward(part, other, pos, raw, hid, pre, emb_part, hid_part, w_out)
    both = jnp.concatenate([g_in.reshape(nb, -1), g_out.reshape(nb, -1)], axis=1)
    both = lax.psum_scatter(both, "batch", scatter_dimension=0, tiled=True).astype(bf16)
    both = lax.all_gather(both, ("proto", "batch"), axis=0, tiled=True)
    cut = g_in.size // nb
    grad_in = both[:, :cut].astype(f32).reshape(wide, hidden_n)
    grad_out = both[:, cut:].astype(f32).reshape(hidden_n, depth)
    return (grad_in, grad_out, grad_proto)


def solution(mesh):
    return jax.shard_map(
        functools.partial(body, mesh.shape["batch"], mesh.shape["proto"]),
        mesh=mesh,
        in_specs=(P("batch", None), P("batch"), P(), P(), P("proto", None)),
        out_specs=(P(), P(), P("proto", None)),
        check_vma=False,
    )
```

```python
import functools
import math

import jax
import jax.numpy as jnp
from jax import lax
from jax.experimental import pallas as pl
from jax.experimental.pallas import tpu as pltpu
from jax.sharding import PartitionSpec as P

ITERS = 3
norm_eps = 1e-06
code_temp = 0.05
pred_temp = 0.1
loss_scale = 64.0
GRAD_SCALE = loss_scale / pred_temp
EXP2_SCALE = math.log2(math.e) / pred_temp
GELU_K = math.sqrt(2.0 / math.pi)
GELU_A = 0.044715

f32 = jnp.float32
bf16 = jnp.bfloat16
NN = (((1,), (0,)), ((), ()))
NT = (((1,), (1,)), ((), ()))
TN = (((0,), (0,)), ((), ()))
VMEM_LIMIT = 20 * 1024 * 1024


def dot(a, b, dims=NN):
    return lax.dot_general(a, b, dims, preferred_element_type=f32)


def params(*semantics):
    return pltpu.CompilerParams(
        dimension_semantics=semantics or None, vmem_limit_bytes=VMEM_LIMIT
    )


def to_column(vec):
    n = vec.shape[1]
    return jnp.broadcast_to(vec, (8, n)).T[:, :1]


def swap_lanes(x):
    half = x.shape[1] // 2
    return jnp.concatenate([x[:, half:], x[:, :half]], axis=1)


def swap_rows(x):
    half = x.shape[0] // 2
    return jnp.concatenate([x[half:], x[:half]], axis=0)


def full(shape):
    return pl.BlockSpec(shape, lambda *_: (0,) * len(shape))


def head_kernel(emb, pairing, w_in, w_out, pre, hid, raw, views, views_t, pos, scratch):
    step = pl.program_id(0)
    rows = emb.shape[0]
    pre_act = dot(emb[...], w_in[...])
    pre[...] = pre_act
    t = jnp.tanh(GELU_K * (pre_act + GELU_A * (pre_act * pre_act * pre_act)))
    hidden = (0.5 * pre_act * (1.0 + t)).astype(bf16)
    hid[...] = hidden
    raw_out = dot(hidden, w_out[...])
    raw[...] = raw_out
    inv = lax.rsqrt(jnp.sum(raw_out * raw_out, axis=1, keepdims=True) + norm_eps)
    scratch[pl.ds(pl.multiple_of(step * rows, rows), rows), :] = (raw_out * inv).astype(bf16)

    @pl.when(step == pl.num_programs(0) - 1)
    def _():
        mate = pairing[...]
        n = mate.shape[1]
        lane = lax.broadcasted_iota(jnp.int32, (1, n), 1)
        first = lane < mate
        low = jnp.minimum(lane, mate)
        sub = lax.broadcasted_iota(jnp.int32, (n, n), 0)
        before = jnp.where(sub < low, 1.0, 0.0).astype(bf16)
        first8 = jnp.broadcast_to(jnp.where(first, 1.0, 0.0), (8, n)).astype(bf16)
        rank = dot(first8, before)[:1].astype(jnp.int32)
        place = jnp.where(first, rank, rank + n // 2)
        pos[...] = place
        move = jnp.where(sub == place, 1.0, 0.0).astype(bf16)
        ordered = dot(move, scratch[...])
        views[...] = ordered.astype(bf16)
        views_t[...] = ordered.T.astype(bf16)


def head(embeddings, pairing, w_in, w_out):
    rows, wide = embeddings.shape
    hidden = w_in.shape[1]
    depth = w_out.shape[1]
    steps = 4
    block = rows // steps
    return pl.pallas_call(
        head_kernel,
        grid=(steps,),
        in_specs=[
            pl.BlockSpec((block, wide), lambda i: (i, 0)),
            full((1, rows)),
            full((wide, hidden)),
            full((hidden, depth)),
        ],
        out_specs=[
            pl.BlockSpec((block, hidden), lambda i: (i, 0)),
            pl.BlockSpec((block, hidden), lambda i: (i, 0)),
            pl.BlockSpec((block, depth), lambda i: (i, 0)),
            full((rows, depth)),
            full((depth, rows)),
            full((1, rows)),
        ],
        out_shape=[
            jax.ShapeDtypeStruct((rows, hidden), f32),
            jax.ShapeDtypeStruct((rows, hidden), bf16),
            jax.ShapeDtypeStruct((rows, depth), f32),
            jax.ShapeDtypeStruct((rows, depth), bf16),
            jax.ShapeDtypeStruct((depth, rows), bf16),
            jax.ShapeDtypeStruct((1, rows), jnp.int32),
        ],
        scratch_shapes=[pltpu.VMEM((rows, depth), bf16)],
        compiler_params=params("arbitrary"),
        name="head",
    )(embeddings, pairing.reshape(1, rows), w_in, w_out)


def unit_of(protos):
    proto_f = protos.astype(f32)
    inv = lax.rsqrt(jnp.sum(proto_f * proto_f, axis=1, keepdims=True) + norm_eps)
    return proto_f, inv, proto_f * inv


def in_vmem(x):
    return pltpu.with_memory_space_constraint(x, pltpu.VMEM)


WHOLE = pl.BlockSpec(memory_space=pltpu.VMEM)


def exp_pair(scores):
    soft = jnp.exp2(scores * EXP2_SCALE)
    return soft, soft * soft


def first_kernel(block, chunk, views, protos, expo, unit_t, col, tot, tot_acc):
    rows, depth = views.shape
    width = protos.shape[0]
    tot_acc[...] = jnp.zeros_like(tot_acc)

    def one(j, carry):
        here = pl.ds(pl.multiple_of(j * block, block), block)
        _, _, unit = unit_of(protos[here, :])
        unit_tr = unit.T.astype(bf16)
        unit_t[:, here] = unit_tr
        running = jnp.zeros((8, block), f32)
        for start in range(0, rows, chunk):
            part = pl.ds(start, chunk)
            soft, hard = exp_pair(dot(views[part, :], unit_tr))
            expo[part, here] = hard.astype(bf16)
            running = running + jnp.sum(hard.reshape(chunk // 8, 8, block), axis=0)
            lanes = soft[:, :128]
            for k in range(1, block // 128):
                lanes = lanes + soft[:, k * 128 : (k + 1) * 128]
            tot_acc[part, :] += lanes
        col[:, here] = jnp.sum(running, axis=0, keepdims=True)
        return carry

    lax.fori_loop(0, width // block, one, 0)
    tot[...] = jnp.sum(tot_acc[...].T, axis=0, keepdims=True)


def first_pass(views, protos):
    rows, depth = views.shape
    width = protos.shape[0]
    block = min(256, width)
    chunk = min(256, rows)
    return pl.pallas_call(
        functools.partial(first_kernel, block, chunk),
        in_specs=[WHOLE] * 2,
        out_specs=[WHOLE] * 4,
        out_shape=[
            pltpu.VMEM((rows, width), bf16),
            jax.ShapeDtypeStruct((depth, width), bf16),
            jax.ShapeDtypeStruct((1, width), f32),
            jax.ShapeDtypeStruct((1, rows), f32),
        ],
        scratch_shapes=[pltpu.VMEM((rows, 128), f32)],
        compiler_params=params(),
        name="first_pass",
    )(views, protos)


def rowsum_kernel(count, expo, *refs):
    parts = refs[:count]
    scale, out, spread, acc = refs[count:]
    rows, width = expo.shape
    total = jnp.sum(parts[0][...], axis=0, keepdims=True)
    for other in parts[1:]:
        total = total + other[...]
    inverse = 1.0 / total
    scale[...] = inverse
    spread[...] = jnp.broadcast_to(inverse, spread.shape).astype(bf16)
    tall = 64

    def one(i, carry):
        here = pl.ds(pl.multiple_of(i * tall, tall), tall)
        running = jnp.zeros((tall, 128), f32)
        for k in range(width // 128):
            lanes = slice(k * 128, (k + 1) * 128)
            weight = jnp.concatenate([spread[:, lanes]] * (tall // 16), axis=0)
            running = running + (expo[here, lanes] * weight).astype(f32)
        acc[here, :] = running
        return carry

    lax.fori_loop(0, rows // tall, one, 0)
    out[...] = jnp.sum(acc[...].T, axis=0, keepdims=True)


def rowsum(expo, parts):
    rows, width = expo.shape
    return pl.pallas_call(
        functools.partial(rowsum_kernel, len(parts)),
        in_specs=[WHOLE] * (1 + len(parts)),
        out_specs=[WHOLE] * 2,
        out_shape=[
            jax.ShapeDtypeStruct((1, width), f32),
            jax.ShapeDtypeStruct((1, rows), f32),
        ],
        scratch_shapes=[pltpu.VMEM((16, width), bf16), pltpu.VMEM((rows, 128), f32)],
        compiler_params=params(),
        name="rowsum",
    )(in_vmem(expo), *parts)


def colsum_kernel(count, expo, *refs):
    parts = refs[:count]
    out, spread = refs[count:]
    rows, width = expo.shape
    total = jnp.sum(parts[0][...], axis=0, keepdims=True)
    for other in parts[1:]:
        total = total + other[...]
    spread[...] = jnp.broadcast_to(1.0 / total, (128, rows)).T.astype(bf16)
    block = min(512, width)

    def one(j, carry):
        here = pl.ds(pl.multiple_of(j * block, block), block)
        running = jnp.zeros((16, block), f32)
        for i in range(rows // 16):
            part = slice(i * 16, (i + 1) * 16)
            weight = jnp.concatenate([spread[part, :]] * (block // 128), axis=1)
            running = running + (expo[part, here] * weight).astype(f32)
        out[:, here] = jnp.sum(running, axis=0, keepdims=True)
        return carry

    lax.fori_loop(0, width // block, one, 0)


def colsum(expo, parts):
    rows, width = expo.shape
    return pl.pallas_call(
        functools.partial(colsum_kernel, len(parts)),
        in_specs=[WHOLE] * (1 + len(parts)),
        out_specs=WHOLE,
        out_shape=jax.ShapeDtypeStruct((1, width), f32),
        scratch_shapes=[pltpu.VMEM((rows, 128), bf16)],
        compiler_params=params(),
        name="colsum",
    )(in_vmem(expo), *parts)


def proto_first_kernel(block, protos, views, totals, expo, grad, weights):
    count, depth, rows = views.shape
    for k in range(count):
        scale = GRAD_SCALE / totals[k]
        weights[:, k * rows : (k + 1) * rows] = (views[k].astype(f32) * scale).astype(bf16)

    def one(j, carry):
        here = pl.ds(pl.multiple_of(j * block, block), block)
        _, _, unit = unit_of(protos[here, :])
        unit16 = unit.astype(bf16)
        running = jnp.zeros((block, depth), f32)
        for k in range(count):
            part = slice(k * rows, (k + 1) * rows)
            soft, hard = exp_pair(dot(unit16, views[k]))
            expo[here, part] = hard.astype(bf16)
            running = running + dot(soft.astype(bf16), weights[:, part], NT)
        grad[here, :] = running
        return carry

    lax.fori_loop(0, protos.shape[0] // block, one, 0)


def proto_first(protos, views, totals):
    width, depth = protos.shape
    count, _, rows = views.shape
    block = min(256, width)
    return pl.pallas_call(
        functools.partial(proto_first_kernel, block),
        in_specs=[WHOLE] * 3,
        out_specs=[WHOLE] * 2,
        out_shape=[
            pltpu.VMEM((width, count * rows), bf16),
            jax.ShapeDtypeStruct((width, depth), f32),
        ],
        scratch_shapes=[pltpu.VMEM((depth, count * rows), bf16)],
        compiler_params=params(),
        name="proto_first",
    )(protos, views, totals)


def proto_last_kernel(block, expo, grad, scale, protos, views, totals, out, weights):
    count, depth, rows = views.shape
    for k in range(count):
        mates = swap_lanes(views[k])
        weights[:, k * rows : (k + 1) * rows] = (
            mates.astype(f32) * (GRAD_SCALE / totals[k])
        ).astype(bf16)

    def one(j, carry):
        here = pl.ds(pl.multiple_of(j * block, block), block)
        code = dot(expo[here, :], weights[...], NT)
        unit_grad = grad[here, :] - to_column(scale[:, here]) * code
        proto_f, inv, _ = unit_of(protos[here, :])
        inner = jnp.sum(proto_f * unit_grad, axis=1, keepdims=True)
        out[here, :] = (inv * unit_grad - proto_f * (inv * inv * inv) * inner).astype(bf16)
        return carry

    lax.fori_loop(0, protos.shape[0] // block, one, 0)


def proto_last(expo, grad, scale, protos, views, totals):
    width, depth = protos.shape
    count, _, rows = views.shape
    block = min(256, width)
    return pl.pallas_call(
        functools.partial(proto_last_kernel, block),
        in_specs=[WHOLE] * 6,
        out_specs=WHOLE,
        out_shape=jax.ShapeDtypeStruct((width, depth), bf16),
        scratch_shapes=[pltpu.VMEM((depth, count * rows), bf16)],
        compiler_params=params(),
        name="proto_last",
    )(in_vmem(expo), grad, scale, protos, views, totals)


def view_grad_kernel(block, views, unit_t, expo, scale, tot, total, out, soft_acc, hard_acc):
    rows, depth = views.shape
    width = expo.shape[1]
    soft_acc[...] = jnp.zeros_like(soft_acc)
    hard_acc[...] = jnp.zeros_like(hard_acc)

    def one(j, carry):
        here = pl.ds(pl.multiple_of(j * block, block), block)
        unit = unit_t[:, here]
        scaled = (unit.astype(f32) * scale[:, here]).astype(bf16)
        soft = jnp.exp2(dot(views[...], unit) * EXP2_SCALE).astype(bf16)
        soft_acc[...] += dot(soft, unit, NT)
        hard_acc[...] += dot(expo[:, here], scaled, NT)
        return carry

    lax.fori_loop(0, width // block, one, 0)
    soft = soft_acc[...] * to_column(GRAD_SCALE / tot[...])
    hard = swap_rows(hard_acc[...] * to_column(GRAD_SCALE / total[...]))
    out[...] = (soft - hard).astype(out.dtype)


def view_grad_part(views, unit_t, expo, scale, tot, total):
    rows, depth = views.shape
    block = min(512, expo.shape[1])
    return pl.pallas_call(
        functools.partial(view_grad_kernel, block),
        in_specs=[WHOLE] * 6,
        out_specs=WHOLE,
        out_shape=jax.ShapeDtypeStruct((rows, depth), bf16),
        scratch_shapes=[pltpu.VMEM((rows, depth), f32)] * 2,
        compiler_params=params(),
        name="view_grad",
    )(views, unit_t, in_vmem(expo), scale, tot, total)


def backward_kernel(grad_a, grad_b, pos, raw, pre, emb, hid_part, w_out, out):
    total = grad_a[...].astype(f32) + grad_b[...].astype(f32)
    n, depth = raw.shape
    place = jnp.broadcast_to(pos[...].astype(f32), (8, n)).T[:, :1].astype(jnp.int32)
    lane = lax.broadcasted_iota(jnp.int32, (n, n), 1)
    move = jnp.where(lane == place, 1.0, 0.0).astype(bf16)
    hi = total.astype(bf16)
    lo = (total - hi.astype(f32)).astype(bf16)
    moved = dot(move, jnp.concatenate([hi, lo], axis=1))
    grad = moved[:, :depth] + moved[:, depth:]
    raw_out = raw[...]
    inv = lax.rsqrt(jnp.sum(raw_out * raw_out, axis=1, keepdims=True) + norm_eps)
    inner = jnp.sum(raw_out * grad, axis=1, keepdims=True)
    d_raw = (inv * grad - raw_out * (inv * inv * inv) * inner).astype(bf16)
    g_out = dot(hid_part[...], d_raw, TN)
    d_hidden = dot(d_raw, w_out[...], NT)
    v = pre[...]
    t = jnp.tanh(GELU_K * (v + GELU_A * (v * v * v)))
    slope = 0.5 * (1.0 + t) + (0.5 * GELU_K) * v * (1.0 - t * t) * (1.0 + (3.0 * GELU_A) * (v * v))
    d_pre = (slope * d_hidden).astype(bf16)
    g_in = dot(emb[...], d_pre, TN)
    count = out.shape[0]
    tall, wide = g_in.shape[0] // count, g_in.shape[1]
    for k in range(count):
        for q in range(wide // 128):
            out[k, q * tall : (q + 1) * tall, :] = g_in[
                k * tall : (k + 1) * tall, q * 128 : (q + 1) * 128
            ]
        base, short = tall * (wide // 128), g_out.shape[0] // count
        out[k, base : base + short, :] = g_out[k * short : (k + 1) * short]


def backward(nb, grad_a, grad_b, pos, raw, pre, emb, hid_part, w_out):
    lines = (emb.shape[1] * pre.shape[1] + hid_part.shape[1] * raw.shape[1]) // (nb * 128)
    return pl.pallas_call(
        backward_kernel,
        in_specs=[WHOLE] * 8,
        out_specs=WHOLE,
        out_shape=jax.ShapeDtypeStruct((nb, lines, 128), f32),
        compiler_params=params(),
        name="backward",
    )(grad_a, grad_b, pos, raw, pre, emb, hid_part, w_out)


def unpack_kernel(both, g_in, g_out):
    count = both.shape[0]
    tall, wide = g_in.shape[0] // count, g_in.shape[1]
    base, short = tall * (wide // 128), g_out.shape[0] // count
    for k in range(count):
        x = both[k].astype(f32)
        for q in range(wide // 128):
            g_in[k * tall : (k + 1) * tall, q * 128 : (q + 1) * 128] = x[
                q * tall : (q + 1) * tall
            ]
        g_out[k * short : (k + 1) * short, :] = x[base : base + short]


def unpack(both, shape_in, shape_out):
    return pl.pallas_call(
        unpack_kernel,
        in_specs=[WHOLE],
        out_specs=[WHOLE] * 2,
        out_shape=[jax.ShapeDtypeStruct(shape_in, f32), jax.ShapeDtypeStruct(shape_out, f32)],
        compiler_params=params(),
        name="unpack",
    )(both)


def body(nb, npr, embeddings, pairing, w_in, w_out, prototypes):
    b = lax.axis_index("batch")
    p = lax.axis_index("proto")
    rows, wide = embeddings.shape
    width, depth = prototypes.shape
    hidden_n = w_in.shape[1]
    own = width // nb

    def doubled(x, axis, size):
        step = 1
        while step < size:
            other = lax.ppermute(x, axis, [(i, i ^ step) for i in range(size)])
            if step * 2 == size:
                return [x, other]
            x = x + other
            step *= 2
        return [x]

    def spread_all(x, axis, size):
        wide_x = jnp.broadcast_to(x, (size,) + x.shape[1:])
        return [lax.all_to_all(wide_x, axis, 0, 0, tiled=True)]

    def gathered(x, axis, size):
        return [lax.all_gather(x, axis, axis=0, tiled=True)]

    pre, hid, raw, views, views_t, pos = head(embeddings, pairing, w_in, w_out)
    views_all = lax.all_gather(views_t, "batch", axis=0)
    expo, unit_t, col, tot = first_pass(views, prototypes)
    protos_own = lax.dynamic_slice_in_dim(prototypes, b * own, own, 0)
    emb_part = lax.dynamic_slice_in_dim(embeddings, p * (wide // npr), wide // npr, 1)
    hid_part = lax.dynamic_slice_in_dim(hid, p * (hidden_n // npr), hidden_n // npr, 1)

    scale, row = rowsum(expo, doubled(col, "batch", nb))
    both = lax.psum(jnp.concatenate([row, tot], axis=0), "proto")
    totals, tot = [both[:1]], both[1:]
    tot_all = lax.all_gather(tot, "batch", axis=0)
    col = colsum(expo, totals)
    scale, row = rowsum(expo, spread_all(col, "batch", nb))
    totals = doubled(row, "proto", npr)
    col = colsum(expo, totals)
    scale, row = rowsum(expo, gathered(col, "batch", nb))
    total = jnp.sum(gathered(row, "proto", npr)[0], axis=0, keepdims=True)
    total_all = lax.all_gather(total, "batch", axis=0)

    expo_own, grad_own = proto_first(protos_own, views_all, tot_all)
    scale_own = lax.dynamic_slice_in_dim(scale, b * own, own, 1)
    proto_part = proto_last(expo_own, grad_own, scale_own, protos_own, views_all, total_all)
    grad_proto = lax.all_gather(proto_part, "batch", axis=0, tiled=True)

    part = view_grad_part(views, unit_t, expo, scale, tot, total)
    step = 1
    other = jnp.zeros_like(part)
    while step < npr:
        other = lax.ppermute(part, "proto", [(i, i ^ step) for i in range(npr)])
        if step * 2 < npr:
            part = (part.astype(f32) + other.astype(f32)).astype(bf16)
        step *= 2
    both = backward(nb, part, other, pos, raw, pre, emb_part, hid_part, w_out)
    both = lax.all_to_all(both.astype(bf16), "batch", 0, 0, tiled=True)
    both = jnp.sum(both.astype(f32), axis=0, keepdims=True).astype(bf16)
    both = lax.all_gather(both, ("proto", "batch"), axis=0, tiled=True)
    grad_in, grad_out = unpack(both, (wide, hidden_n), (hidden_n, depth))
    return (grad_in, grad_out, grad_proto.astype(f32))


def solution(mesh):
    return jax.shard_map(
        functools.partial(body, mesh.shape["batch"], mesh.shape["proto"]),
        mesh=mesh,
        in_specs=(P("batch", None), P("batch"), P(), P(), P("proto", None)),
        out_specs=(P(), P(), P("proto", None)),
        check_vma=False,
    )
```

```python
import functools
import math

import jax
import jax.numpy as jnp
from jax import lax
from jax.experimental import pallas as pl
from jax.experimental.pallas import tpu as pltpu
from jax.sharding import PartitionSpec as P

ITERS = 3
norm_eps = 1e-06
code_temp = 0.05
pred_temp = 0.1
loss_scale = 64.0
GRAD_SCALE = loss_scale / pred_temp
EXP2_SCALE = math.log2(math.e) / pred_temp
GELU_K = math.sqrt(2.0 / math.pi)
GELU_A = 0.044715

f32 = jnp.float32
bf16 = jnp.bfloat16
NN = (((1,), (0,)), ((), ()))
NT = (((1,), (1,)), ((), ()))
TN = (((0,), (0,)), ((), ()))
VMEM_LIMIT = 12 * 1024 * 1024


def dot(a, b, dims=NN):
    return lax.dot_general(a, b, dims, preferred_element_type=f32)


SMALL = pl.CostEstimate(flops=1000, bytes_accessed=1000, transcendentals=0)


def params(*semantics):
    return pltpu.CompilerParams(
        dimension_semantics=semantics or None, vmem_limit_bytes=VMEM_LIMIT
    )


def to_column(vec):
    n = vec.shape[1]
    return jnp.broadcast_to(vec, (8, n)).T[:, :1]


def swap_lanes(x):
    half = x.shape[1] // 2
    return jnp.concatenate([x[:, half:], x[:, :half]], axis=1)


def swap_rows(x):
    half = x.shape[0] // 2
    return jnp.concatenate([x[half:], x[:half]], axis=0)


def in_vmem(x):
    return pltpu.with_memory_space_constraint(x, pltpu.VMEM)


def in_hbm(x):
    return pltpu.with_memory_space_constraint(x, pltpu.HBM)


def full(shape):
    return pl.BlockSpec(shape, lambda *_: (0,) * len(shape))


def head_kernel(emb, pairing, w_in, w_out, pre, hid, raw, views, views_t, pos, scratch):
    step = pl.program_id(0)
    rows = emb.shape[0]
    pre_act = dot(emb[...], w_in[...])
    pre[...] = pre_act
    t = jnp.tanh(GELU_K * (pre_act + GELU_A * (pre_act * pre_act * pre_act)))
    hidden = (0.5 * pre_act * (1.0 + t)).astype(bf16)
    hid[...] = hidden
    raw_out = dot(hidden, w_out[...])
    raw[...] = raw_out
    inv = lax.rsqrt(jnp.sum(raw_out * raw_out, axis=1, keepdims=True) + norm_eps)
    scratch[pl.ds(pl.multiple_of(step * rows, rows), rows), :] = (raw_out * inv).astype(bf16)

    @pl.when(step == pl.num_programs(0) - 1)
    def _():
        mate = pairing[...]
        n = mate.shape[1]
        lane = lax.broadcasted_iota(jnp.int32, (1, n), 1)
        first = lane < mate
        low = jnp.minimum(lane, mate)
        sub = lax.broadcasted_iota(jnp.int32, (n, n), 0)
        before = jnp.where(sub < low, 1.0, 0.0).astype(bf16)
        first8 = jnp.broadcast_to(jnp.where(first, 1.0, 0.0), (8, n)).astype(bf16)
        rank = dot(first8, before)[:1].astype(jnp.int32)
        place = jnp.where(first, rank, rank + n // 2)
        pos[...] = place
        move = jnp.where(sub == place, 1.0, 0.0).astype(bf16)
        ordered = dot(move, scratch[...])
        views[...] = ordered.astype(bf16)
        views_t[...] = ordered.T.astype(bf16)


def head(embeddings, pairing, w_in, w_out):
    rows, wide = embeddings.shape
    hidden = w_in.shape[1]
    depth = w_out.shape[1]
    steps = 4
    block = rows // steps
    return pl.pallas_call(
        head_kernel,
        grid=(steps,),
        in_specs=[
            pl.BlockSpec((block, wide), lambda i: (i, 0)),
            full((1, rows)),
            full((wide, hidden)),
            full((hidden, depth)),
        ],
        out_specs=[
            pl.BlockSpec((block, hidden), lambda i: (i, 0)),
            pl.BlockSpec((block, hidden), lambda i: (i, 0)),
            pl.BlockSpec((block, depth), lambda i: (i, 0)),
            full((rows, depth)),
            full((depth, rows)),
            full((1, rows)),
        ],
        out_shape=[
            pltpu.HBM((rows, hidden), f32),
            pltpu.HBM((rows, hidden), bf16),
            pltpu.HBM((rows, depth), f32),
            jax.ShapeDtypeStruct((rows, depth), bf16),
            jax.ShapeDtypeStruct((depth, rows), bf16),
            jax.ShapeDtypeStruct((1, rows), jnp.int32),
        ],
        scratch_shapes=[pltpu.VMEM((rows, depth), bf16)],
        compiler_params=params("arbitrary"),
        name="head",
    )(in_hbm(embeddings), pairing.reshape(1, rows), in_hbm(w_in), in_hbm(w_out))


def unit_of(protos):
    proto_f = protos.astype(f32)
    inv = lax.rsqrt(jnp.sum(proto_f * proto_f, axis=1, keepdims=True) + norm_eps)
    return proto_f, inv, proto_f * inv


WHOLE = pl.BlockSpec(memory_space=pltpu.VMEM)


def scaled_pair(x, axis):
    wide = x.astype(f32) * EXP2_SCALE
    hi = wide.astype(bf16)
    lo = (wide - hi.astype(f32)).astype(bf16)
    return jnp.concatenate([hi, lo], axis=axis)


def first_kernel(block, chunk, tile, views, protos, expo, col, tot, pair, stage, tot_acc):
    rows, depth = views.shape
    width = protos.shape[0]
    tot_acc[...] = jnp.zeros_like(tot_acc)
    pair[...] = scaled_pair(views[...], 1)

    def one(j, carry):
        here = pl.ds(pl.multiple_of(j * block, block), block)
        _, _, unit = unit_of(protos[here, :])
        unit16 = unit.astype(bf16)
        twice = jnp.concatenate([unit16, unit16], axis=1)
        running = jnp.zeros((8, block), f32)
        for c in range(rows // chunk):
            stage[c % 2] = dot(pair[c * chunk : (c + 1) * chunk, :], twice, NT)
            for start in range(0, chunk, tile):
                part = slice(c * chunk + start, c * chunk + start + tile)
                soft = jnp.exp2(stage[c % 2, start : start + tile, :])
                hard = soft * soft
                expo[part, here] = hard.astype(bf16)
                lanes = soft[:, :128]
                for k in range(1, block // 128):
                    lanes = lanes + soft[:, k * 128 : (k + 1) * 128]
                tot_acc[part, :] += lanes
                for k in range(0, tile, 8):
                    running = running + hard[k : k + 8]
        col[:, here] = jnp.sum(running, axis=0, keepdims=True)
        return carry

    lax.fori_loop(0, width // block, one, 0)
    tot[...] = jnp.sum(tot_acc[...].T, axis=0, keepdims=True)


def first_pass(views, protos):
    rows, depth = views.shape
    width = protos.shape[0]
    block = min(512, width)
    chunk = min(256, rows)
    tile = min(32, chunk)
    return pl.pallas_call(
        functools.partial(first_kernel, block, chunk, tile),
        in_specs=[WHOLE] * 2,
        out_specs=[WHOLE] * 3,
        out_shape=[
            pltpu.VMEM((rows, width), bf16),
            jax.ShapeDtypeStruct((1, width), f32),
            jax.ShapeDtypeStruct((1, rows), f32),
        ],
        scratch_shapes=[
            pltpu.VMEM((rows, 2 * depth), bf16),
            pltpu.VMEM((2, chunk, block), f32),
            pltpu.VMEM((rows, 128), f32),
        ],
        compiler_params=params(),
        cost_estimate=SMALL,
        name="first_pass",
    )(views, protos)


def sum_parts(parts, width):
    if len(parts[0].shape) == 3:
        parts = [parts[0].at[k] for k in range(parts[0].shape[0])]
    total = parts[0][:, :width]
    for other in parts[1:]:
        total = total + other[:, :width]
    return total


def rowsum_kernel(count, expo, *refs):
    parts = refs[:count]
    scale, out, spread, acc = refs[count:]
    rows, width = expo.shape
    inverse = 1.0 / sum_parts(parts, width)
    scale[...] = inverse
    spread[...] = jnp.broadcast_to(inverse, spread.shape).astype(bf16)
    tall = 64

    def one(i, carry):
        here = pl.ds(pl.multiple_of(i * tall, tall), tall)
        running = jnp.zeros((tall, 128), f32)
        for k in range(width // 128):
            lanes = slice(k * 128, (k + 1) * 128)
            weight = jnp.concatenate([spread[:, lanes]] * (tall // 16), axis=0)
            running = running + (expo[here, lanes] * weight).astype(f32)
        acc[here, :] = running
        return carry

    lax.fori_loop(0, rows // tall, one, 0)
    out[...] = jnp.sum(acc[...].T, axis=0, keepdims=True)


def rowsum(expo, parts):
    rows, width = expo.shape
    return pl.pallas_call(
        functools.partial(rowsum_kernel, len(parts)),
        in_specs=[WHOLE] * (1 + len(parts)),
        out_specs=[WHOLE] * 2,
        out_shape=[
            jax.ShapeDtypeStruct((1, width), f32),
            jax.ShapeDtypeStruct((1, rows), f32),
        ],
        scratch_shapes=[pltpu.VMEM((16, width), bf16), pltpu.VMEM((rows, 128), f32)],
        compiler_params=params(),
        cost_estimate=SMALL,
        name="rowsum",
    )(in_vmem(expo), *parts)


def colsum_kernel(count, expo, *refs):
    parts = refs[:count]
    rest = refs[count:]
    out, spread = rest[-2:]
    rows, width = expo.shape
    inverse = 1.0 / sum_parts(parts, rows)
    spread[...] = jnp.broadcast_to(inverse, (128, rows)).T.astype(bf16)
    block = min(512, width)

    def one(j, carry):
        here = pl.ds(pl.multiple_of(j * block, block), block)
        running = jnp.zeros((16, block), f32)
        for i in range(rows // 16):
            part = slice(i * 16, (i + 1) * 16)
            weight = jnp.concatenate([spread[part, :]] * (block // 128), axis=1)
            running = running + (expo[part, here] * weight).astype(f32)
        total = jnp.sum(running, axis=0, keepdims=True)
        for k in range(out.shape[0]):
            out[k, :, here] = total
        return carry

    lax.fori_loop(0, width // block, one, 0)
    if len(rest) > 2:
        for k in range(out.shape[0]):
            out[k, :, width:] = rest[0][...]


def colsum(expo, parts, copies=1, behind=()):
    rows, width = expo.shape
    long = width + sum(x.shape[1] for x in behind)
    return pl.pallas_call(
        functools.partial(colsum_kernel, len(parts)),
        in_specs=[WHOLE] * (1 + len(parts) + len(behind)),
        out_specs=WHOLE,
        out_shape=jax.ShapeDtypeStruct((copies, 1, long), f32),
        scratch_shapes=[pltpu.VMEM((rows, 128), bf16)],
        compiler_params=params(),
        cost_estimate=SMALL,
        name="colsum",
    )(in_vmem(expo), *parts, *behind)


def proto_first_kernel(block, tile, base, protos, views, totals, expo, grad, weights, twice, stage, soft16):
    count, depth, rows = views.shape
    for k in range(count):
        total = totals[k, :, base : base + rows]
        here = slice(k * rows, (k + 1) * rows)
        weights[:, here] = (views[k].astype(f32) * (GRAD_SCALE / total)).astype(bf16)
        twice[:depth, here] = views[k]
        twice[depth:, here] = views[k]

    def one(j, carry):
        here = pl.ds(pl.multiple_of(j * block, block), block)
        _, _, unit = unit_of(protos[here, :])
        pair = scaled_pair(unit.astype(bf16), 1)
        running = jnp.zeros((block, depth), f32)
        for k in range(count):
            part = slice(k * rows, (k + 1) * rows)
            stage[k % 2] = dot(pair, twice[:, part])
            for start in range(0, block, tile):
                soft = jnp.exp2(stage[k % 2, start : start + tile, :])
                soft16[k % 2, start : start + tile, :] = soft.astype(bf16)
                expo[pl.ds(pl.multiple_of(j * block + start, tile), tile), part] = (
                    soft * soft
                ).astype(bf16)
            running = running + dot(soft16[k % 2], weights[:, part], NT)
        grad[here, :] = running
        return carry

    lax.fori_loop(0, protos.shape[0] // block, one, 0)


def proto_first(protos, views, totals, base):
    width, depth = protos.shape
    count, _, rows = views.shape
    block = min(256, width)
    tile = min(16, block)
    return pl.pallas_call(
        functools.partial(proto_first_kernel, block, tile, base),
        in_specs=[WHOLE] * 3,
        out_specs=[WHOLE] * 2,
        out_shape=[
            pltpu.VMEM((width, count * rows), bf16),
            jax.ShapeDtypeStruct((width, depth), f32),
        ],
        scratch_shapes=[
            pltpu.VMEM((depth, count * rows), bf16),
            pltpu.VMEM((2 * depth, count * rows), bf16),
            pltpu.VMEM((2, block, rows), f32),
            pltpu.VMEM((2, block, rows), bf16),
        ],
        compiler_params=params(),
        name="proto_first",
    )(protos, views, totals)


def proto_last_kernel(block, place, expo, grad, scale, protos, views, totals, out, weights):
    count, depth, rows = views.shape
    for k in range(count):
        mates = swap_lanes(views[k])
        weights[:, k * rows : (k + 1) * rows] = (
            mates.astype(f32) * (GRAD_SCALE / totals[place[0] ^ k])
        ).astype(bf16)

    def one(j, carry):
        here = pl.ds(pl.multiple_of(j * block, block), block)
        code = dot(expo[here, :], weights[...], NT)
        there = pl.ds(pl.multiple_of(place[0] * expo.shape[0] + j * block, block), block)
        unit_grad = grad[here, :] - to_column(scale[:, there]) * code
        proto_f, inv, _ = unit_of(protos[here, :])
        inner = jnp.sum(proto_f * unit_grad, axis=1, keepdims=True)
        out[here, :] = (inv * unit_grad - proto_f * (inv * inv * inv) * inner).astype(bf16)
        return carry

    lax.fori_loop(0, protos.shape[0] // block, one, 0)


def proto_last(place, expo, grad, scale, protos, views, totals):
    width, depth = protos.shape
    count, _, rows = views.shape
    block = min(256, width)
    return pl.pallas_call(
        functools.partial(proto_last_kernel, block),
        in_specs=[pl.BlockSpec(memory_space=pltpu.SMEM)] + [WHOLE] * 6,
        out_specs=WHOLE,
        out_shape=jax.ShapeDtypeStruct((width, depth), bf16),
        scratch_shapes=[pltpu.VMEM((depth, count * rows), bf16)],
        compiler_params=params(),
        name="proto_last",
    )(place, in_vmem(expo), grad, scale, protos, views, totals)


def view_grad_kernel(block, tile, views, protos, expo, scale, tot, total, out, *scratch):
    pair, stage, soft16, soft_acc, hard_acc = scratch
    rows, depth = views.shape
    width = expo.shape[1]
    pair[...] = scaled_pair(views[...], 1)
    soft_acc[...] = jnp.zeros_like(soft_acc)
    hard_acc[...] = jnp.zeros_like(hard_acc)

    def one(j, carry):
        here = pl.ds(pl.multiple_of(j * block, block), block)
        _, _, unit = unit_of(protos[here, :])
        unit16 = unit.astype(bf16)
        scaled = (unit16.astype(f32) * to_column(scale[:, here])).astype(bf16)
        stage[...] = dot(pair[...], jnp.concatenate([unit16, unit16], axis=1), NT)
        for start in range(0, rows, tile):
            part = slice(start, start + tile)
            soft16[part, :] = jnp.exp2(stage[part, :]).astype(bf16)
        soft_acc[...] += dot(soft16[...], unit16)
        hard_acc[...] += dot(expo[:, here], scaled)
        return carry

    lax.fori_loop(0, width // block, one, 0)
    soft = soft_acc[...] * to_column(GRAD_SCALE / tot[...])
    hard = swap_rows(hard_acc[...] * to_column(GRAD_SCALE / total[...]))
    out[...] = (soft - hard).astype(out.dtype)


def view_grad_part(views, protos, expo, scale, tot, total):
    rows, depth = views.shape
    block = min(512, expo.shape[1])
    return pl.pallas_call(
        functools.partial(view_grad_kernel, block, min(32, rows)),
        in_specs=[WHOLE] * 6,
        out_specs=WHOLE,
        out_shape=jax.ShapeDtypeStruct((rows, depth), bf16),
        scratch_shapes=[
            pltpu.VMEM((rows, 2 * depth), bf16),
            pltpu.VMEM((rows, block), f32),
            pltpu.VMEM((rows, block), bf16),
            pltpu.VMEM((rows, depth), f32),
            pltpu.VMEM((rows, depth), f32),
        ],
        compiler_params=params(),
        name="view_grad",
    )(views, protos, in_vmem(expo), scale, tot, total)


def backward_kernel(grad_a, grad_b, pos, raw, pre, emb, hid_part, w_out, out):
    total = grad_a[...].astype(f32) + grad_b[...].astype(f32)
    n, depth = raw.shape
    place = jnp.broadcast_to(pos[...].astype(f32), (8, n)).T[:, :1].astype(jnp.int32)
    lane = lax.broadcasted_iota(jnp.int32, (n, n), 1)
    move = jnp.where(lane == place, 1.0, 0.0).astype(bf16)
    hi = total.astype(bf16)
    lo = (total - hi.astype(f32)).astype(bf16)
    moved = dot(move, jnp.concatenate([hi, lo], axis=1))
    grad = moved[:, :depth] + moved[:, depth:]
    raw_out = raw[...]
    inv = lax.rsqrt(jnp.sum(raw_out * raw_out, axis=1, keepdims=True) + norm_eps)
    inner = jnp.sum(raw_out * grad, axis=1, keepdims=True)
    d_raw = (inv * grad - raw_out * (inv * inv * inv) * inner).astype(bf16)
    g_out = dot(hid_part[...], d_raw, TN)
    d_hidden = dot(d_raw, w_out[...], NT)
    v = pre[...]
    t = jnp.tanh(GELU_K * (v + GELU_A * (v * v * v)))
    slope = 0.5 * (1.0 + t) + (0.5 * GELU_K) * v * (1.0 - t * t) * (1.0 + (3.0 * GELU_A) * (v * v))
    d_pre = (slope * d_hidden).astype(bf16)
    g_in = dot(emb[...], d_pre, TN)
    count = out.shape[0]
    tall, wide = g_in.shape[0] // count, g_in.shape[1]
    for k in range(count):
        for q in range(wide // 128):
            out[k, q * tall : (q + 1) * tall, :] = g_in[
                k * tall : (k + 1) * tall, q * 128 : (q + 1) * 128
            ]
        base, short = tall * (wide // 128), g_out.shape[0] // count
        out[k, base : base + short, :] = g_out[k * short : (k + 1) * short]


def backward(nb, grad_a, grad_b, pos, raw, pre, emb, hid_part, w_out):
    lines = (emb.shape[1] * pre.shape[1] + hid_part.shape[1] * raw.shape[1]) // (nb * 128)
    return pl.pallas_call(
        backward_kernel,
        in_specs=[WHOLE] * 8,
        out_specs=WHOLE,
        out_shape=jax.ShapeDtypeStruct((nb, lines, 128), f32),
        compiler_params=params(),
        name="backward",
    )(grad_a, grad_b, pos, raw, pre, emb, hid_part, w_out)


def unpack_kernel(order, place, *refs):
    pieces, (g_in, g_out) = refs[:-2], refs[-2:]
    nb = pieces[0].shape[1]
    npr = len(order)
    tall, wide = g_in.shape[0] // (nb * npr), g_in.shape[1]
    base, short = tall * (wide // 128), g_out.shape[0] // (nb * npr)
    half = pieces[0].shape[0]
    for n, flip in enumerate(order):
        owner = place[0] ^ flip
        for k in range(nb):
            x = pieces[n // half][n % half, k].astype(f32)
            low = pl.multiple_of((owner * nb + k) * tall, tall)
            for q in range(wide // 128):
                g_in[pl.ds(low, tall), q * 128 : (q + 1) * 128] = x[q * tall : (q + 1) * tall]
            low = pl.multiple_of((owner * nb + k) * short, short)
            g_out[pl.ds(low, short), :] = x[base : base + short]


def unpack(order, place, pieces, shape_in, shape_out):
    return pl.pallas_call(
        functools.partial(unpack_kernel, order),
        in_specs=[pl.BlockSpec(memory_space=pltpu.SMEM)] + [WHOLE] * len(pieces),
        out_specs=[WHOLE] * 2,
        out_shape=[jax.ShapeDtypeStruct(shape_in, f32), jax.ShapeDtypeStruct(shape_out, f32)],
        compiler_params=params(),
        name="unpack",
    )(place, *pieces)


def body(nb, npr, embeddings, pairing, w_in, w_out, prototypes):
    b = lax.axis_index("batch")
    p = lax.axis_index("proto")
    rows, wide = embeddings.shape
    width, depth = prototypes.shape
    hidden_n = w_in.shape[1]
    own = width // nb

    def flipped(x, axis, size, step):
        return lax.ppermute(x, axis, [(i, i ^ step) for i in range(size)])

    def doubled(x, axis, size):
        step = 1
        while step * 2 < size:
            x = x + flipped(x, axis, size, step)
            step *= 2
        return [x, flipped(x, axis, size, step)] if size > 1 else [x]

    def shared(x):
        wide_x = jnp.broadcast_to(x, (nb,) + x.shape[1:])
        return lax.all_to_all(wide_x, "batch", 0, 0, tiled=True)

    pre, hid, raw, views, views_t, pos = head(embeddings, pairing, w_in, w_out)
    views_all = lax.all_gather(views_t, "batch", axis=0)
    protos_own = lax.dynamic_slice_in_dim(prototypes, b * own, own, 0)
    place = b.astype(jnp.int32).reshape(1)
    views, protos_own, place = lax.optimization_barrier((views, protos_own, place))
    expo, col, tot = first_pass(views, prototypes)

    scale, row = rowsum(expo, doubled(col, "batch", nb))
    first, second = doubled(jnp.concatenate([row, tot], axis=0), "proto", npr)
    both = first + second
    totals, tot = [both[:1]], both[1:]
    packed = lax.all_to_all(colsum(expo, totals, nb, [tot]), "batch", 0, 0, tiled=True)
    scale, row = rowsum(expo, [packed])
    col = colsum(expo, doubled(row, "proto", npr))
    col, views_all = lax.optimization_barrier((col, views_all))
    expo_own, grad_own = proto_first(protos_own, views_all, packed, width)
    scale, row = rowsum(expo, doubled(col[0], "batch", nb))
    first, second = doubled(row, "proto", npr)
    total = first + second
    total_all = total[None]
    step = 1
    while step < nb:
        total_all = jnp.concatenate([total_all, flipped(total_all, "batch", nb, step)], axis=0)
        step *= 2

    proto_part = proto_last(
        place, expo_own, grad_own, scale, protos_own, views_all, total_all)
    grad_proto = lax.all_gather(proto_part, "batch", axis=0, tiled=True)

    part = view_grad_part(views, prototypes, expo, scale, tot, total)
    step = 1
    while step * 2 < npr:
        other = flipped(part, "proto", npr, step)
        part = (part.astype(f32) + other.astype(f32)).astype(bf16)
        step *= 2
    other = flipped(part, "proto", npr, step)
    emb_part = lax.dynamic_slice_in_dim(embeddings, p * (wide // npr), wide // npr, 1)
    hid_part = lax.dynamic_slice_in_dim(hid, p * (hidden_n // npr), hidden_n // npr, 1)
    both = backward(nb, part, other, pos, raw, pre, emb_part, hid_part, w_out)
    both = lax.all_to_all(both.astype(bf16), "batch", 0, 0, tiled=True)
    both = jnp.sum(both.astype(f32), axis=0, keepdims=True).astype(bf16)
    piece = shared(both)[None]
    order = [0]
    step = npr // 2
    while step > 1:
        piece = jnp.concatenate([piece, flipped(piece, "proto", npr, step)], axis=0)
        order = order + [i ^ step for i in order]
        step //= 2
    pieces = [piece, flipped(piece, "proto", npr, 1)]
    order = order + [i ^ 1 for i in order]
    grad_in, grad_out = unpack(
        order, p.astype(jnp.int32).reshape(1), pieces, (wide, hidden_n), (hidden_n, depth)
    )
    return (grad_in, grad_out, grad_proto.astype(f32))


def solution(mesh):
    return jax.shard_map(
        functools.partial(body, mesh.shape["batch"], mesh.shape["proto"]),
        mesh=mesh,
        in_specs=(P("batch", None), P("batch"), P(), P(), P("proto", None)),
        out_specs=(P(), P(), P("proto", None)),
        check_vma=False,
    )
```

```python
import functools
import math

import jax
import jax.numpy as jnp
from jax import lax
from jax.experimental import pallas as pl
from jax.experimental.pallas import tpu as pltpu
from jax.sharding import PartitionSpec as P

ITERS = 3
norm_eps = 1e-06
code_temp = 0.05
pred_temp = 0.1
loss_scale = 64.0
GRAD_SCALE = loss_scale / pred_temp
EXP2_SCALE = math.log2(math.e) / pred_temp
GELU_K = math.sqrt(2.0 / math.pi)
GELU_A = 0.044715

f32 = jnp.float32
bf16 = jnp.bfloat16
NN = (((1,), (0,)), ((), ()))
NT = (((1,), (1,)), ((), ()))
TN = (((0,), (0,)), ((), ()))
VMEM_LIMIT = 12 * 1024 * 1024


def dot(a, b, dims=NN):
    return lax.dot_general(a, b, dims, preferred_element_type=f32)


SMALL = pl.CostEstimate(flops=1000, bytes_accessed=1000, transcendentals=0)


def params(*semantics):
    return pltpu.CompilerParams(
        dimension_semantics=semantics or None, vmem_limit_bytes=VMEM_LIMIT
    )


def to_column(vec):
    n = vec.shape[1]
    return jnp.broadcast_to(vec, (8, n)).T[:, :1]


def swap_lanes(x):
    half = x.shape[1] // 2
    return jnp.concatenate([x[:, half:], x[:, :half]], axis=1)


def swap_rows(x):
    half = x.shape[0] // 2
    return jnp.concatenate([x[half:], x[:half]], axis=0)


def in_vmem(x):
    return pltpu.with_memory_space_constraint(x, pltpu.VMEM)


def in_hbm(x):
    return pltpu.with_memory_space_constraint(x, pltpu.HBM)


def full(shape):
    return pl.BlockSpec(shape, lambda *_: (0,) * len(shape))


def head_kernel(emb, pairing, w_in, w_out, pre, hid, raw, views, views_t, pos, scratch):
    step = pl.program_id(0)
    rows = emb.shape[0]
    pre_act = dot(emb[...], w_in[...])
    pre[...] = pre_act
    t = jnp.tanh(GELU_K * (pre_act + GELU_A * (pre_act * pre_act * pre_act)))
    hidden = (0.5 * pre_act * (1.0 + t)).astype(bf16)
    hid[...] = hidden
    raw_out = dot(hidden, w_out[...])
    raw[...] = raw_out
    inv = lax.rsqrt(jnp.sum(raw_out * raw_out, axis=1, keepdims=True) + norm_eps)
    scratch[pl.ds(pl.multiple_of(step * rows, rows), rows), :] = (raw_out * inv).astype(bf16)

    @pl.when(step == pl.num_programs(0) - 1)
    def _():
        mate = pairing[...]
        n = mate.shape[1]
        lane = lax.broadcasted_iota(jnp.int32, (1, n), 1)
        first = lane < mate
        low = jnp.minimum(lane, mate)
        sub = lax.broadcasted_iota(jnp.int32, (n, n), 0)
        before = jnp.where(sub < low, 1.0, 0.0).astype(bf16)
        first8 = jnp.broadcast_to(jnp.where(first, 1.0, 0.0), (8, n)).astype(bf16)
        rank = dot(first8, before)[:1].astype(jnp.int32)
        place = jnp.where(first, rank, rank + n // 2)
        pos[...] = place
        move = jnp.where(sub == place, 1.0, 0.0).astype(bf16)
        ordered = dot(move, scratch[...])
        views[...] = ordered.astype(bf16)
        views_t[...] = ordered.T.astype(bf16)


def head(embeddings, pairing, w_in, w_out):
    rows, wide = embeddings.shape
    hidden = w_in.shape[1]
    depth = w_out.shape[1]
    steps = 4
    block = rows // steps
    return pl.pallas_call(
        head_kernel,
        grid=(steps,),
        in_specs=[
            pl.BlockSpec((block, wide), lambda i: (i, 0)),
            full((1, rows)),
            full((wide, hidden)),
            full((hidden, depth)),
        ],
        out_specs=[
            pl.BlockSpec((block, hidden), lambda i: (i, 0)),
            pl.BlockSpec((block, hidden), lambda i: (i, 0)),
            pl.BlockSpec((block, depth), lambda i: (i, 0)),
            full((rows, depth)),
            full((depth, rows)),
            full((1, rows)),
        ],
        out_shape=[
            pltpu.HBM((rows, hidden), f32),
            pltpu.HBM((rows, hidden), bf16),
            pltpu.HBM((rows, depth), f32),
            jax.ShapeDtypeStruct((rows, depth), bf16),
            jax.ShapeDtypeStruct((depth, rows), bf16),
            jax.ShapeDtypeStruct((1, rows), jnp.int32),
        ],
        scratch_shapes=[pltpu.VMEM((rows, depth), bf16)],
        compiler_params=params("arbitrary"),
        name="head",
    )(in_hbm(embeddings), pairing.reshape(1, rows), in_hbm(w_in), in_hbm(w_out))


def unit_of(protos):
    proto_f = protos.astype(f32)
    inv = lax.rsqrt(jnp.sum(proto_f * proto_f, axis=1, keepdims=True) + norm_eps)
    return proto_f, inv, proto_f * inv


WHOLE = pl.BlockSpec(memory_space=pltpu.VMEM)


def scaled_pair(x, axis):
    wide = x.astype(f32) * EXP2_SCALE
    hi = wide.astype(bf16)
    lo = (wide - hi.astype(f32)).astype(bf16)
    return jnp.concatenate([hi, lo], axis=axis)


def first_kernel(block, chunk, tile, views, protos, expo, col, tot, pair, stage, tot_acc):
    rows, depth = views.shape
    width = protos.shape[0]
    tot_acc[...] = jnp.zeros_like(tot_acc)
    pair[...] = scaled_pair(views[...], 1)

    def one(j, carry):
        here = pl.ds(pl.multiple_of(j * block, block), block)
        _, _, unit = unit_of(protos[here, :])
        unit16 = unit.astype(bf16)
        twice = jnp.concatenate([unit16, unit16], axis=1)
        running = jnp.zeros((8, block), f32)
        for c in range(rows // chunk):
            stage[c % 2] = dot(pair[c * chunk : (c + 1) * chunk, :], twice, NT)
            for start in range(0, chunk, tile):
                part = slice(c * chunk + start, c * chunk + start + tile)
                soft = jnp.exp2(stage[c % 2, start : start + tile, :])
                hard = soft * soft
                expo[part, here] = hard.astype(bf16)
                lanes = soft[:, :128]
                for k in range(1, block // 128):
                    lanes = lanes + soft[:, k * 128 : (k + 1) * 128]
                tot_acc[part, :] += lanes
                for k in range(0, tile, 8):
                    running = running + hard[k : k + 8]
        col[:, here] = jnp.sum(running, axis=0, keepdims=True)
        return carry

    lax.fori_loop(0, width // block, one, 0)
    tot[...] = jnp.sum(tot_acc[...].T, axis=0, keepdims=True)


def first_pass(views, protos):
    rows, depth = views.shape
    width = protos.shape[0]
    block = min(512, width)
    chunk = min(256, rows)
    tile = min(32, chunk)
    return pl.pallas_call(
        functools.partial(first_kernel, block, chunk, tile),
        in_specs=[WHOLE] * 2,
        out_specs=[WHOLE] * 3,
        out_shape=[
            pltpu.VMEM((rows, width), bf16),
            jax.ShapeDtypeStruct((1, width), f32),
            jax.ShapeDtypeStruct((1, rows), f32),
        ],
        scratch_shapes=[
            pltpu.VMEM((rows, 2 * depth), bf16),
            pltpu.VMEM((2, chunk, block), f32),
            pltpu.VMEM((rows, 128), f32),
        ],
        compiler_params=params(),
        cost_estimate=SMALL,
        name="first_pass",
    )(views, protos)


def sum_parts(parts, width):
    if len(parts[0].shape) == 3:
        parts = [parts[0].at[k] for k in range(parts[0].shape[0])]
    total = parts[0][:, :width]
    for other in parts[1:]:
        total = total + other[:, :width]
    return total


def add_fours(terms):
    total = None
    for k in range(0, len(terms), 4):
        four = terms[k : k + 4]
        while len(four) > 1:
            four = [x + y for x, y in zip(four[::2], four[1::2])]
        part = four[0].astype(f32)
        total = part if total is None else total + part
    return total


def rowsum_tile(expo, here, spread, tall, width):
    terms = []
    total = None
    for k in range(width // 128):
        lanes = slice(k * 128, (k + 1) * 128)
        weight = jnp.concatenate([spread[:, lanes]] * (tall // 16), axis=0)
        terms.append(expo[here, lanes] * weight)
        if len(terms) == 4 or k == width // 128 - 1:
            part = add_fours(terms)
            total = part if total is None else total + part
            terms = []
    return total


def rowsum_kernel(count, expo, *refs):
    parts = refs[:count]
    scale, out, spread, acc = refs[count:]
    rows, width = expo.shape
    inverse = 1.0 / sum_parts(parts, width)
    scale[...] = inverse
    spread[...] = jnp.broadcast_to(inverse, spread.shape).astype(bf16)
    tall = 64

    def one(i, carry):
        here = pl.ds(pl.multiple_of(i * tall, tall), tall)
        acc[here, :] = rowsum_tile(expo, here, spread, tall, width)
        return carry

    lax.fori_loop(0, rows // tall, one, 0)
    out[...] = jnp.sum(acc[...].T, axis=0, keepdims=True)


def rowsum(expo, parts):
    rows, width = expo.shape
    return pl.pallas_call(
        functools.partial(rowsum_kernel, len(parts)),
        in_specs=[WHOLE] * (1 + len(parts)),
        out_specs=[WHOLE] * 2,
        out_shape=[
            jax.ShapeDtypeStruct((1, width), f32),
            jax.ShapeDtypeStruct((1, rows), f32),
        ],
        scratch_shapes=[pltpu.VMEM((16, width), bf16), pltpu.VMEM((rows, 128), f32)],
        compiler_params=params(),
        cost_estimate=SMALL,
        name="rowsum",
    )(in_vmem(expo), *parts)


def rowsum_stream_kernel(count, expo, *refs):
    parts = refs[:count]
    scale, out, spread, acc = refs[count:]
    block, width = expo.shape
    step = pl.program_id(0)

    @pl.when(step == 0)
    def _():
        inverse = 1.0 / sum_parts(parts, width)
        scale[...] = inverse
        spread[...] = jnp.broadcast_to(inverse, spread.shape).astype(bf16)

    tall = 64
    for i in range(block // tall):
        here = pl.ds(pl.multiple_of(step * block + i * tall, tall), tall)
        acc[here, :] = rowsum_tile(expo, slice(i * tall, (i + 1) * tall), spread, tall, width)

    @pl.when(step == pl.num_programs(0) - 1)
    def _():
        out[...] = jnp.sum(acc[...].T, axis=0, keepdims=True)


def rowsum_stream(expo, parts):
    rows, width = expo.shape
    block = min(128, rows)
    return pl.pallas_call(
        functools.partial(rowsum_stream_kernel, len(parts)),
        grid=(rows // block,),
        in_specs=[pl.BlockSpec((block, width), lambda i: (i, 0))]
        + [full((1, width))] * len(parts),
        out_specs=[full((1, width)), full((1, rows))],
        out_shape=[
            jax.ShapeDtypeStruct((1, width), f32),
            jax.ShapeDtypeStruct((1, rows), f32),
        ],
        scratch_shapes=[pltpu.VMEM((16, width), bf16), pltpu.VMEM((rows, 128), f32)],
        compiler_params=params("arbitrary"),
        cost_estimate=SMALL,
        name="rowsum_stream",
    )(in_hbm(expo), *parts)


def colsum_kernel(count, expo, *refs):
    parts = refs[:count]
    rest = refs[count:]
    out, spread = rest[-2:]
    rows, width = expo.shape
    inverse = 1.0 / sum_parts(parts, rows)
    spread[...] = jnp.broadcast_to(inverse, (128, rows)).T.astype(bf16)
    block = min(512, width)

    def one(j, carry):
        here = pl.ds(pl.multiple_of(j * block, block), block)
        running = jnp.zeros((16, block), f32)
        for i in range(0, rows // 16, 4):
            terms = []
            for k in range(i, min(i + 4, rows // 16)):
                part = slice(k * 16, (k + 1) * 16)
                weight = jnp.concatenate([spread[part, :]] * (block // 128), axis=1)
                terms.append(expo[part, here] * weight)
            running = running + add_fours(terms)
        total = jnp.sum(running, axis=0, keepdims=True)
        for k in range(out.shape[0]):
            out[k, :, here] = total
        return carry

    lax.fori_loop(0, width // block, one, 0)
    if len(rest) > 2:
        for k in range(out.shape[0]):
            out[k, :, width:] = rest[0][...]


def colsum(expo, parts, copies=1, behind=()):
    rows, width = expo.shape
    long = width + sum(x.shape[1] for x in behind)
    return pl.pallas_call(
        functools.partial(colsum_kernel, len(parts)),
        in_specs=[WHOLE] * (1 + len(parts) + len(behind)),
        out_specs=WHOLE,
        out_shape=jax.ShapeDtypeStruct((copies, 1, long), f32),
        scratch_shapes=[pltpu.VMEM((rows, 128), bf16)],
        compiler_params=params(),
        cost_estimate=SMALL,
        name="colsum",
    )(in_vmem(expo), *parts, *behind)


def proto_first_kernel(chunk, tile, lead, place, protos, views, totals, expo, grad, *scratch):
    weights, twice, pair, stage, soft16, acc = scratch
    count = expo.shape[1] // views.shape[2]
    _, depth, rows = views.shape
    width = protos.shape[0]
    _, _, unit = unit_of(protos[...])
    pair[...] = scaled_pair(unit.astype(bf16), 1)
    for n in range(count):
        k = lead + n
        weights[...] = (views[k].astype(f32) * (GRAD_SCALE / totals[place[0] ^ k])).astype(bf16)
        twice[:depth, :] = views[k]
        twice[depth:, :] = views[k]
        for c in range(width // chunk):
            stage[c % 2] = dot(pair[c * chunk : (c + 1) * chunk, :], twice[...])
            for start in range(0, chunk, tile):
                part = slice(c * chunk + start, c * chunk + start + tile)
                soft = jnp.exp2(stage[c % 2, start : start + tile, :])
                soft16[part, :] = soft.astype(bf16)
                expo[part, n * rows : (n + 1) * rows] = (soft * soft).astype(bf16)
        found = dot(soft16[...], weights[...], NT)
        if n == 0:
            acc[...] = found
        else:
            acc[...] += found
    grad[...] = acc[...]


def proto_first(place, protos, views, totals, lead, count):
    width, depth = protos.shape
    rows = views.shape[2]
    chunk = min(256, width)
    tile = min(16, chunk)
    return pl.pallas_call(
        functools.partial(proto_first_kernel, chunk, tile, lead),
        in_specs=[pl.BlockSpec(memory_space=pltpu.SMEM)] + [WHOLE] * 3,
        out_specs=[WHOLE] * 2,
        out_shape=[
            pltpu.VMEM((width, count * rows), bf16),
            jax.ShapeDtypeStruct((width, depth), f32),
        ],
        scratch_shapes=[
            pltpu.VMEM((depth, rows), bf16),
            pltpu.VMEM((2 * depth, rows), bf16),
            pltpu.VMEM((width, 2 * depth), bf16),
            pltpu.VMEM((2, chunk, rows), f32),
            pltpu.VMEM((width, rows), bf16),
            pltpu.VMEM((width, depth), f32),
        ],
        compiler_params=params(),
        cost_estimate=SMALL,
        name="proto_first",
    )(place, protos, views, totals)


def proto_last_kernel(groups, place, *refs):
    expos, grads = refs[:groups], refs[groups : 2 * groups]
    scale, protos, views, totals, out, weights, acc = refs[2 * groups :]
    count, depth, rows = views.shape
    each = count // groups
    for k in range(count):
        mates = swap_lanes(views[k])
        weights[...] = (mates.astype(f32) * (GRAD_SCALE / totals[place[0] ^ k])).astype(bf16)
        found = dot(expos[k // each][:, (k % each) * rows : (k % each + 1) * rows], weights[...], NT)
        if k == 0:
            acc[...] = found
        else:
            acc[...] += found
    width = protos.shape[0]
    there = pl.ds(pl.multiple_of(place[0] * width, width), width)
    unit_grad = grads[0][...]
    for other in grads[1:]:
        unit_grad = unit_grad + other[...]
    unit_grad = unit_grad - to_column(scale[:, there]) * acc[...]
    proto_f, inv, _ = unit_of(protos[...])
    inner = jnp.sum(proto_f * unit_grad, axis=1, keepdims=True)
    out[...] = (inv * unit_grad - proto_f * (inv * inv * inv) * inner).astype(bf16)


def proto_last(place, expos, grads, scale, protos, views, totals):
    width, depth = protos.shape
    rows = views.shape[2]
    groups = len(expos)
    return pl.pallas_call(
        functools.partial(proto_last_kernel, groups),
        in_specs=[pl.BlockSpec(memory_space=pltpu.SMEM)] + [WHOLE] * (2 * groups + 4),
        out_specs=WHOLE,
        out_shape=jax.ShapeDtypeStruct((width, depth), bf16),
        scratch_shapes=[pltpu.VMEM((depth, rows), bf16), pltpu.VMEM((width, depth), f32)],
        compiler_params=params(),
        name="proto_last",
    )(place, *[in_vmem(x) for x in expos], *grads, scale, protos, views, totals)


def view_soft_kernel(block, tile, lead, views, protos, out, pair, stage, soft16):
    rows, depth = views.shape
    pair[...] = scaled_pair(views[...], 1)
    out[...] = jnp.zeros_like(out)
    chunk = stage.shape[1]

    def one(j, carry):
        here = pl.ds(pl.multiple_of(lead + j * block, block), block)
        _, _, unit = unit_of(protos[here, :])
        unit16 = unit.astype(bf16)
        twice = jnp.concatenate([unit16, unit16], axis=1)
        for c in range(rows // chunk):
            stage[c % 2] = dot(pair[c * chunk : (c + 1) * chunk, :], twice, NT)
            for start in range(0, chunk, tile):
                part = slice(c * chunk + start, c * chunk + start + tile)
                soft16[part, :] = jnp.exp2(stage[c % 2, start : start + tile, :]).astype(bf16)
        out[...] += dot(soft16[...], unit16)
        return carry

    return one


def view_soft_body(block, tile, lead, count, *refs):
    lax.fori_loop(0, count // block, view_soft_kernel(block, tile, lead, *refs), 0)


def view_soft(views, protos, lead, count):
    rows, depth = views.shape
    block = min(512, count)
    chunk = min(256, rows)
    return pl.pallas_call(
        functools.partial(view_soft_body, block, min(32, chunk), lead, count),
        in_specs=[WHOLE] * 2,
        out_specs=WHOLE,
        out_shape=jax.ShapeDtypeStruct((rows, depth), f32),
        scratch_shapes=[
            pltpu.VMEM((rows, 2 * depth), bf16),
            pltpu.VMEM((2, chunk, block), f32),
            pltpu.VMEM((rows, block), bf16),
        ],
        compiler_params=params(),
        cost_estimate=SMALL,
        name="view_soft",
    )(views, protos)


def view_grad_kernel(groups, protos, expo, scale, tot, total, *refs):
    softs, (out, acc) = refs[:groups], refs[groups:]
    step = pl.program_id(0)
    _, _, unit = unit_of(protos[...])
    scaled = (unit.astype(bf16).astype(f32) * to_column(scale[...])).astype(bf16)
    found = dot(expo[...], scaled)

    @pl.when(step == 0)
    def _():
        acc[...] = found

    @pl.when(step > 0)
    def _():
        acc[...] += found

    @pl.when(step == pl.num_programs(0) - 1)
    def _():
        soft = softs[0][...]
        for other in softs[1:]:
            soft = soft + other[...]
        soft = soft * to_column(GRAD_SCALE / tot[...])
        hard = swap_rows(acc[...] * to_column(GRAD_SCALE / total[...]))
        out[...] = (soft - hard).astype(out.dtype)


def view_grad_part(protos, expo, scale, tot, total, softs):
    rows, width = expo.shape
    depth = protos.shape[1]
    block = min(1024, width)
    return pl.pallas_call(
        functools.partial(view_grad_kernel, len(softs)),
        grid=(width // block,),
        in_specs=[
            pl.BlockSpec((block, depth), lambda j: (j, 0)),
            pl.BlockSpec((rows, block), lambda j: (0, j)),
            pl.BlockSpec((1, block), lambda j: (0, j)),
            full((1, rows)),
            full((1, rows)),
        ]
        + [full((rows, depth))] * len(softs),
        out_specs=full((rows, depth)),
        out_shape=jax.ShapeDtypeStruct((rows, depth), bf16),
        scratch_shapes=[pltpu.VMEM((rows, depth), f32)],
        compiler_params=params("arbitrary"),
        name="view_grad",
    )(protos, in_hbm(expo), scale, tot, total, *[in_hbm(x) for x in softs])


def backward_kernel(grad_a, grad_b, pos, raw, pre, emb, hid_part, w_out, out):
    total = grad_a[...].astype(f32) + grad_b[...].astype(f32)
    n, depth = raw.shape
    place = jnp.broadcast_to(pos[...].astype(f32), (8, n)).T[:, :1].astype(jnp.int32)
    lane = lax.broadcasted_iota(jnp.int32, (n, n), 1)
    move = jnp.where(lane == place, 1.0, 0.0).astype(bf16)
    hi = total.astype(bf16)
    lo = (total - hi.astype(f32)).astype(bf16)
    moved = dot(move, jnp.concatenate([hi, lo], axis=1))
    grad = moved[:, :depth] + moved[:, depth:]
    raw_out = raw[...]
    inv = lax.rsqrt(jnp.sum(raw_out * raw_out, axis=1, keepdims=True) + norm_eps)
    inner = jnp.sum(raw_out * grad, axis=1, keepdims=True)
    d_raw = (inv * grad - raw_out * (inv * inv * inv) * inner).astype(bf16)
    g_out = dot(hid_part[...], d_raw, TN)
    d_hidden = dot(d_raw, w_out[...], NT)
    v = pre[...]
    t = jnp.tanh(GELU_K * (v + GELU_A * (v * v * v)))
    slope = 0.5 * (1.0 + t) + (0.5 * GELU_K) * v * (1.0 - t * t) * (1.0 + (3.0 * GELU_A) * (v * v))
    d_pre = (slope * d_hidden).astype(bf16)
    g_in = dot(emb[...], d_pre, TN)
    count = out.shape[0]
    tall, wide = g_in.shape[0] // count, g_in.shape[1]
    for k in range(count):
        for q in range(wide // 128):
            out[k, q * tall : (q + 1) * tall, :] = g_in[
                k * tall : (k + 1) * tall, q * 128 : (q + 1) * 128
            ]
        base, short = tall * (wide // 128), g_out.shape[0] // count
        out[k, base : base + short, :] = g_out[k * short : (k + 1) * short]


def backward(nb, grad_a, grad_b, pos, raw, pre, emb, hid_part, w_out):
    lines = (emb.shape[1] * pre.shape[1] + hid_part.shape[1] * raw.shape[1]) // (nb * 128)
    return pl.pallas_call(
        backward_kernel,
        in_specs=[WHOLE] * 8,
        out_specs=WHOLE,
        out_shape=jax.ShapeDtypeStruct((nb, lines, 128), f32),
        compiler_params=params(),
        name="backward",
    )(grad_a, grad_b, pos, raw, pre, emb, hid_part, w_out)


def unpack_kernel(order, place, *refs):
    pieces, (g_in, g_out) = refs[:-2], refs[-2:]
    nb = pieces[0].shape[1]
    npr = len(order)
    tall, wide = g_in.shape[0] // (nb * npr), g_in.shape[1]
    base, short = tall * (wide // 128), g_out.shape[0] // (nb * npr)
    half = pieces[0].shape[0]
    for n, flip in enumerate(order):
        owner = place[0] ^ flip
        for k in range(nb):
            x = pieces[n // half][n % half, k].astype(f32)
            low = pl.multiple_of((owner * nb + k) * tall, tall)
            for q in range(wide // 128):
                g_in[pl.ds(low, tall), q * 128 : (q + 1) * 128] = x[q * tall : (q + 1) * tall]
            low = pl.multiple_of((owner * nb + k) * short, short)
            g_out[pl.ds(low, short), :] = x[base : base + short]


def unpack(order, place, pieces, shape_in, shape_out):
    return pl.pallas_call(
        functools.partial(unpack_kernel, order),
        in_specs=[pl.BlockSpec(memory_space=pltpu.SMEM)] + [WHOLE] * len(pieces),
        out_specs=[WHOLE] * 2,
        out_shape=[jax.ShapeDtypeStruct(shape_in, f32), jax.ShapeDtypeStruct(shape_out, f32)],
        compiler_params=params(),
        name="unpack",
    )(place, *pieces)


def widen_kernel(x, out):
    out[...] = x[...].astype(f32)


def widen(x):
    rows, depth = x.shape
    block = min(1024, rows)
    spec = pl.BlockSpec((block, depth), lambda i: (i, 0))
    return pl.pallas_call(
        widen_kernel,
        grid=(rows // block,),
        in_specs=[spec],
        out_specs=spec,
        out_shape=jax.ShapeDtypeStruct((rows, depth), f32),
        compiler_params=params("arbitrary"),
        name="widen",
    )(in_hbm(x))


def body(nb, npr, embeddings, pairing, w_in, w_out, prototypes):
    b = lax.axis_index("batch")
    p = lax.axis_index("proto")
    rows, wide = embeddings.shape
    width, depth = prototypes.shape
    hidden_n = w_in.shape[1]
    own = width // nb

    def flipped(x, axis, size, step):
        return lax.ppermute(x, axis, [(i, i ^ step) for i in range(size)])

    def exchange(x, axis, size, step, queue, results):
        other = flipped(x, axis, size, step)
        if queue:
            work, operands = queue.pop(0)
            operands, _ = lax.optimization_barrier((operands, x))
            other, found = lax.optimization_barrier((other, work(*operands)))
            results.append(found)
        return other

    def doubled(x, axis, size, queue=(), results=None):
        step = 1
        while step * 2 < size:
            x = x + exchange(x, axis, size, step, queue, results)
            step *= 2
        return [x, exchange(x, axis, size, step, queue, results)]

    def shared(x):
        wide_x = jnp.broadcast_to(x, (nb,) + x.shape[1:])
        return lax.all_to_all(wide_x, "batch", 0, 0, tiled=True)

    pre, hid, raw, views, views_t, pos = head(embeddings, pairing, w_in, w_out)
    views_all = lax.all_gather(views_t, "batch", axis=0)
    protos_own = lax.dynamic_slice_in_dim(prototypes, b * own, own, 0)
    place = b.astype(jnp.int32).reshape(1)
    views, protos_own, place = lax.optimization_barrier((views, protos_own, place))
    expo, col, tot = first_pass(views, prototypes)

    groups = 4
    cols = width // groups
    softs = []
    queue = [
        (functools.partial(view_soft, lead=k * cols, count=cols), (views, prototypes))
        for k in range(groups)
    ]
    scale, row = rowsum(expo, doubled(col, "batch", nb, queue, softs))
    first, second = doubled(jnp.concatenate([row, tot], axis=0), "proto", npr, queue, softs)
    both = first + second
    totals, tot = [both[:1]], both[1:]

    col = colsum(expo, totals)[0]
    tot_all = tot[None]
    step = 1
    while step < nb:
        other = flipped(tot_all, "batch", nb, step)
        part = flipped(col, "batch", nb, step)
        other, part = lax.optimization_barrier((other, part))
        tot_all = jnp.concatenate([tot_all, other], axis=0)
        step *= 2
        if step < nb:
            col = col + part
    scale, row = rowsum(expo, [col, part])
    col = colsum(expo, doubled(row, "proto", npr, queue, softs))[0]
    while queue:
        work, operands = queue.pop(0)
        softs.append(work(*operands))

    col, views_all = lax.optimization_barrier((col, views_all))
    each = nb // groups
    owns = []
    queue = [
        (
            functools.partial(proto_first, lead=k * each, count=each),
            (place, protos_own, views_all, tot_all),
        )
        for k in range(groups)
    ]
    scale, row = rowsum_stream(expo, doubled(col, "batch", nb, queue, owns))
    first, second = doubled(row, "proto", npr, queue, owns)
    total = first + second
    total_all = total[None]
    step = 1
    while step < nb:
        other = exchange(total_all, "batch", nb, step, queue, owns)
        total_all = jnp.concatenate([total_all, other], axis=0)
        step *= 2

    proto_part = proto_last(
        place,
        [x for x, _ in owns],
        [x for _, x in owns],
        scale,
        protos_own,
        views_all,
        total_all,
    )
    grad_proto = lax.all_gather(proto_part, "batch", axis=0, tiled=True)

    part = view_grad_part(prototypes, expo, scale, tot, total, softs)
    step = 1
    while step * 2 < npr:
        other = flipped(part, "proto", npr, step)
        part = (part.astype(f32) + other.astype(f32)).astype(bf16)
        step *= 2
    other = flipped(part, "proto", npr, step)
    emb_part = lax.dynamic_slice_in_dim(embeddings, p * (wide // npr), wide // npr, 1)
    hid_part = lax.dynamic_slice_in_dim(hid, p * (hidden_n // npr), hidden_n // npr, 1)
    both = backward(nb, part, other, pos, raw, pre, emb_part, hid_part, w_out)
    both = lax.all_to_all(both.astype(bf16), "batch", 0, 0, tiled=True)
    both = jnp.sum(both.astype(f32), axis=0, keepdims=True).astype(bf16)
    piece = shared(both)[None]
    order = [0]
    step = npr // 2
    while step > 1:
        piece = jnp.concatenate([piece, flipped(piece, "proto", npr, step)], axis=0)
        order = order + [i ^ step for i in order]
        step //= 2
    pieces = [piece, flipped(piece, "proto", npr, 1)]
    order = order + [i ^ 1 for i in order]
    grad_in, grad_out = unpack(
        order, p.astype(jnp.int32).reshape(1), pieces, (wide, hidden_n), (hidden_n, depth)
    )
    return (grad_in, grad_out, widen(grad_proto))


def solution(mesh):
    return jax.shard_map(
        functools.partial(body, mesh.shape["batch"], mesh.shape["proto"]),
        mesh=mesh,
        in_specs=(P("batch", None), P("batch"), P(), P(), P("proto", None)),
        out_specs=(P(), P(), P("proto", None)),
        check_vma=False,
    )
```

```python
import functools
import math

import jax
import jax.numpy as jnp
from jax import lax
from jax.experimental import pallas as pl
from jax.experimental.pallas import tpu as pltpu
from jax.sharding import PartitionSpec as P

ITERS = 3
norm_eps = 1e-06
code_temp = 0.05
pred_temp = 0.1
loss_scale = 64.0
GRAD_SCALE = loss_scale / pred_temp
EXP2_SCALE = math.log2(math.e) / pred_temp
GELU_K = math.sqrt(2.0 / math.pi)
GELU_A = 0.044715

f32 = jnp.float32
bf16 = jnp.bfloat16
NN = (((1,), (0,)), ((), ()))
NT = (((1,), (1,)), ((), ()))
TN = (((0,), (0,)), ((), ()))
VMEM_LIMIT = 12 * 1024 * 1024


def dot(a, b, dims=NN):
    return lax.dot_general(a, b, dims, preferred_element_type=f32)


SMALL = pl.CostEstimate(flops=1000, bytes_accessed=1000, transcendentals=0)


def params(*semantics):
    return pltpu.CompilerParams(
        dimension_semantics=semantics or None, vmem_limit_bytes=VMEM_LIMIT
    )


def to_column(vec):
    n = vec.shape[1]
    return jnp.broadcast_to(vec, (8, n)).T[:, :1]


def swap_lanes(x):
    half = x.shape[1] // 2
    return jnp.concatenate([x[:, half:], x[:, :half]], axis=1)


def swap_rows(x):
    half = x.shape[0] // 2
    return jnp.concatenate([x[half:], x[:half]], axis=0)


def in_vmem(x):
    return pltpu.with_memory_space_constraint(x, pltpu.VMEM)


def in_hbm(x):
    return pltpu.with_memory_space_constraint(x, pltpu.HBM)


def full(shape):
    return pl.BlockSpec(shape, lambda *_: (0,) * len(shape))


def head_kernel(emb, pairing, w_in, w_out, pre, hid, raw, views, views_t, pos, scratch):
    step = pl.program_id(0)
    rows = emb.shape[0]
    pre_act = dot(emb[...], w_in[...])
    pre[...] = pre_act
    t = jnp.tanh(GELU_K * (pre_act + GELU_A * (pre_act * pre_act * pre_act)))
    hidden = (0.5 * pre_act * (1.0 + t)).astype(bf16)
    hid[...] = hidden
    raw_out = dot(hidden, w_out[...])
    raw[...] = raw_out
    inv = lax.rsqrt(jnp.sum(raw_out * raw_out, axis=1, keepdims=True) + norm_eps)
    scratch[pl.ds(pl.multiple_of(step * rows, rows), rows), :] = (raw_out * inv).astype(bf16)

    @pl.when(step == pl.num_programs(0) - 1)
    def _():
        mate = pairing[...]
        n = mate.shape[1]
        lane = lax.broadcasted_iota(jnp.int32, (1, n), 1)
        first = lane < mate
        low = jnp.minimum(lane, mate)
        sub = lax.broadcasted_iota(jnp.int32, (n, n), 0)
        before = jnp.where(sub < low, 1.0, 0.0).astype(bf16)
        first8 = jnp.broadcast_to(jnp.where(first, 1.0, 0.0), (8, n)).astype(bf16)
        rank = dot(first8, before)[:1].astype(jnp.int32)
        place = jnp.where(first, rank, rank + n // 2)
        pos[...] = place
        move = jnp.where(sub == place, 1.0, 0.0).astype(bf16)
        ordered = dot(move, scratch[...])
        views[...] = ordered.astype(bf16)
        views_t[...] = ordered.T.astype(bf16)


def head(embeddings, pairing, w_in, w_out):
    rows, wide = embeddings.shape
    hidden = w_in.shape[1]
    depth = w_out.shape[1]
    steps = 4
    block = rows // steps
    return pl.pallas_call(
        head_kernel,
        grid=(steps,),
        in_specs=[
            pl.BlockSpec((block, wide), lambda i: (i, 0)),
            full((1, rows)),
            full((wide, hidden)),
            full((hidden, depth)),
        ],
        out_specs=[
            pl.BlockSpec((block, hidden), lambda i: (i, 0)),
            pl.BlockSpec((block, hidden), lambda i: (i, 0)),
            pl.BlockSpec((block, depth), lambda i: (i, 0)),
            full((rows, depth)),
            full((depth, rows)),
            full((1, rows)),
        ],
        out_shape=[
            pltpu.HBM((rows, hidden), f32),
            pltpu.HBM((rows, hidden), bf16),
            pltpu.HBM((rows, depth), f32),
            jax.ShapeDtypeStruct((rows, depth), bf16),
            jax.ShapeDtypeStruct((depth, rows), bf16),
            jax.ShapeDtypeStruct((1, rows), jnp.int32),
        ],
        scratch_shapes=[pltpu.VMEM((rows, depth), bf16)],
        compiler_params=params("arbitrary"),
        name="head",
    )(in_hbm(embeddings), pairing.reshape(1, rows), in_hbm(w_in), in_hbm(w_out))


def unit_of(protos):
    proto_f = protos.astype(f32)
    inv = lax.rsqrt(jnp.sum(proto_f * proto_f, axis=1, keepdims=True) + norm_eps)
    return proto_f, inv, proto_f * inv


WHOLE = pl.BlockSpec(memory_space=pltpu.VMEM)


def scaled_pair(x, axis):
    wide = x.astype(f32) * EXP2_SCALE
    hi = wide.astype(bf16)
    lo = (wide - hi.astype(f32)).astype(bf16)
    return jnp.concatenate([hi, lo], axis=axis)


def first_kernel(block, chunk, tile, views, protos, expo, col, tot, pair, stage, tot_acc):
    rows, depth = views.shape
    width = protos.shape[0]
    tot_acc[...] = jnp.zeros_like(tot_acc)
    pair[...] = scaled_pair(views[...], 1)

    def one(j, carry):
        here = pl.ds(pl.multiple_of(j * block, block), block)
        _, _, unit = unit_of(protos[here, :])
        unit16 = unit.astype(bf16)
        twice = jnp.concatenate([unit16, unit16], axis=1)
        running = jnp.zeros((8, block), f32)
        for c in range(rows // chunk):
            stage[c % 2] = dot(pair[c * chunk : (c + 1) * chunk, :], twice, NT)
            for start in range(0, chunk, tile):
                part = slice(c * chunk + start, c * chunk + start + tile)
                soft = jnp.exp2(stage[c % 2, start : start + tile, :])
                hard = soft * soft
                expo[part, here] = hard.astype(bf16)
                lanes = soft[:, :128]
                for k in range(1, block // 128):
                    lanes = lanes + soft[:, k * 128 : (k + 1) * 128]
                tot_acc[part, :] += lanes
                for k in range(0, tile, 8):
                    running = running + hard[k : k + 8]
        col[:, here] = jnp.sum(running, axis=0, keepdims=True)
        return carry

    lax.fori_loop(0, width // block, one, 0)
    tot[...] = jnp.sum(tot_acc[...].T, axis=0, keepdims=True)


def first_pass(views, protos):
    rows, depth = views.shape
    width = protos.shape[0]
    block = min(512, width)
    chunk = min(256, rows)
    tile = min(32, chunk)
    return pl.pallas_call(
        functools.partial(first_kernel, block, chunk, tile),
        in_specs=[WHOLE] * 2,
        out_specs=[WHOLE] * 3,
        out_shape=[
            pltpu.VMEM((rows, width), bf16),
            jax.ShapeDtypeStruct((1, width), f32),
            jax.ShapeDtypeStruct((1, rows), f32),
        ],
        scratch_shapes=[
            pltpu.VMEM((rows, 2 * depth), bf16),
            pltpu.VMEM((2, chunk, block), f32),
            pltpu.VMEM((rows, 128), f32),
        ],
        compiler_params=params(),
        cost_estimate=SMALL,
        name="first_pass",
    )(views, protos)


def sum_parts(parts, width):
    if len(parts[0].shape) == 3:
        parts = [parts[0].at[k] for k in range(parts[0].shape[0])]
    total = parts[0][:, :width]
    for other in parts[1:]:
        total = total + other[:, :width]
    return total


def add_fours(terms):
    total = None
    for k in range(0, len(terms), 4):
        four = terms[k : k + 4]
        while len(four) > 1:
            four = [x + y for x, y in zip(four[::2], four[1::2])]
        part = four[0].astype(f32)
        total = part if total is None else total + part
    return total


def rowsum_tile(expo, here, spread, tall, width):
    terms = []
    total = None
    for k in range(width // 128):
        lanes = slice(k * 128, (k + 1) * 128)
        weight = jnp.concatenate([spread[:, lanes]] * (tall // 16), axis=0)
        terms.append(expo[here, lanes] * weight)
        if len(terms) == 4 or k == width // 128 - 1:
            part = add_fours(terms)
            total = part if total is None else total + part
            terms = []
    return total


def rowsum_kernel(count, expo, *refs):
    parts = refs[:count]
    scale, out, spread, acc = refs[count:]
    rows, width = expo.shape
    inverse = 1.0 / sum_parts(parts, width)
    scale[...] = inverse
    spread[...] = jnp.broadcast_to(inverse, spread.shape).astype(bf16)
    tall = 64

    def one(i, carry):
        here = pl.ds(pl.multiple_of(i * tall, tall), tall)
        acc[here, :] = rowsum_tile(expo, here, spread, tall, width)
        return carry

    lax.fori_loop(0, rows // tall, one, 0)
    out[...] = jnp.sum(acc[...].T, axis=0, keepdims=True)


def rowsum(expo, parts):
    rows, width = expo.shape
    return pl.pallas_call(
        functools.partial(rowsum_kernel, len(parts)),
        in_specs=[WHOLE] * (1 + len(parts)),
        out_specs=[WHOLE] * 2,
        out_shape=[
            jax.ShapeDtypeStruct((1, width), f32),
            jax.ShapeDtypeStruct((1, rows), f32),
        ],
        scratch_shapes=[pltpu.VMEM((16, width), bf16), pltpu.VMEM((rows, 128), f32)],
        compiler_params=params(),
        cost_estimate=SMALL,
        name="rowsum",
    )(in_vmem(expo), *parts)


def split_rows(vec):
    hi = vec.astype(bf16).astype(f32)
    n = vec.shape[1]
    row = lax.broadcasted_iota(jnp.int32, (8, n), 0)
    hi8 = jnp.broadcast_to(hi, (8, n))
    lo8 = jnp.broadcast_to(vec - hi, (8, n))
    return jnp.where(row == 0, hi8, jnp.where(row == 1, lo8, 0.0))


def rowsum_last_kernel(pieces, count, *refs):
    expos = refs[:pieces]
    parts = refs[pieces : pieces + count]
    unit_t, scale, out, code, acc = refs[pieces + count :]
    step = pl.program_id(0)
    depth, block = unit_t.shape
    tall = expos[0].shape[0]
    inverse = 1.0 / sum_parts(parts, block)
    scale[...] = inverse
    scaled = unit_t[...].astype(f32) * inverse
    pad = jnp.zeros((depth - 8, block), f32)
    weights = jnp.concatenate([scaled, split_rows(inverse), pad], axis=0).astype(bf16)
    for k in range(pieces):
        part = slice(k * tall, (k + 1) * tall)
        found = dot(expos[k][...], weights, NT)

        @pl.when(step == 0)
        def _():
            acc[part, :] = found

        @pl.when(step > 0)
        def _():
            acc[part, :] += found

    @pl.when(step == pl.num_programs(0) - 1)
    def _():
        sums = acc[:, depth:].T
        out[...] = sums[0:1] + sums[1:2]
        code[...] = acc[:, :depth]


def rowsum_last(expo, parts, unit_t):
    rows, width = expo.shape
    depth = unit_t.shape[0]
    block = min(1024, width)
    pieces = 4
    tall = rows // pieces
    vec = pl.BlockSpec((1, block), lambda j: (0, j))
    return pl.pallas_call(
        functools.partial(rowsum_last_kernel, pieces, len(parts)),
        grid=(width // block,),
        in_specs=[pl.BlockSpec((tall, block), lambda j, k=k: (k, j)) for k in range(pieces)]
        + [vec] * len(parts)
        + [pl.BlockSpec((depth, block), lambda j: (0, j))],
        out_specs=[vec, full((1, rows)), full((rows, depth))],
        out_shape=[
            jax.ShapeDtypeStruct((1, width), f32),
            jax.ShapeDtypeStruct((1, rows), f32),
            jax.ShapeDtypeStruct((rows, depth), f32),
        ],
        scratch_shapes=[pltpu.VMEM((rows, 2 * depth), f32)],
        compiler_params=params("arbitrary"),
        cost_estimate=SMALL,
        name="rowsum_last",
    )(*[in_hbm(expo)] * pieces, *parts, in_hbm(unit_t))


def unit_t_kernel(block, protos, out):
    def one(j, carry):
        here = pl.ds(pl.multiple_of(j * block, block), block)
        _, _, unit = unit_of(protos[here, :])
        out[:, here] = unit.astype(bf16).astype(f32).T.astype(bf16)
        return carry

    lax.fori_loop(0, protos.shape[0] // block, one, 0)


def unit_transposed(protos):
    width, depth = protos.shape
    return pl.pallas_call(
        functools.partial(unit_t_kernel, min(512, width)),
        in_specs=[WHOLE],
        out_specs=WHOLE,
        out_shape=jax.ShapeDtypeStruct((depth, width), bf16),
        compiler_params=params(),
        cost_estimate=SMALL,
        name="unit_t",
    )(protos)


def colsum_kernel(count, expo, *refs):
    parts = refs[:count]
    rest = refs[count:]
    out, spread = rest[-2:]
    rows, width = expo.shape
    inverse = 1.0 / sum_parts(parts, rows)
    spread[...] = jnp.broadcast_to(inverse, (128, rows)).T.astype(bf16)
    block = min(512, width)

    def one(j, carry):
        here = pl.ds(pl.multiple_of(j * block, block), block)
        running = jnp.zeros((16, block), f32)
        for i in range(0, rows // 16, 4):
            terms = []
            for k in range(i, min(i + 4, rows // 16)):
                part = slice(k * 16, (k + 1) * 16)
                weight = jnp.concatenate([spread[part, :]] * (block // 128), axis=1)
                terms.append(expo[part, here] * weight)
            running = running + add_fours(terms)
        total = jnp.sum(running, axis=0, keepdims=True)
        for k in range(out.shape[0]):
            out[k, :, here] = total
        return carry

    lax.fori_loop(0, width // block, one, 0)
    if len(rest) > 2:
        for k in range(out.shape[0]):
            out[k, :, width:] = rest[0][...]


def colsum(expo, parts, copies=1, behind=()):
    rows, width = expo.shape
    long = width + sum(x.shape[1] for x in behind)
    return pl.pallas_call(
        functools.partial(colsum_kernel, len(parts)),
        in_specs=[WHOLE] * (1 + len(parts) + len(behind)),
        out_specs=WHOLE,
        out_shape=jax.ShapeDtypeStruct((copies, 1, long), f32),
        scratch_shapes=[pltpu.VMEM((rows, 128), bf16)],
        compiler_params=params(),
        cost_estimate=SMALL,
        name="colsum",
    )(in_vmem(expo), *parts, *behind)


def proto_first_kernel(chunk, tile, lead, place, protos, views, totals, expo, grad, *scratch):
    weights, twice, pair, stage, soft16, acc = scratch
    count = expo.shape[1] // views.shape[2]
    _, depth, rows = views.shape
    width = protos.shape[0]
    _, _, unit = unit_of(protos[...])
    pair[...] = scaled_pair(unit.astype(bf16), 1)
    for n in range(count):
        k = lead + n
        weights[...] = (views[k].astype(f32) * (GRAD_SCALE / totals[place[0] ^ k])).astype(bf16)
        twice[:depth, :] = views[k]
        twice[depth:, :] = views[k]
        for c in range(width // chunk):
            stage[c % 2] = dot(pair[c * chunk : (c + 1) * chunk, :], twice[...])
            for start in range(0, chunk, tile):
                part = slice(c * chunk + start, c * chunk + start + tile)
                soft = jnp.exp2(stage[c % 2, start : start + tile, :])
                soft16[part, :] = soft.astype(bf16)
                expo[part, n * rows : (n + 1) * rows] = (soft * soft).astype(bf16)
        found = dot(soft16[...], weights[...], NT)
        if n == 0:
            acc[...] = found
        else:
            acc[...] += found
    grad[...] = acc[...]


def proto_first(place, protos, views, totals, lead, count):
    width, depth = protos.shape
    rows = views.shape[2]
    chunk = min(256, width)
    tile = min(16, chunk)
    return pl.pallas_call(
        functools.partial(proto_first_kernel, chunk, tile, lead),
        in_specs=[pl.BlockSpec(memory_space=pltpu.SMEM)] + [WHOLE] * 3,
        out_specs=[WHOLE] * 2,
        out_shape=[
            pltpu.VMEM((width, count * rows), bf16),
            jax.ShapeDtypeStruct((width, depth), f32),
        ],
        scratch_shapes=[
            pltpu.VMEM((depth, rows), bf16),
            pltpu.VMEM((2 * depth, rows), bf16),
            pltpu.VMEM((width, 2 * depth), bf16),
            pltpu.VMEM((2, chunk, rows), f32),
            pltpu.VMEM((width, rows), bf16),
            pltpu.VMEM((width, depth), f32),
        ],
        compiler_params=params(),
        cost_estimate=SMALL,
        name="proto_first",
    )(place, protos, views, totals)


def proto_last_kernel(groups, place, *refs):
    expos, grads = refs[:groups], refs[groups : 2 * groups]
    scale, protos, views, totals, out, weights, acc = refs[2 * groups :]
    count, depth, rows = views.shape
    each = count // groups
    for k in range(count):
        mates = swap_lanes(views[k])
        weights[...] = (mates.astype(f32) * (GRAD_SCALE / totals[place[0] ^ k])).astype(bf16)
        found = dot(expos[k // each][:, (k % each) * rows : (k % each + 1) * rows], weights[...], NT)
        if k == 0:
            acc[...] = found
        else:
            acc[...] += found
    width = protos.shape[0]
    there = pl.ds(pl.multiple_of(place[0] * width, width), width)
    unit_grad = grads[0][...]
    for other in grads[1:]:
        unit_grad = unit_grad + other[...]
    unit_grad = unit_grad - to_column(scale[:, there]) * acc[...]
    proto_f, inv, _ = unit_of(protos[...])
    inner = jnp.sum(proto_f * unit_grad, axis=1, keepdims=True)
    out[...] = (inv * unit_grad - proto_f * (inv * inv * inv) * inner).astype(bf16)


def proto_last(place, expos, grads, scale, protos, views, totals):
    width, depth = protos.shape
    rows = views.shape[2]
    groups = len(expos)
    return pl.pallas_call(
        functools.partial(proto_last_kernel, groups),
        in_specs=[pl.BlockSpec(memory_space=pltpu.SMEM)] + [WHOLE] * (2 * groups + 4),
        out_specs=WHOLE,
        out_shape=jax.ShapeDtypeStruct((width, depth), bf16),
        scratch_shapes=[pltpu.VMEM((depth, rows), bf16), pltpu.VMEM((width, depth), f32)],
        compiler_params=params(),
        name="proto_last",
    )(place, *[in_vmem(x) for x in expos], *grads, scale, protos, views, totals)


def view_soft_kernel(block, tile, lead, views, protos, out, pair, stage, soft16):
    rows, depth = views.shape
    pair[...] = scaled_pair(views[...], 1)
    out[...] = jnp.zeros_like(out)
    chunk = stage.shape[1]

    def one(j, carry):
        here = pl.ds(pl.multiple_of(lead + j * block, block), block)
        _, _, unit = unit_of(protos[here, :])
        unit16 = unit.astype(bf16)
        twice = jnp.concatenate([unit16, unit16], axis=1)
        for c in range(rows // chunk):
            stage[c % 2] = dot(pair[c * chunk : (c + 1) * chunk, :], twice, NT)
            for start in range(0, chunk, tile):
                part = slice(c * chunk + start, c * chunk + start + tile)
                soft16[part, :] = jnp.exp2(stage[c % 2, start : start + tile, :]).astype(bf16)
        out[...] += dot(soft16[...], unit16)
        return carry

    return one


def view_soft_body(block, tile, lead, count, *refs):
    lax.fori_loop(0, count // block, view_soft_kernel(block, tile, lead, *refs), 0)


def view_soft(views, protos, lead, count):
    rows, depth = views.shape
    block = min(512, count)
    chunk = min(256, rows)
    return pl.pallas_call(
        functools.partial(view_soft_body, block, min(32, chunk), lead, count),
        in_specs=[WHOLE] * 2,
        out_specs=WHOLE,
        out_shape=jax.ShapeDtypeStruct((rows, depth), f32),
        scratch_shapes=[
            pltpu.VMEM((rows, 2 * depth), bf16),
            pltpu.VMEM((2, chunk, block), f32),
            pltpu.VMEM((rows, block), bf16),
        ],
        compiler_params=params(),
        cost_estimate=SMALL,
        name="view_soft",
    )(views, protos)


def view_grad_kernel(code, tot, total, *refs):
    softs, out = refs[:-1], refs[-1]
    soft = softs[0][...]
    for other in softs[1:]:
        soft = soft + other[...]
    soft = soft * to_column(GRAD_SCALE / tot[...])
    hard = swap_rows(code[...] * to_column(GRAD_SCALE / total[...]))
    out[...] = (soft - hard).astype(out.dtype)


def view_grad_part(code, tot, total, *softs):
    return pl.pallas_call(
        view_grad_kernel,
        in_specs=[WHOLE] * (3 + len(softs)),
        out_specs=WHOLE,
        out_shape=jax.ShapeDtypeStruct(code.shape, bf16),
        compiler_params=params(),
        cost_estimate=SMALL,
        name="view_grad",
    )(code, tot, total, *softs)


def backward_kernel(grad_a, grad_b, pos, raw, pre, emb, hid_part, w_out, out):
    total = grad_a[...].astype(f32) + grad_b[...].astype(f32)
    n, depth = raw.shape
    place = jnp.broadcast_to(pos[...].astype(f32), (8, n)).T[:, :1].astype(jnp.int32)
    lane = lax.broadcasted_iota(jnp.int32, (n, n), 1)
    move = jnp.where(lane == place, 1.0, 0.0).astype(bf16)
    hi = total.astype(bf16)
    lo = (total - hi.astype(f32)).astype(bf16)
    moved = dot(move, jnp.concatenate([hi, lo], axis=1))
    grad = moved[:, :depth] + moved[:, depth:]
    raw_out = raw[...]
    inv = lax.rsqrt(jnp.sum(raw_out * raw_out, axis=1, keepdims=True) + norm_eps)
    inner = jnp.sum(raw_out * grad, axis=1, keepdims=True)
    d_raw = (inv * grad - raw_out * (inv * inv * inv) * inner).astype(bf16)
    g_out = dot(hid_part[...], d_raw, TN)
    d_hidden = dot(d_raw, w_out[...], NT)
    v = pre[...]
    t = jnp.tanh(GELU_K * (v + GELU_A * (v * v * v)))
    slope = 0.5 * (1.0 + t) + (0.5 * GELU_K) * v * (1.0 - t * t) * (1.0 + (3.0 * GELU_A) * (v * v))
    d_pre = (slope * d_hidden).astype(bf16)
    g_in = dot(emb[...], d_pre, TN)
    count = out.shape[0]
    tall, wide = g_in.shape[0] // count, g_in.shape[1]
    base, short = tall * (wide // 128), g_out.shape[0] // count
    for k in range(count):
        n = mirrored(k, count)
        for q in range(wide // 128):
            out[n, q * tall : (q + 1) * tall, :] = g_in[
                k * tall : (k + 1) * tall, q * 128 : (q + 1) * 128
            ]
        out[n, base : base + short, :] = g_out[k * short : (k + 1) * short]


def mirrored(k, count):
    found = 0
    while count > 1:
        found = found * 2 + k % 2
        k //= 2
        count //= 2
    return found


def backward(nb, grad_a, grad_b, pos, raw, pre, emb, hid_part, w_out):
    lines = (emb.shape[1] * pre.shape[1] + hid_part.shape[1] * raw.shape[1]) // (nb * 128)
    return pl.pallas_call(
        backward_kernel,
        in_specs=[WHOLE] * 8,
        out_specs=WHOLE,
        out_shape=jax.ShapeDtypeStruct((nb, lines, 128), f32),
        compiler_params=params(),
        name="backward",
    )(grad_a, grad_b, pos, raw, pre, emb, hid_part, w_out)


def unpack_kernel(order, order_b, place, *refs):
    pieces, (g_in, g_out) = refs[:-2], refs[-2:]
    nb = len(order_b)
    npr = len(order)
    tall, wide = g_in.shape[0] // (nb * npr), g_in.shape[1]
    base, short = tall * (wide // 128), g_out.shape[0] // (nb * npr)
    half = pieces[0].shape[0]
    for n, flip in enumerate(order):
        for k, flip_b in enumerate(order_b):
            owner = (place[0] ^ flip) * nb + (place[1] ^ flip_b)
            x = pieces[n // half][n % half, k].astype(f32)
            low = pl.multiple_of(owner * tall, tall)
            for q in range(wide // 128):
                g_in[pl.ds(low, tall), q * 128 : (q + 1) * 128] = x[q * tall : (q + 1) * tall]
            low = pl.multiple_of(owner * short, short)
            g_out[pl.ds(low, short), :] = x[base : base + short]


def unpack(order, order_b, place, pieces, shape_in, shape_out):
    return pl.pallas_call(
        functools.partial(unpack_kernel, order, order_b),
        in_specs=[pl.BlockSpec(memory_space=pltpu.SMEM)] + [WHOLE] * len(pieces),
        out_specs=[WHOLE] * 2,
        out_shape=[jax.ShapeDtypeStruct(shape_in, f32), jax.ShapeDtypeStruct(shape_out, f32)],
        compiler_params=params(),
        name="unpack",
    )(place, *pieces)


def body(nb, npr, embeddings, pairing, w_in, w_out, prototypes):
    b = lax.axis_index("batch")
    p = lax.axis_index("proto")
    rows, wide = embeddings.shape
    width, depth = prototypes.shape
    hidden_n = w_in.shape[1]
    own = width // nb

    def flipped(x, axis, size, step):
        return lax.ppermute(x, axis, [(i, i ^ step) for i in range(size)])

    def exchange(x, axis, size, step, queue, results):
        other = flipped(x, axis, size, step)
        if queue:
            work, operands = queue.pop(0)
            operands, _ = lax.optimization_barrier((operands, x))
            other, found = lax.optimization_barrier((other, work(*operands)))
            results.append(found)
        return other

    def doubled(x, axis, size, queue=(), results=None):
        step = 1
        while step * 2 < size:
            x = x + exchange(x, axis, size, step, queue, results)
            step *= 2
        return [x, exchange(x, axis, size, step, queue, results)]

    pre, hid, raw, views, views_t, pos = head(embeddings, pairing, w_in, w_out)
    views_all = lax.all_gather(views_t, "batch", axis=0)
    protos_own = lax.dynamic_slice_in_dim(prototypes, b * own, own, 0)
    place = b.astype(jnp.int32).reshape(1)
    views, protos_own, place = lax.optimization_barrier((views, protos_own, place))
    expo, col, tot = first_pass(views, prototypes)

    groups = 4
    cols = width // groups
    softs = []
    queue = [
        (functools.partial(view_soft, lead=k * cols, count=cols), (views, prototypes))
        for k in range(groups)
    ]
    scale, row = rowsum(expo, doubled(col, "batch", nb, queue, softs))
    first, second = doubled(jnp.concatenate([row, tot], axis=0), "proto", npr, queue, softs)
    both = first + second
    totals, tot = [both[:1]], both[1:]

    col = colsum(expo, totals)[0]
    tot_all = tot[None]
    step = 1
    while step < nb:
        other = flipped(tot_all, "batch", nb, step)
        part = flipped(col, "batch", nb, step)
        other, part = lax.optimization_barrier((other, part))
        tot_all = jnp.concatenate([tot_all, other], axis=0)
        step *= 2
        if step < nb:
            col = col + part
    scale, row = rowsum(expo, [col, part])
    units = []
    queue = [(unit_transposed, (prototypes,))]
    col = colsum(expo, doubled(row, "proto", npr, queue, units))[0]

    col, views_all = lax.optimization_barrier((col, views_all))
    each = nb // groups
    owns = []
    queue = [
        (
            functools.partial(proto_first, lead=k * each, count=each),
            (place, protos_own, views_all, tot_all),
        )
        for k in range(groups)
    ]
    scale, row, code = rowsum_last(expo, doubled(col, "batch", nb, queue, owns), units[0])
    first, second = doubled(row, "proto", npr, queue, owns)
    total = first + second
    total_all = total[None]
    grads = []
    queue = [(view_grad_part, (code, tot, total, *softs))]
    step = 1
    turn = 1
    while step < nb:
        other = exchange(total_all, "batch", nb, step, queue, grads)
        if step > 1 and turn < npr:
            if len(grads) > 1:
                grads = [(grads[0].astype(f32) + grads[1].astype(f32)).astype(bf16)]
            grads = [grads[0], flipped(grads[0], "proto", npr, turn)]
            turn *= 2
        total_all = jnp.concatenate([total_all, other], axis=0)
        step *= 2

    proto_part = proto_last(
        place,
        [x for x, _ in owns],
        [x for _, x in owns],
        scale,
        protos_own,
        views_all,
        total_all,
    )
    grad_proto = lax.all_gather(proto_part, "batch", axis=0, tiled=True)

    while turn < npr:
        if len(grads) > 1:
            grads = [(grads[0].astype(f32) + grads[1].astype(f32)).astype(bf16)]
        grads = [grads[0], flipped(grads[0], "proto", npr, turn)]
        turn *= 2
    emb_part = lax.dynamic_slice_in_dim(embeddings, p * (wide // npr), wide // npr, 1)
    hid_part = lax.dynamic_slice_in_dim(hid, p * (hidden_n // npr), hidden_n // npr, 1)
    both = backward(nb, *grads, pos, raw, pre, emb_part, hid_part, w_out)
    step = 1
    while step < nb:
        half = both.shape[0] // 2
        bit = (b // step) % 2
        away = lax.dynamic_slice_in_dim(both, (1 - bit) * half, half, 0).astype(bf16)
        kept = lax.dynamic_slice_in_dim(both, bit * half, half, 0)
        both = kept + flipped(away, "batch", nb, step).astype(f32)
        step *= 2
    piece = both.astype(bf16)
    order_b = [0]
    while step > 1:
        step //= 2
        piece = jnp.concatenate([piece, flipped(piece, "batch", nb, step)], axis=0)
        order_b = order_b + [i ^ step for i in order_b]
    piece = piece[None]
    order = [0]
    step = npr // 2
    while step > 1:
        piece = jnp.concatenate([piece, flipped(piece, "proto", npr, step)], axis=0)
        order = order + [i ^ step for i in order]
        step //= 2
    pieces = [piece, flipped(piece, "proto", npr, 1)]
    order = order + [i ^ 1 for i in order]
    places = jnp.stack([p, b]).astype(jnp.int32)
    grad_in, grad_out = unpack(
        order, order_b, places, pieces, (wide, hidden_n), (hidden_n, depth)
    )
    return (grad_in, grad_out, grad_proto.astype(f32))


def solution(mesh):
    return jax.shard_map(
        functools.partial(body, mesh.shape["batch"], mesh.shape["proto"]),
        mesh=mesh,
        in_specs=(P("batch", None), P("batch"), P(), P(), P("proto", None)),
        out_specs=(P(), P(), P("proto", None)),
        check_vma=False,
    )
```

```python
import functools
import math

import jax
import jax.numpy as jnp
from jax import lax
from jax.experimental import pallas as pl
from jax.experimental.pallas import tpu as pltpu
from jax.sharding import PartitionSpec as P

ITERS = 3
norm_eps = 1e-06
code_temp = 0.05
pred_temp = 0.1
loss_scale = 64.0
GRAD_SCALE = loss_scale / pred_temp
EXP2_SCALE = math.log2(math.e) / pred_temp
GELU_K = math.sqrt(2.0 / math.pi)
GELU_A = 0.044715

f32 = jnp.float32
bf16 = jnp.bfloat16
NN = (((1,), (0,)), ((), ()))
NT = (((1,), (1,)), ((), ()))
TN = (((0,), (0,)), ((), ()))
VMEM_LIMIT = 12 * 1024 * 1024


def dot(a, b, dims=NN):
    return lax.dot_general(a, b, dims, preferred_element_type=f32)


SMALL = pl.CostEstimate(flops=1000, bytes_accessed=1000, transcendentals=0)


def params(*semantics, limit=VMEM_LIMIT):
    return pltpu.CompilerParams(dimension_semantics=semantics or None, vmem_limit_bytes=limit)


def to_column(vec):
    n = vec.shape[1]
    return jnp.broadcast_to(vec, (8, n)).T[:, :1]


def swap_lanes(x):
    half = x.shape[1] // 2
    return jnp.concatenate([x[:, half:], x[:, :half]], axis=1)


def swap_rows(x):
    half = x.shape[0] // 2
    return jnp.concatenate([x[half:], x[:half]], axis=0)


def in_vmem(x):
    return pltpu.with_memory_space_constraint(x, pltpu.VMEM)


def in_hbm(x):
    return pltpu.with_memory_space_constraint(x, pltpu.HBM)


def full(shape):
    return pl.BlockSpec(shape, lambda *_: (0,) * len(shape))


def head_kernel(emb, pairing, w_in, w_out, pre, hid, raw, views, views_t, pos, scratch):
    step = pl.program_id(0)
    rows = emb.shape[0]
    pre_act = dot(emb[...], w_in[...])
    pre[...] = pre_act
    t = jnp.tanh(GELU_K * (pre_act + GELU_A * (pre_act * pre_act * pre_act)))
    hidden = (0.5 * pre_act * (1.0 + t)).astype(bf16)
    hid[...] = hidden
    raw_out = dot(hidden, w_out[...])
    raw[...] = raw_out
    inv = lax.rsqrt(jnp.sum(raw_out * raw_out, axis=1, keepdims=True) + norm_eps)
    scratch[pl.ds(pl.multiple_of(step * rows, rows), rows), :] = (raw_out * inv).astype(bf16)

    @pl.when(step == pl.num_programs(0) - 1)
    def _():
        mate = pairing[...]
        n = mate.shape[1]
        lane = lax.broadcasted_iota(jnp.int32, (1, n), 1)
        first = lane < mate
        low = jnp.minimum(lane, mate)
        sub = lax.broadcasted_iota(jnp.int32, (n, n), 0)
        before = jnp.where(sub < low, 1.0, 0.0).astype(bf16)
        first8 = jnp.broadcast_to(jnp.where(first, 1.0, 0.0), (8, n)).astype(bf16)
        rank = dot(first8, before)[:1].astype(jnp.int32)
        place = jnp.where(first, rank, rank + n // 2)
        pos[...] = place
        move = jnp.where(sub == place, 1.0, 0.0).astype(bf16)
        ordered = dot(move, scratch[...])
        views[...] = ordered.astype(bf16)
        views_t[...] = ordered.T.astype(bf16)


def head(embeddings, pairing, w_in, w_out):
    rows, wide = embeddings.shape
    hidden = w_in.shape[1]
    depth = w_out.shape[1]
    steps = 4
    block = rows // steps
    return pl.pallas_call(
        head_kernel,
        grid=(steps,),
        in_specs=[
            pl.BlockSpec((block, wide), lambda i: (i, 0)),
            full((1, rows)),
            full((wide, hidden)),
            full((hidden, depth)),
        ],
        out_specs=[
            pl.BlockSpec((block, hidden), lambda i: (i, 0)),
            pl.BlockSpec((block, hidden), lambda i: (i, 0)),
            pl.BlockSpec((block, depth), lambda i: (i, 0)),
            full((rows, depth)),
            full((depth, rows)),
            full((1, rows)),
        ],
        out_shape=[
            pltpu.HBM((rows, hidden), f32),
            pltpu.HBM((rows, hidden), bf16),
            pltpu.HBM((rows, depth), f32),
            jax.ShapeDtypeStruct((rows, depth), bf16),
            jax.ShapeDtypeStruct((depth, rows), bf16),
            jax.ShapeDtypeStruct((1, rows), jnp.int32),
        ],
        scratch_shapes=[pltpu.VMEM((rows, depth), bf16)],
        compiler_params=params("arbitrary"),
        name="head",
    )(in_hbm(embeddings), pairing.reshape(1, rows), in_hbm(w_in), in_hbm(w_out))


def unit_of(protos):
    proto_f = protos.astype(f32)
    inv = lax.rsqrt(jnp.sum(proto_f * proto_f, axis=1, keepdims=True) + norm_eps)
    return proto_f, inv, proto_f * inv


WHOLE = pl.BlockSpec(memory_space=pltpu.VMEM)


def scaled_pair(x, axis):
    wide = x.astype(f32) * EXP2_SCALE
    hi = wide.astype(bf16)
    lo = (wide - hi.astype(f32)).astype(bf16)
    return jnp.concatenate([hi, lo], axis=axis)


def first_kernel(block, chunk, tile, views, protos, expo, col, tot, pair, stage, tot_acc):
    rows, depth = views.shape
    width = protos.shape[0]
    tot_acc[...] = jnp.zeros_like(tot_acc)
    pair[...] = scaled_pair(views[...], 1)

    def one(j, carry):
        here = pl.ds(pl.multiple_of(j * block, block), block)
        _, _, unit = unit_of(protos[here, :])
        unit16 = unit.astype(bf16)
        twice = jnp.concatenate([unit16, unit16], axis=1)
        running = jnp.zeros((8, block), f32)
        for c in range(rows // chunk):
            stage[c % 2] = dot(pair[c * chunk : (c + 1) * chunk, :], twice, NT)
            for start in range(0, chunk, tile):
                part = slice(c * chunk + start, c * chunk + start + tile)
                soft = jnp.exp2(stage[c % 2, start : start + tile, :])
                hard = soft * soft
                expo[part, here] = hard.astype(bf16)
                lanes = soft[:, :128]
                for k in range(1, block // 128):
                    lanes = lanes + soft[:, k * 128 : (k + 1) * 128]
                tot_acc[part, :] += lanes
                for k in range(0, tile, 8):
                    running = running + hard[k : k + 8]
        col[:, here] = jnp.sum(running, axis=0, keepdims=True)
        return carry

    lax.fori_loop(0, width // block, one, 0)
    tot[...] = jnp.sum(tot_acc[...].T, axis=0, keepdims=True)


def first_pass(views, protos):
    rows, depth = views.shape
    width = protos.shape[0]
    block = min(512, width)
    chunk = min(256, rows)
    tile = min(32, chunk)
    return pl.pallas_call(
        functools.partial(first_kernel, block, chunk, tile),
        in_specs=[WHOLE] * 2,
        out_specs=[WHOLE] * 3,
        out_shape=[
            pltpu.VMEM((rows, width), bf16),
            jax.ShapeDtypeStruct((1, width), f32),
            jax.ShapeDtypeStruct((1, rows), f32),
        ],
        scratch_shapes=[
            pltpu.VMEM((rows, 2 * depth), bf16),
            pltpu.VMEM((2, chunk, block), f32),
            pltpu.VMEM((rows, 128), f32),
        ],
        compiler_params=params(),
        cost_estimate=SMALL,
        name="first_pass",
    )(views, protos)


def sum_parts(parts, width):
    if len(parts[0].shape) == 3:
        parts = [parts[0].at[k] for k in range(parts[0].shape[0])]
    total = parts[0][:, :width]
    for other in parts[1:]:
        total = total + other[:, :width]
    return total


def add_fours(terms):
    total = None
    for k in range(0, len(terms), 4):
        four = terms[k : k + 4]
        while len(four) > 1:
            four = [x + y for x, y in zip(four[::2], four[1::2])]
        part = four[0].astype(f32)
        total = part if total is None else total + part
    return total


def rowsum_tile(expo, here, spread, tall, width):
    terms = []
    total = None
    for k in range(width // 128):
        lanes = slice(k * 128, (k + 1) * 128)
        weight = jnp.concatenate([spread[:, lanes]] * (tall // 16), axis=0)
        terms.append(expo[here, lanes] * weight)
        if len(terms) == 4 or k == width // 128 - 1:
            part = add_fours(terms)
            total = part if total is None else total + part
            terms = []
    return total


def rowsum_kernel(count, expo, *refs):
    parts = refs[:count]
    scale, out, spread, acc = refs[count:]
    rows, width = expo.shape
    inverse = 1.0 / sum_parts(parts, width)
    scale[...] = inverse
    spread[...] = jnp.broadcast_to(inverse, spread.shape).astype(bf16)
    tall = 64

    def one(i, carry):
        here = pl.ds(pl.multiple_of(i * tall, tall), tall)
        acc[here, :] = rowsum_tile(expo, here, spread, tall, width)
        return carry

    lax.fori_loop(0, rows // tall, one, 0)
    out[...] = jnp.sum(acc[...].T, axis=0, keepdims=True)


def rowsum(expo, parts):
    rows, width = expo.shape
    return pl.pallas_call(
        functools.partial(rowsum_kernel, len(parts)),
        in_specs=[WHOLE] * (1 + len(parts)),
        out_specs=[WHOLE] * 2,
        out_shape=[
            jax.ShapeDtypeStruct((1, width), f32),
            jax.ShapeDtypeStruct((1, rows), f32),
        ],
        scratch_shapes=[pltpu.VMEM((16, width), bf16), pltpu.VMEM((rows, 128), f32)],
        compiler_params=params(),
        cost_estimate=SMALL,
        name="rowsum",
    )(in_vmem(expo), *parts)


def split_rows(vec):
    hi = vec.astype(bf16).astype(f32)
    n = vec.shape[1]
    row = lax.broadcasted_iota(jnp.int32, (8, n), 0)
    hi8 = jnp.broadcast_to(hi, (8, n))
    lo8 = jnp.broadcast_to(vec - hi, (8, n))
    return jnp.where(row == 0, hi8, jnp.where(row == 1, lo8, 0.0))


def rowsum_last_kernel(pieces, count, *refs):
    expos = refs[:pieces]
    parts = refs[pieces : pieces + count]
    unit_t, scale, out, code, acc = refs[pieces + count :]
    step = pl.program_id(0)
    depth, block = unit_t.shape
    deep = expos[0].shape[1]
    inverse = 1.0 / sum_parts(parts, block)
    scale[...] = inverse

    @pl.when(step == 0)
    def _():
        acc[...] = jnp.zeros_like(acc)

    for k in range(pieces):
        here = slice(k * deep, (k + 1) * deep)
        scaled = unit_t[:, here].astype(f32) * inverse[:, here]
        pad = jnp.zeros((depth - 8, deep), f32)
        weights = jnp.concatenate([scaled, split_rows(inverse[:, here]), pad], axis=0)
        acc[...] += dot(expos[k][...], weights.astype(bf16), NT)

    @pl.when(step == pl.num_programs(0) - 1)
    def _():
        sums = acc[:, depth:].T
        out[...] = sums[0:1] + sums[1:2]
        code[...] = acc[:, :depth]


def rowsum_last(expo, parts, unit_t):
    rows, width = expo.shape
    depth = unit_t.shape[0]
    block = min(2048, width)
    pieces = 4
    deep = block // pieces
    vec = pl.BlockSpec((1, block), lambda j: (0, j))
    return pl.pallas_call(
        functools.partial(rowsum_last_kernel, pieces, len(parts)),
        grid=(width // block,),
        in_specs=[
            pl.BlockSpec((rows, deep), lambda j, k=k: (0, j * pieces + k)) for k in range(pieces)
        ]
        + [vec] * len(parts)
        + [pl.BlockSpec((depth, block), lambda j: (0, j))],
        out_specs=[vec, full((1, rows)), full((rows, depth))],
        out_shape=[
            jax.ShapeDtypeStruct((1, width), f32),
            jax.ShapeDtypeStruct((1, rows), f32),
            jax.ShapeDtypeStruct((rows, depth), f32),
        ],
        scratch_shapes=[pltpu.VMEM((rows, 2 * depth), f32)],
        compiler_params=params("arbitrary", limit=VMEM_LIMIT + 4 * 1024 * 1024),
        cost_estimate=SMALL,
        name="rowsum_last",
    )(*[in_hbm(expo)] * pieces, *parts, in_hbm(unit_t))


def unit_t_kernel(block, protos, out):
    def one(j, carry):
        here = pl.ds(pl.multiple_of(j * block, block), block)
        _, _, unit = unit_of(protos[here, :])
        out[:, here] = unit.astype(bf16).astype(f32).T.astype(bf16)
        return carry

    lax.fori_loop(0, protos.shape[0] // block, one, 0)


def unit_transposed(protos):
    width, depth = protos.shape
    return pl.pallas_call(
        functools.partial(unit_t_kernel, min(512, width)),
        in_specs=[WHOLE],
        out_specs=WHOLE,
        out_shape=jax.ShapeDtypeStruct((depth, width), bf16),
        compiler_params=params(),
        cost_estimate=SMALL,
        name="unit_t",
    )(protos)


def colsum_kernel(count, expo, *refs):
    parts = refs[:count]
    rest = refs[count:]
    out, spread = rest[-2:]
    rows, width = expo.shape
    inverse = 1.0 / sum_parts(parts, rows)
    spread[...] = jnp.broadcast_to(inverse, (128, rows)).T.astype(bf16)
    block = min(512, width)

    def one(j, carry):
        here = pl.ds(pl.multiple_of(j * block, block), block)
        running = jnp.zeros((16, block), f32)
        for i in range(0, rows // 16, 4):
            terms = []
            for k in range(i, min(i + 4, rows // 16)):
                part = slice(k * 16, (k + 1) * 16)
                weight = jnp.concatenate([spread[part, :]] * (block // 128), axis=1)
                terms.append(expo[part, here] * weight)
            running = running + add_fours(terms)
        total = jnp.sum(running, axis=0, keepdims=True)
        for k in range(out.shape[0]):
            out[k, :, here] = total
        return carry

    lax.fori_loop(0, width // block, one, 0)
    if len(rest) > 2:
        for k in range(out.shape[0]):
            out[k, :, width:] = rest[0][...]


def colsum(expo, parts, copies=1, behind=()):
    rows, width = expo.shape
    long = width + sum(x.shape[1] for x in behind)
    return pl.pallas_call(
        functools.partial(colsum_kernel, len(parts)),
        in_specs=[WHOLE] * (1 + len(parts) + len(behind)),
        out_specs=WHOLE,
        out_shape=jax.ShapeDtypeStruct((copies, 1, long), f32),
        scratch_shapes=[pltpu.VMEM((rows, 128), bf16)],
        compiler_params=params(),
        cost_estimate=SMALL,
        name="colsum",
    )(in_vmem(expo), *parts, *behind)


def proto_first_kernel(chunk, tile, lead, place, protos, views, totals, expo, grad, *scratch):
    weights, twice, pair, stage, soft16, acc = scratch
    count = expo.shape[1] // views.shape[2]
    _, depth, rows = views.shape
    width = protos.shape[0]
    _, _, unit = unit_of(protos[...])
    pair[...] = scaled_pair(unit.astype(bf16), 1)
    for n in range(count):
        k = lead + n
        weights[...] = (views[k].astype(f32) * (GRAD_SCALE / totals[place[0] ^ k])).astype(bf16)
        twice[:depth, :] = views[k]
        twice[depth:, :] = views[k]
        for c in range(width // chunk):
            stage[c % 2] = dot(pair[c * chunk : (c + 1) * chunk, :], twice[...])
            for start in range(0, chunk, tile):
                part = slice(c * chunk + start, c * chunk + start + tile)
                soft = jnp.exp2(stage[c % 2, start : start + tile, :])
                soft16[part, :] = soft.astype(bf16)
                expo[part, n * rows : (n + 1) * rows] = (soft * soft).astype(bf16)
        found = dot(soft16[...], weights[...], NT)
        if n == 0:
            acc[...] = found
        else:
            acc[...] += found
    grad[...] = acc[...]


def proto_first(place, protos, views, totals, lead, count):
    width, depth = protos.shape
    rows = views.shape[2]
    chunk = min(256, width)
    tile = min(16, chunk)
    return pl.pallas_call(
        functools.partial(proto_first_kernel, chunk, tile, lead),
        in_specs=[pl.BlockSpec(memory_space=pltpu.SMEM)] + [WHOLE] * 3,
        out_specs=[WHOLE] * 2,
        out_shape=[
            pltpu.VMEM((width, count * rows), bf16),
            jax.ShapeDtypeStruct((width, depth), f32),
        ],
        scratch_shapes=[
            pltpu.VMEM((depth, rows), bf16),
            pltpu.VMEM((2 * depth, rows), bf16),
            pltpu.VMEM((width, 2 * depth), bf16),
            pltpu.VMEM((2, chunk, rows), f32),
            pltpu.VMEM((width, rows), bf16),
            pltpu.VMEM((width, depth), f32),
        ],
        compiler_params=params(),
        cost_estimate=SMALL,
        name="proto_first",
    )(place, protos, views, totals)


def proto_last_kernel(groups, place, *refs):
    expos, grads = refs[:groups], refs[groups : 2 * groups]
    scale, protos, views, totals, out, weights, acc = refs[2 * groups :]
    count, depth, rows = views.shape
    each = count // groups
    for k in range(count):
        mates = swap_lanes(views[k])
        weights[...] = (mates.astype(f32) * (GRAD_SCALE / totals[place[0] ^ k])).astype(bf16)
        found = dot(expos[k // each][:, (k % each) * rows : (k % each + 1) * rows], weights[...], NT)
        if k == 0:
            acc[...] = found
        else:
            acc[...] += found
    width = protos.shape[0]
    there = pl.ds(pl.multiple_of(place[0] * width, width), width)
    unit_grad = grads[0][...]
    for other in grads[1:]:
        unit_grad = unit_grad + other[...]
    unit_grad = unit_grad - to_column(scale[:, there]) * acc[...]
    proto_f, inv, _ = unit_of(protos[...])
    inner = jnp.sum(proto_f * unit_grad, axis=1, keepdims=True)
    out[...] = (inv * unit_grad - proto_f * (inv * inv * inv) * inner).astype(bf16)


def proto_last(place, expos, grads, scale, protos, views, totals):
    width, depth = protos.shape
    rows = views.shape[2]
    groups = len(expos)
    return pl.pallas_call(
        functools.partial(proto_last_kernel, groups),
        in_specs=[pl.BlockSpec(memory_space=pltpu.SMEM)] + [WHOLE] * (2 * groups + 4),
        out_specs=WHOLE,
        out_shape=jax.ShapeDtypeStruct((width, depth), bf16),
        scratch_shapes=[pltpu.VMEM((depth, rows), bf16), pltpu.VMEM((width, depth), f32)],
        compiler_params=params(),
        name="proto_last",
    )(place, *[in_vmem(x) for x in expos], *grads, scale, protos, views, totals)


def view_soft_kernel(block, tile, lead, views, protos, out, pair, stage, soft16):
    rows, depth = views.shape
    pair[...] = scaled_pair(views[...], 1)
    out[...] = jnp.zeros_like(out)
    chunk = stage.shape[1]

    def one(j, carry):
        here = pl.ds(pl.multiple_of(lead + j * block, block), block)
        _, _, unit = unit_of(protos[here, :])
        unit16 = unit.astype(bf16)
        twice = jnp.concatenate([unit16, unit16], axis=1)
        for c in range(rows // chunk):
            stage[c % 2] = dot(pair[c * chunk : (c + 1) * chunk, :], twice, NT)
            for start in range(0, chunk, tile):
                part = slice(c * chunk + start, c * chunk + start + tile)
                soft16[part, :] = jnp.exp2(stage[c % 2, start : start + tile, :]).astype(bf16)
        out[...] += dot(soft16[...], unit16)
        return carry

    return one


def view_soft_body(block, tile, lead, count, *refs):
    lax.fori_loop(0, count // block, view_soft_kernel(block, tile, lead, *refs), 0)


def view_soft(views, protos, lead, count):
    rows, depth = views.shape
    block = min(512, count)
    chunk = min(256, rows)
    return pl.pallas_call(
        functools.partial(view_soft_body, block, min(32, chunk), lead, count),
        in_specs=[WHOLE] * 2,
        out_specs=WHOLE,
        out_shape=jax.ShapeDtypeStruct((rows, depth), f32),
        scratch_shapes=[
            pltpu.VMEM((rows, 2 * depth), bf16),
            pltpu.VMEM((2, chunk, block), f32),
            pltpu.VMEM((rows, block), bf16),
        ],
        compiler_params=params(),
        cost_estimate=SMALL,
        name="view_soft",
    )(views, protos)


def view_grad_kernel(code, tot, total, *refs):
    softs, out = refs[:-1], refs[-1]
    soft = softs[0][...]
    for other in softs[1:]:
        soft = soft + other[...]
    soft = soft * to_column(GRAD_SCALE / tot[...])
    hard = swap_rows(code[...] * to_column(GRAD_SCALE / total[...]))
    out[...] = (soft - hard).astype(out.dtype)


def view_grad_part(code, tot, total, *softs):
    operands = [code, tot, total, *softs]
    return pl.pallas_call(
        view_grad_kernel,
        grid=(1,),
        in_specs=[full(x.shape) for x in operands],
        out_specs=full(code.shape),
        out_shape=jax.ShapeDtypeStruct(code.shape, bf16),
        compiler_params=params("arbitrary"),
        cost_estimate=SMALL,
        name="view_grad",
    )(code, tot, total, *[in_hbm(x) for x in softs])


def backward_kernel(grad_a, grad_b, pos, raw, pre, emb, hid_part, w_out, out):
    total = grad_a[...].astype(f32) + grad_b[...].astype(f32)
    n, depth = raw.shape
    place = jnp.broadcast_to(pos[...].astype(f32), (8, n)).T[:, :1].astype(jnp.int32)
    lane = lax.broadcasted_iota(jnp.int32, (n, n), 1)
    move = jnp.where(lane == place, 1.0, 0.0).astype(bf16)
    hi = total.astype(bf16)
    lo = (total - hi.astype(f32)).astype(bf16)
    moved = dot(move, jnp.concatenate([hi, lo], axis=1))
    grad = moved[:, :depth] + moved[:, depth:]
    raw_out = raw[...]
    inv = lax.rsqrt(jnp.sum(raw_out * raw_out, axis=1, keepdims=True) + norm_eps)
    inner = jnp.sum(raw_out * grad, axis=1, keepdims=True)
    d_raw = (inv * grad - raw_out * (inv * inv * inv) * inner).astype(bf16)
    g_out = dot(hid_part[...], d_raw, TN)
    d_hidden = dot(d_raw, w_out[...], NT)
    v = pre[...]
    t = jnp.tanh(GELU_K * (v + GELU_A * (v * v * v)))
    slope = 0.5 * (1.0 + t) + (0.5 * GELU_K) * v * (1.0 - t * t) * (1.0 + (3.0 * GELU_A) * (v * v))
    d_pre = (slope * d_hidden).astype(bf16)
    g_in = dot(emb[...], d_pre, TN)
    count = out.shape[0]
    tall, wide = g_in.shape[0] // count, g_in.shape[1]
    base, short = tall * (wide // 128), g_out.shape[0] // count
    for k in range(count):
        n = mirrored(k, count)
        for q in range(wide // 128):
            out[n, q * tall : (q + 1) * tall, :] = g_in[
                k * tall : (k + 1) * tall, q * 128 : (q + 1) * 128
            ]
        out[n, base : base + short, :] = g_out[k * short : (k + 1) * short]


def mirrored(k, count):
    found = 0
    while count > 1:
        found = found * 2 + k % 2
        k //= 2
        count //= 2
    return found


def backward(nb, grad_a, grad_b, pos, raw, pre, emb, hid_part, w_out):
    lines = (emb.shape[1] * pre.shape[1] + hid_part.shape[1] * raw.shape[1]) // (nb * 128)
    operands = [grad_a, grad_b, pos, raw, pre, emb, hid_part, w_out]
    return pl.pallas_call(
        backward_kernel,
        grid=(1,),
        in_specs=[full(x.shape) for x in operands],
        out_specs=full((nb, lines, 128)),
        out_shape=jax.ShapeDtypeStruct((nb, lines, 128), f32),
        compiler_params=params("arbitrary"),
        name="backward",
    )(grad_a, grad_b, pos, *[in_hbm(x) for x in operands[3:]])


def unpack_kernel(order, order_b, place, *refs):
    pieces, (g_in, g_out) = refs[:-2], refs[-2:]
    nb = len(order_b)
    npr = len(order)
    tall, wide = g_in.shape[0] // (nb * npr), g_in.shape[1]
    base, short = tall * (wide // 128), g_out.shape[0] // (nb * npr)
    half = pieces[0].shape[0]
    for n, flip in enumerate(order):
        for k, flip_b in enumerate(order_b):
            owner = (place[0] ^ flip) * nb + (place[1] ^ flip_b)
            x = pieces[n // half][n % half, k].astype(f32)
            low = pl.multiple_of(owner * tall, tall)
            for q in range(wide // 128):
                g_in[pl.ds(low, tall), q * 128 : (q + 1) * 128] = x[q * tall : (q + 1) * tall]
            low = pl.multiple_of(owner * short, short)
            g_out[pl.ds(low, short), :] = x[base : base + short]


def unpack(order, order_b, place, pieces, shape_in, shape_out):
    return pl.pallas_call(
        functools.partial(unpack_kernel, order, order_b),
        in_specs=[pl.BlockSpec(memory_space=pltpu.SMEM)] + [WHOLE] * len(pieces),
        out_specs=[WHOLE] * 2,
        out_shape=[jax.ShapeDtypeStruct(shape_in, f32), jax.ShapeDtypeStruct(shape_out, f32)],
        compiler_params=params(),
        name="unpack",
    )(place, *pieces)


def body(nb, npr, embeddings, pairing, w_in, w_out, prototypes):
    b = lax.axis_index("batch")
    p = lax.axis_index("proto")
    rows, wide = embeddings.shape
    width, depth = prototypes.shape
    hidden_n = w_in.shape[1]
    own = width // nb

    def flipped(x, axis, size, step):
        return lax.ppermute(x, axis, [(i, i ^ step) for i in range(size)])

    def exchange(x, axis, size, step, queue, results):
        other = flipped(x, axis, size, step)
        if queue:
            work, operands = queue.pop(0)
            operands, _ = lax.optimization_barrier((operands, x))
            other, found = lax.optimization_barrier((other, work(*operands)))
            results.append(found)
        return other

    def doubled(x, axis, size, queue=(), results=None):
        step = 1
        while step * 2 < size:
            x = x + exchange(x, axis, size, step, queue, results)
            step *= 2
        return [x, exchange(x, axis, size, step, queue, results)]

    pre, hid, raw, views, views_t, pos = head(embeddings, pairing, w_in, w_out)
    views_all = lax.all_gather(views_t, "batch", axis=0)
    protos_own = lax.dynamic_slice_in_dim(prototypes, b * own, own, 0)
    place = b.astype(jnp.int32).reshape(1)
    at_in = (p * (wide // npr)).astype(jnp.uint32)
    at_out = (p * (hidden_n // npr)).astype(jnp.uint32)
    views, protos_own, place, at_in, at_out = lax.optimization_barrier(
        (views, protos_own, place, at_in, at_out)
    )
    expo, col, tot = first_pass(views, prototypes)

    groups = 4
    cols = width // groups
    softs = []
    queue = [
        (functools.partial(view_soft, lead=k * cols, count=cols), (views, prototypes))
        for k in range(groups)
    ]
    scale, row = rowsum(expo, doubled(col, "batch", nb, queue, softs))
    first, second = doubled(jnp.concatenate([row, tot], axis=0), "proto", npr, queue, softs)
    both = first + second
    totals, tot = [both[:1]], both[1:]

    def slices(embeddings, hid):
        none = jnp.uint32(0)
        return (
            lax.dynamic_slice(embeddings, (none, at_in), (rows, wide // npr)),
            lax.dynamic_slice(hid, (none, at_out), (rows, hidden_n // npr)),
        )

    taken = []
    queue = [(unit_transposed, (prototypes,)), (slices, (embeddings, hid))]
    col = colsum(expo, totals)[0]
    tot_all = tot[None]
    step = 1
    while step < nb:
        other = flipped(tot_all, "batch", nb, step)
        part = exchange(col, "batch", nb, step, queue, taken)
        other, part = lax.optimization_barrier((other, part))
        tot_all = jnp.concatenate([tot_all, other], axis=0)
        step *= 2
        if step < nb:
            col = col + part
    unit_t, (emb_part, hid_part) = taken
    scale, row = rowsum(expo, [col, part])
    col = colsum(expo, doubled(row, "proto", npr))[0]

    col, views_all = lax.optimization_barrier((col, views_all))
    each = nb // groups
    owns = []
    queue = [
        (
            functools.partial(proto_first, lead=k * each, count=each),
            (place, protos_own, views_all, tot_all),
        )
        for k in range(groups)
    ]
    scale, row, code = rowsum_last(expo, doubled(col, "batch", nb, queue, owns), unit_t)
    first, second = doubled(row, "proto", npr, queue, owns)
    total = first + second
    total_all = total[None]
    grads = []
    queue = [(view_grad_part, (code, tot, total, *softs))]
    step = 1
    turn = 1
    while step < nb:
        other = exchange(total_all, "batch", nb, step, queue, grads)
        if len(grads) > 1:
            grads = [(grads[0].astype(f32) + grads[1].astype(f32)).astype(bf16)]
            other, grads[0] = lax.optimization_barrier((other, grads[0]))
        if turn * 2 < npr:
            grads = [grads[0], flipped(grads[0], "proto", npr, turn)]
            turn *= 2
        total_all = jnp.concatenate([total_all, other], axis=0)
        step *= 2

    if len(grads) > 1:
        grads = [(grads[0].astype(f32) + grads[1].astype(f32)).astype(bf16)]
    expos, parts = [x for x, _ in owns], [x for _, x in owns]
    queue = [(proto_last, (place, expos, parts, scale, protos_own, views_all, total_all))]
    found = []
    grads = [grads[0], exchange(grads[0], "proto", npr, npr // 2, queue, found)]
    grad_proto = lax.all_gather(found[0], "batch", axis=0, tiled=True)
    both = backward(nb, *grads, pos, raw, pre, emb_part, hid_part, w_out)
    step = 1
    while step < nb:
        half = both.shape[0] // 2
        bit = (b // step) % 2
        away = lax.dynamic_slice_in_dim(both, (1 - bit) * half, half, 0).astype(bf16)
        kept = lax.dynamic_slice_in_dim(both, bit * half, half, 0)
        both = kept + flipped(away, "batch", nb, step).astype(f32)
        step *= 2
    piece = both.astype(bf16)
    order_b = [0]
    while step > 1:
        step //= 2
        piece = jnp.concatenate([piece, flipped(piece, "batch", nb, step)], axis=0)
        order_b = order_b + [i ^ step for i in order_b]
    piece = piece[None]
    order = [0]
    step = npr // 2
    while step > 1:
        piece = jnp.concatenate([piece, flipped(piece, "proto", npr, step)], axis=0)
        order = order + [i ^ step for i in order]
        step //= 2
    pieces = [piece, flipped(piece, "proto", npr, 1)]
    order = order + [i ^ 1 for i in order]
    places = jnp.stack([p, b]).astype(jnp.int32)
    grad_in, grad_out = unpack(
        order, order_b, places, pieces, (wide, hidden_n), (hidden_n, depth)
    )
    return (grad_in, grad_out, grad_proto.astype(f32))


def solution(mesh):
    return jax.shard_map(
        functools.partial(body, mesh.shape["batch"], mesh.shape["proto"]),
        mesh=mesh,
        in_specs=(P("batch", None), P("batch"), P(), P(), P("proto", None)),
        out_specs=(P(), P(), P("proto", None)),
        check_vma=False,
    )
```

```python
import functools
import math

import jax
import jax.numpy as jnp
from jax import lax
from jax.experimental import pallas as pl
from jax.experimental.pallas import tpu as pltpu
from jax.sharding import PartitionSpec as P

ITERS = 3
norm_eps = 1e-06
code_temp = 0.05
pred_temp = 0.1
loss_scale = 64.0
GRAD_SCALE = loss_scale / pred_temp
EXP2_SCALE = math.log2(math.e) / pred_temp
GELU_K = math.sqrt(2.0 / math.pi)
GELU_A = 0.044715

f32 = jnp.float32
bf16 = jnp.bfloat16
NN = (((1,), (0,)), ((), ()))
NT = (((1,), (1,)), ((), ()))
TN = (((0,), (0,)), ((), ()))
VMEM_LIMIT = 12 * 1024 * 1024


def dot(a, b, dims=NN):
    return lax.dot_general(a, b, dims, preferred_element_type=f32)


SMALL = pl.CostEstimate(flops=1000, bytes_accessed=1000, transcendentals=0)


def params(*semantics, limit=VMEM_LIMIT):
    return pltpu.CompilerParams(dimension_semantics=semantics or None, vmem_limit_bytes=limit)


def to_column(vec):
    n = vec.shape[1]
    return jnp.broadcast_to(vec, (8, n)).T[:, :1]


def swap_lanes(x):
    half = x.shape[1] // 2
    return jnp.concatenate([x[:, half:], x[:, :half]], axis=1)


def swap_rows(x):
    half = x.shape[0] // 2
    return jnp.concatenate([x[half:], x[:half]], axis=0)


def in_vmem(x):
    return pltpu.with_memory_space_constraint(x, pltpu.VMEM)


def in_hbm(x):
    return pltpu.with_memory_space_constraint(x, pltpu.HBM)


def full(shape):
    return pl.BlockSpec(shape, lambda *_: (0,) * len(shape))


def head_kernel(emb, pairing, w_in, w_out, pre, hid, raw, views, views_t, pos, scratch):
    step = pl.program_id(0)
    rows = emb.shape[0]
    pre_act = dot(emb[...], w_in[...])
    pre[...] = pre_act
    t = jnp.tanh(GELU_K * (pre_act + GELU_A * (pre_act * pre_act * pre_act)))
    hidden = (0.5 * pre_act * (1.0 + t)).astype(bf16)
    hid[...] = hidden
    raw_out = dot(hidden, w_out[...])
    raw[...] = raw_out
    inv = lax.rsqrt(jnp.sum(raw_out * raw_out, axis=1, keepdims=True) + norm_eps)
    scratch[pl.ds(pl.multiple_of(step * rows, rows), rows), :] = (raw_out * inv).astype(bf16)

    @pl.when(step == pl.num_programs(0) - 1)
    def _():
        mate = pairing[...]
        n = mate.shape[1]
        lane = lax.broadcasted_iota(jnp.int32, (1, n), 1)
        first = lane < mate
        low = jnp.minimum(lane, mate)
        sub = lax.broadcasted_iota(jnp.int32, (n, n), 0)
        before = jnp.where(sub < low, 1.0, 0.0).astype(bf16)
        first8 = jnp.broadcast_to(jnp.where(first, 1.0, 0.0), (8, n)).astype(bf16)
        rank = dot(first8, before)[:1].astype(jnp.int32)
        place = jnp.where(first, rank, rank + n // 2)
        pos[...] = place
        move = jnp.where(sub == place, 1.0, 0.0).astype(bf16)
        ordered = dot(move, scratch[...])
        views[...] = ordered.astype(bf16)
        views_t[...] = ordered.T.astype(bf16)


def head(embeddings, pairing, w_in, w_out):
    rows, wide = embeddings.shape
    hidden = w_in.shape[1]
    depth = w_out.shape[1]
    steps = 4
    block = rows // steps
    return pl.pallas_call(
        head_kernel,
        grid=(steps,),
        in_specs=[
            pl.BlockSpec((block, wide), lambda i: (i, 0)),
            full((1, rows)),
            full((wide, hidden)),
            full((hidden, depth)),
        ],
        out_specs=[
            pl.BlockSpec((block, hidden), lambda i: (i, 0)),
            pl.BlockSpec((block, hidden), lambda i: (i, 0)),
            pl.BlockSpec((block, depth), lambda i: (i, 0)),
            full((rows, depth)),
            full((depth, rows)),
            full((1, rows)),
        ],
        out_shape=[
            pltpu.HBM((rows, hidden), f32),
            pltpu.HBM((rows, hidden), bf16),
            pltpu.HBM((rows, depth), f32),
            jax.ShapeDtypeStruct((rows, depth), bf16),
            jax.ShapeDtypeStruct((depth, rows), bf16),
            jax.ShapeDtypeStruct((1, rows), jnp.int32),
        ],
        scratch_shapes=[pltpu.VMEM((rows, depth), bf16)],
        compiler_params=params("arbitrary"),
        name="head",
    )(in_hbm(embeddings), in_hbm(pairing.reshape(1, rows)), in_hbm(w_in), in_hbm(w_out))


def unit_of(protos):
    proto_f = protos.astype(f32)
    inv = lax.rsqrt(jnp.sum(proto_f * proto_f, axis=1, keepdims=True) + norm_eps)
    return proto_f, inv, proto_f * inv


WHOLE = pl.BlockSpec(memory_space=pltpu.VMEM)


def scaled_pair(x, axis):
    wide = x.astype(f32) * EXP2_SCALE
    hi = wide.astype(bf16)
    lo = (wide - hi.astype(f32)).astype(bf16)
    return jnp.concatenate([hi, lo], axis=axis)


def first_kernel(block, chunk, tile, views, protos, expo, col, tot, pair, stage, tot_acc):
    rows, depth = views.shape
    width = protos.shape[0]
    tot_acc[...] = jnp.zeros_like(tot_acc)
    pair[...] = scaled_pair(views[...], 1)

    def one(j, carry):
        here = pl.ds(pl.multiple_of(j * block, block), block)
        _, _, unit = unit_of(protos[here, :])
        unit16 = unit.astype(bf16)
        twice = jnp.concatenate([unit16, unit16], axis=1)
        running = jnp.zeros((8, block), f32)
        for c in range(rows // chunk):
            stage[c % 2] = dot(pair[c * chunk : (c + 1) * chunk, :], twice, NT)
            for start in range(0, chunk, tile):
                part = slice(c * chunk + start, c * chunk + start + tile)
                soft = jnp.exp2(stage[c % 2, start : start + tile, :])
                hard = soft * soft
                expo[part, here] = hard.astype(bf16)
                lanes = soft[:, :128]
                for k in range(1, block // 128):
                    lanes = lanes + soft[:, k * 128 : (k + 1) * 128]
                tot_acc[part, :] += lanes
                for k in range(0, tile, 8):
                    running = running + hard[k : k + 8]
        col[:, here] = jnp.sum(running, axis=0, keepdims=True)
        return carry

    lax.fori_loop(0, width // block, one, 0)
    tot[...] = jnp.sum(tot_acc[...].T, axis=0, keepdims=True)


def first_pass(views, protos):
    rows, depth = views.shape
    width = protos.shape[0]
    block = min(512, width)
    chunk = min(256, rows)
    tile = min(32, chunk)
    return pl.pallas_call(
        functools.partial(first_kernel, block, chunk, tile),
        in_specs=[WHOLE] * 2,
        out_specs=[WHOLE] * 3,
        out_shape=[
            pltpu.VMEM((rows, width), bf16),
            jax.ShapeDtypeStruct((1, width), f32),
            jax.ShapeDtypeStruct((1, rows), f32),
        ],
        scratch_shapes=[
            pltpu.VMEM((rows, 2 * depth), bf16),
            pltpu.VMEM((2, chunk, block), f32),
            pltpu.VMEM((rows, 128), f32),
        ],
        compiler_params=params(),
        cost_estimate=SMALL,
        name="first_pass",
    )(views, protos)


def sum_parts(parts, width):
    if len(parts[0].shape) == 3:
        parts = [parts[0].at[k] for k in range(parts[0].shape[0])]
    total = parts[0][:, :width]
    for other in parts[1:]:
        total = total + other[:, :width]
    return total


def add_fours(terms):
    total = None
    for k in range(0, len(terms), 4):
        four = terms[k : k + 4]
        while len(four) > 1:
            four = [x + y for x, y in zip(four[::2], four[1::2])]
        part = four[0].astype(f32)
        total = part if total is None else total + part
    return total


def rowsum_tile(expo, here, spread, tall, width):
    terms = []
    total = None
    for k in range(width // 128):
        lanes = slice(k * 128, (k + 1) * 128)
        weight = jnp.concatenate([spread[:, lanes]] * (tall // 16), axis=0)
        terms.append(expo[here, lanes] * weight)
        if len(terms) == 4 or k == width // 128 - 1:
            part = add_fours(terms)
            total = part if total is None else total + part
            terms = []
    return total


def rowsum_kernel(count, expo, *refs):
    parts = refs[:count]
    scale, out, spread, acc = refs[count:]
    rows, width = expo.shape
    inverse = 1.0 / sum_parts(parts, width)
    scale[...] = inverse
    spread[...] = jnp.broadcast_to(inverse, spread.shape).astype(bf16)
    tall = 64

    def one(i, carry):
        here = pl.ds(pl.multiple_of(i * tall, tall), tall)
        acc[here, :] = rowsum_tile(expo, here, spread, tall, width)
        return carry

    lax.fori_loop(0, rows // tall, one, 0)
    out[...] = jnp.sum(acc[...].T, axis=0, keepdims=True)


def rowsum(expo, parts):
    rows, width = expo.shape
    return pl.pallas_call(
        functools.partial(rowsum_kernel, len(parts)),
        in_specs=[WHOLE] * (1 + len(parts)),
        out_specs=[WHOLE] * 2,
        out_shape=[
            jax.ShapeDtypeStruct((1, width), f32),
            jax.ShapeDtypeStruct((1, rows), f32),
        ],
        scratch_shapes=[pltpu.VMEM((16, width), bf16), pltpu.VMEM((rows, 128), f32)],
        compiler_params=params(),
        cost_estimate=SMALL,
        name="rowsum",
    )(in_vmem(expo), *parts)


def split_rows(vec):
    hi = vec.astype(bf16).astype(f32)
    n = vec.shape[1]
    row = lax.broadcasted_iota(jnp.int32, (8, n), 0)
    hi8 = jnp.broadcast_to(hi, (8, n))
    lo8 = jnp.broadcast_to(vec - hi, (8, n))
    return jnp.where(row == 0, hi8, jnp.where(row == 1, lo8, 0.0))


def rowsum_last_kernel(pieces, count, *refs):
    expos = refs[:pieces]
    parts = refs[pieces : pieces + count]
    unit_t, scale, out, code, acc = refs[pieces + count :]
    step = pl.program_id(0)
    depth, block = unit_t.shape
    deep = expos[0].shape[1]
    inverse = 1.0 / sum_parts(parts, block)
    scale[...] = inverse

    @pl.when(step == 0)
    def _():
        acc[...] = jnp.zeros_like(acc)

    for k in range(pieces):
        here = slice(k * deep, (k + 1) * deep)
        scaled = unit_t[:, here].astype(f32) * inverse[:, here]
        pad = jnp.zeros((depth - 8, deep), f32)
        weights = jnp.concatenate([scaled, split_rows(inverse[:, here]), pad], axis=0)
        acc[...] += dot(expos[k][...], weights.astype(bf16), NT)

    @pl.when(step == pl.num_programs(0) - 1)
    def _():
        sums = acc[:, depth:].T
        out[...] = sums[0:1] + sums[1:2]
        code[...] = acc[:, :depth]


def rowsum_last(expo, parts, unit_t):
    rows, width = expo.shape
    depth = unit_t.shape[0]
    block = min(2048, width)
    pieces = 4
    deep = block // pieces
    vec = pl.BlockSpec((1, block), lambda j: (0, j))
    return pl.pallas_call(
        functools.partial(rowsum_last_kernel, pieces, len(parts)),
        grid=(width // block,),
        in_specs=[
            pl.BlockSpec((rows, deep), lambda j, k=k: (0, j * pieces + k)) for k in range(pieces)
        ]
        + [vec] * len(parts)
        + [pl.BlockSpec((depth, block), lambda j: (0, j))],
        out_specs=[vec, full((1, rows)), full((rows, depth))],
        out_shape=[
            jax.ShapeDtypeStruct((1, width), f32),
            jax.ShapeDtypeStruct((1, rows), f32),
            jax.ShapeDtypeStruct((rows, depth), f32),
        ],
        scratch_shapes=[pltpu.VMEM((rows, 2 * depth), f32)],
        compiler_params=params("arbitrary", limit=VMEM_LIMIT + 4 * 1024 * 1024),
        cost_estimate=SMALL,
        name="rowsum_last",
    )(*[in_hbm(expo)] * pieces, *parts, in_hbm(unit_t))


def unit_t_kernel(block, lead, protos, *refs):
    out = refs[-1]

    def one(j, carry):
        here = pl.ds(pl.multiple_of(lead + j * block, block), block)
        _, _, unit = unit_of(protos[here, :])
        out[:, here] = unit.astype(bf16).astype(f32).T.astype(bf16)
        return carry

    lax.fori_loop(0, protos.shape[0] // 2 // block, one, 0)


def unit_transposed(protos, *before):
    width, depth = protos.shape
    lead = width // 2 if before else 0
    return pl.pallas_call(
        functools.partial(unit_t_kernel, min(512, width // 2), lead),
        in_specs=[WHOLE] * (1 + len(before)),
        out_specs=WHOLE,
        out_shape=jax.ShapeDtypeStruct((depth, width), bf16),
        input_output_aliases={1: 0} if before else {},
        compiler_params=params(),
        cost_estimate=SMALL,
        name="unit_t",
    )(protos, *before)


def colsum_kernel(count, expo, *refs):
    parts = refs[:count]
    rest = refs[count:]
    out, spread = rest[-2:]
    rows, width = expo.shape
    inverse = 1.0 / sum_parts(parts, rows)
    spread[...] = jnp.broadcast_to(inverse, (128, rows)).T.astype(bf16)
    block = min(512, width)

    def one(j, carry):
        here = pl.ds(pl.multiple_of(j * block, block), block)
        running = jnp.zeros((16, block), f32)
        for i in range(0, rows // 16, 4):
            terms = []
            for k in range(i, min(i + 4, rows // 16)):
                part = slice(k * 16, (k + 1) * 16)
                weight = jnp.concatenate([spread[part, :]] * (block // 128), axis=1)
                terms.append(expo[part, here] * weight)
            running = running + add_fours(terms)
        total = jnp.sum(running, axis=0, keepdims=True)
        for k in range(out.shape[0]):
            out[k, :, here] = total
        return carry

    lax.fori_loop(0, width // block, one, 0)
    if len(rest) > 2:
        for k in range(out.shape[0]):
            out[k, :, width:] = rest[0][...]


def colsum(expo, parts, copies=1, behind=()):
    rows, width = expo.shape
    long = width + sum(x.shape[1] for x in behind)
    return pl.pallas_call(
        functools.partial(colsum_kernel, len(parts)),
        in_specs=[WHOLE] * (1 + len(parts) + len(behind)),
        out_specs=WHOLE,
        out_shape=jax.ShapeDtypeStruct((copies, 1, long), f32),
        scratch_shapes=[pltpu.VMEM((rows, 128), bf16)],
        compiler_params=params(),
        cost_estimate=SMALL,
        name="colsum",
    )(in_vmem(expo), *parts, *behind)


def proto_first_kernel(chunk, tile, lead, place, protos, views, totals, expo, grad, *scratch):
    weights, twice, pair, stage, soft16, acc = scratch
    count = expo.shape[1] // views.shape[2]
    _, depth, rows = views.shape
    width = protos.shape[0]
    _, _, unit = unit_of(protos[...])
    pair[...] = scaled_pair(unit.astype(bf16), 1)
    for n in range(count):
        k = lead + n
        weights[...] = (views[k].astype(f32) * (GRAD_SCALE / totals[place[0] ^ k])).astype(bf16)
        twice[:depth, :] = views[k]
        twice[depth:, :] = views[k]
        for c in range(width // chunk):
            stage[c % 2] = dot(pair[c * chunk : (c + 1) * chunk, :], twice[...])
            for start in range(0, chunk, tile):
                part = slice(c * chunk + start, c * chunk + start + tile)
                soft = jnp.exp2(stage[c % 2, start : start + tile, :])
                soft16[part, :] = soft.astype(bf16)
                expo[part, n * rows : (n + 1) * rows] = (soft * soft).astype(bf16)
        found = dot(soft16[...], weights[...], NT)
        if n == 0:
            acc[...] = found
        else:
            acc[...] += found
    grad[...] = acc[...]


def proto_first(place, protos, views, totals, lead, count):
    width, depth = protos.shape
    rows = views.shape[2]
    chunk = min(256, width)
    tile = min(16, chunk)
    return pl.pallas_call(
        functools.partial(proto_first_kernel, chunk, tile, lead),
        in_specs=[pl.BlockSpec(memory_space=pltpu.SMEM)] + [WHOLE] * 3,
        out_specs=[WHOLE] * 2,
        out_shape=[
            pltpu.VMEM((width, count * rows), bf16),
            jax.ShapeDtypeStruct((width, depth), f32),
        ],
        scratch_shapes=[
            pltpu.VMEM((depth, rows), bf16),
            pltpu.VMEM((2 * depth, rows), bf16),
            pltpu.VMEM((width, 2 * depth), bf16),
            pltpu.VMEM((2, chunk, rows), f32),
            pltpu.VMEM((width, rows), bf16),
            pltpu.VMEM((width, depth), f32),
        ],
        compiler_params=params(),
        cost_estimate=SMALL,
        name="proto_first",
    )(place, protos, views, totals)


def proto_last_kernel(groups, place, *refs):
    expos, grads = refs[:groups], refs[groups : 2 * groups]
    scale, protos, views, totals, out, weights, acc = refs[2 * groups :]
    count, depth, rows = views.shape
    each = count // groups
    for k in range(count):
        mates = swap_lanes(views[k])
        weights[...] = (mates.astype(f32) * (GRAD_SCALE / totals[place[0] ^ k])).astype(bf16)
        found = dot(expos[k // each][:, (k % each) * rows : (k % each + 1) * rows], weights[...], NT)
        if k == 0:
            acc[...] = found
        else:
            acc[...] += found
    width = protos.shape[0]
    there = pl.ds(pl.multiple_of(place[0] * width, width), width)
    unit_grad = grads[0][...]
    for other in grads[1:]:
        unit_grad = unit_grad + other[...]
    unit_grad = unit_grad - to_column(scale[:, there]) * acc[...]
    proto_f, inv, _ = unit_of(protos[...])
    inner = jnp.sum(proto_f * unit_grad, axis=1, keepdims=True)
    out[...] = (inv * unit_grad - proto_f * (inv * inv * inv) * inner).astype(bf16)


def proto_last(place, expos, grads, scale, protos, views, totals):
    width, depth = protos.shape
    rows = views.shape[2]
    groups = len(expos)
    return pl.pallas_call(
        functools.partial(proto_last_kernel, groups),
        in_specs=[pl.BlockSpec(memory_space=pltpu.SMEM)] + [WHOLE] * (2 * groups + 4),
        out_specs=WHOLE,
        out_shape=jax.ShapeDtypeStruct((width, depth), bf16),
        scratch_shapes=[pltpu.VMEM((depth, rows), bf16), pltpu.VMEM((width, depth), f32)],
        compiler_params=params(),
        name="proto_last",
    )(place, *[in_vmem(x) for x in expos], *grads, scale, protos, views, totals)


def view_soft_kernel(block, tile, lead, views, protos, out, pair, stage, soft16):
    rows, depth = views.shape
    pair[...] = scaled_pair(views[...], 1)
    out[...] = jnp.zeros_like(out)
    chunk = stage.shape[1]

    def one(j, carry):
        here = pl.ds(pl.multiple_of(lead + j * block, block), block)
        _, _, unit = unit_of(protos[here, :])
        unit16 = unit.astype(bf16)
        twice = jnp.concatenate([unit16, unit16], axis=1)
        for c in range(rows // chunk):
            stage[c % 2] = dot(pair[c * chunk : (c + 1) * chunk, :], twice, NT)
            for start in range(0, chunk, tile):
                part = slice(c * chunk + start, c * chunk + start + tile)
                soft16[part, :] = jnp.exp2(stage[c % 2, start : start + tile, :]).astype(bf16)
        out[...] += dot(soft16[...], unit16)
        return carry

    return one


def view_soft_body(block, tile, lead, count, *refs):
    lax.fori_loop(0, count // block, view_soft_kernel(block, tile, lead, *refs), 0)


def view_soft(views, protos, lead, count):
    rows, depth = views.shape
    block = min(512, count)
    chunk = min(256, rows)
    return pl.pallas_call(
        functools.partial(view_soft_body, block, min(32, chunk), lead, count),
        in_specs=[WHOLE] * 2,
        out_specs=WHOLE,
        out_shape=jax.ShapeDtypeStruct((rows, depth), f32),
        scratch_shapes=[
            pltpu.VMEM((rows, 2 * depth), bf16),
            pltpu.VMEM((2, chunk, block), f32),
            pltpu.VMEM((rows, block), bf16),
        ],
        compiler_params=params(),
        cost_estimate=SMALL,
        name="view_soft",
    )(views, protos)


def view_grad_kernel(code, tot, total, *refs):
    softs, out = refs[:-1], refs[-1]
    soft = softs[0][...]
    for other in softs[1:]:
        soft = soft + other[...]
    soft = soft * to_column(GRAD_SCALE / tot[...])
    hard = swap_rows(code[...] * to_column(GRAD_SCALE / total[...]))
    out[...] = (soft - hard).astype(out.dtype)


def view_grad_part(code, tot, total, *softs):
    operands = [code, tot, total, *softs]
    return pl.pallas_call(
        view_grad_kernel,
        grid=(1,),
        in_specs=[full(x.shape) for x in operands],
        out_specs=full(code.shape),
        out_shape=jax.ShapeDtypeStruct(code.shape, bf16),
        compiler_params=params("arbitrary"),
        cost_estimate=SMALL,
        name="view_grad",
    )(code, tot, total, *[in_hbm(x) for x in softs])


def backward_kernel(share, turn, grad_a, grad_b, pos, raw, pre, emb, hid, w_out, out, g_all):
    total = grad_a[...].astype(f32) + grad_b[...].astype(f32)
    n, depth = raw.shape
    place = jnp.broadcast_to(pos[...].astype(f32), (8, n)).T[:, :1].astype(jnp.int32)
    lane = lax.broadcasted_iota(jnp.int32, (n, n), 1)
    move = jnp.where(lane == place, 1.0, 0.0).astype(bf16)
    hi = total.astype(bf16)
    lo = (total - hi.astype(f32)).astype(bf16)
    moved = dot(move, jnp.concatenate([hi, lo], axis=1))
    grad = moved[:, :depth] + moved[:, depth:]
    raw_out = raw[...]
    inv = lax.rsqrt(jnp.sum(raw_out * raw_out, axis=1, keepdims=True) + norm_eps)
    inner = jnp.sum(raw_out * grad, axis=1, keepdims=True)
    d_raw = (inv * grad - raw_out * (inv * inv * inv) * inner).astype(bf16)
    g_all[...] = dot(hid[...], d_raw, TN)
    d_hidden = dot(d_raw, w_out[...], NT)
    v = pre[...]
    t = jnp.tanh(GELU_K * (v + GELU_A * (v * v * v)))
    slope = 0.5 * (1.0 + t) + (0.5 * GELU_K) * v * (1.0 - t * t) * (1.0 + (3.0 * GELU_A) * (v * v))
    d_pre = (slope * d_hidden).astype(bf16)
    g_in = dot(emb[...], d_pre, TN)
    count = out.shape[0]
    tall, wide = g_in.shape[0] // count, g_in.shape[1]
    base, short = tall * (wide // 128), share // count
    for k in range(count):
        n = mirrored(k, count)
        for q in range(wide // 128):
            out[n, q * tall : (q + 1) * tall, :] = g_in[
                k * tall : (k + 1) * tall, q * 128 : (q + 1) * 128
            ]
        low = pl.multiple_of(turn[0] * share + k * short, short)
        out[n, base : base + short, :] = g_all[pl.ds(low, short), :]


def mirrored(k, count):
    found = 0
    while count > 1:
        found = found * 2 + k % 2
        k //= 2
        count //= 2
    return found


def backward(nb, npr, turn, grad_a, grad_b, pos, raw, pre, emb, hid, w_out):
    rows, wide = emb.shape
    hidden, depth = w_out.shape
    part = wide // npr
    share = hidden // npr
    lines = (part * hidden + share * depth) // (nb * 128)
    operands = [grad_a, grad_b, pos, raw, pre, emb, hid, w_out]
    specs = [full(x.shape) for x in operands]
    specs[5] = pl.BlockSpec((rows, part), lambda i, turn: (0, turn[0]))
    return pl.pallas_call(
        functools.partial(backward_kernel, share),
        grid_spec=pltpu.PrefetchScalarGridSpec(
            num_scalar_prefetch=1,
            grid=(1,),
            in_specs=specs,
            out_specs=full((nb, lines, 128)),
            scratch_shapes=[pltpu.VMEM((hidden, depth), f32)],
        ),
        out_shape=jax.ShapeDtypeStruct((nb, lines, 128), f32),
        compiler_params=params("arbitrary"),
        name="backward",
    )(turn, grad_a, grad_b, pos, *[in_hbm(x) for x in operands[3:]])


def unpack_kernel(order, order_b, place, *refs):
    pieces, (g_in, g_out) = refs[:-2], refs[-2:]
    nb = len(order_b)
    npr = len(order)
    tall, wide = g_in.shape[0] // (nb * npr), g_in.shape[1]
    base, short = tall * (wide // 128), g_out.shape[0] // (nb * npr)
    half = pieces[0].shape[0]
    for n, flip in enumerate(order):
        for k, flip_b in enumerate(order_b):
            owner = (place[0] ^ flip) * nb + (place[1] ^ flip_b)
            x = pieces[n // half][n % half, k].astype(f32)
            low = pl.multiple_of(owner * tall, tall)
            for q in range(wide // 128):
                g_in[pl.ds(low, tall), q * 128 : (q + 1) * 128] = x[q * tall : (q + 1) * tall]
            low = pl.multiple_of(owner * short, short)
            g_out[pl.ds(low, short), :] = x[base : base + short]


def unpack(order, order_b, place, pieces, shape_in, shape_out):
    return pl.pallas_call(
        functools.partial(unpack_kernel, order, order_b),
        in_specs=[pl.BlockSpec(memory_space=pltpu.SMEM)] + [WHOLE] * len(pieces),
        out_specs=[WHOLE] * 2,
        out_shape=[jax.ShapeDtypeStruct(shape_in, f32), jax.ShapeDtypeStruct(shape_out, f32)],
        compiler_params=params(),
        name="unpack",
    )(place, *pieces)


def stages(size):
    found, step = [[1]], 2
    while step < size:
        if step * 2 < size:
            found.append([step, step * 2, step * 3])
            step *= 4
        else:
            found.append([step])
            step *= 2
    return found


def body(nb, npr, embeddings, pairing, w_in, w_out, prototypes):
    b = lax.axis_index("batch")
    p = lax.axis_index("proto")
    rows, wide = embeddings.shape
    width, depth = prototypes.shape
    hidden_n = w_in.shape[1]
    own = width // nb

    def flipped(x, axis, size, step):
        return lax.ppermute(x, axis, [(i, i ^ step) for i in range(size)])

    def exchange(x, axis, size, step, queue, results):
        other = flipped(x, axis, size, step)
        if queue and (axis == "batch" or step > 1):
            work, operands = queue.pop(0)
            operands, _ = lax.optimization_barrier((operands, x))
            other, found = lax.optimization_barrier((other, work(*operands)))
            results.append(found)
        return other

    def doubled(x, axis, size, queue=(), results=None):
        step = 1
        while step * 2 < size:
            x = x + exchange(x, axis, size, step, queue, results)
            step *= 2
        return [x, exchange(x, axis, size, step, queue, results)]

    pre, hid, raw, views, views_t, pos = head(embeddings, pairing, w_in, w_out)
    views_all = lax.all_gather(views_t, "batch", axis=0)
    protos_own = lax.dynamic_slice_in_dim(prototypes, b * own, own, 0)
    place = b.astype(jnp.int32).reshape(1)
    turn_p = p.astype(jnp.int32).reshape(1)
    views, protos_own, place, turn_p = lax.optimization_barrier(
        (views, protos_own, place, turn_p)
    )
    expo, col, tot = first_pass(views, prototypes)

    groups = 4
    cols = width // groups
    softs = []
    queue = [
        (functools.partial(view_soft, lead=k * cols, count=cols), (views, prototypes))
        for k in range(groups)
    ]
    scale, row = rowsum(expo, doubled(col, "batch", nb, queue, softs))
    first, second = doubled(jnp.concatenate([row, tot], axis=0), "proto", npr, queue, softs)
    both = first + second
    totals, tot = [both[:1]], both[1:]

    def unit_half(protos):
        return unit_transposed(protos, *taken)

    taken = []
    queue = [(unit_half, (prototypes,))] * 2
    col = colsum(expo, totals)[0]
    tot_all = tot[None]
    step = 1
    while step < nb:
        other = flipped(tot_all, "batch", nb, step)
        part = exchange(col, "batch", nb, step, queue, taken)
        other, part = lax.optimization_barrier((other, part))
        tot_all = jnp.concatenate([tot_all, other], axis=0)
        step *= 2
        if step < nb:
            col = col + part
    unit_t = taken[-1]
    scale, row = rowsum(expo, [col, part])
    col = colsum(expo, doubled(row, "proto", npr))[0]

    col, views_all = lax.optimization_barrier((col, views_all))
    each = nb // groups
    owns = []
    queue = [
        (
            functools.partial(proto_first, lead=k * each, count=each),
            (place, protos_own, views_all, tot_all),
        )
        for k in range(groups)
    ]
    scale, row, code = rowsum_last(expo, doubled(col, "batch", nb, queue, owns), unit_t)
    first, second = doubled(row, "proto", npr, queue, owns)
    total = first + second
    total_all = total[None]
    grads = []
    queue = [(view_grad_part, (code, tot, total, *softs))]
    turn = 1
    for steps in stages(nb):
        others = [exchange(total_all, "batch", nb, step, queue, grads) for step in steps]
        if len(grads) > 1:
            grads = [(grads[0].astype(f32) + grads[1].astype(f32)).astype(bf16)]
            others[0], grads[0] = lax.optimization_barrier((others[0], grads[0]))
        if turn * 2 < npr:
            grads = [grads[0], flipped(grads[0], "proto", npr, turn)]
            turn *= 2
        total_all = jnp.concatenate([total_all, *others], axis=0)

    while turn * 2 < npr:
        if len(grads) > 1:
            grads = [(grads[0].astype(f32) + grads[1].astype(f32)).astype(bf16)]
        grads = [grads[0], flipped(grads[0], "proto", npr, turn)]
        turn *= 2
    if len(grads) > 1:
        grads = [(grads[0].astype(f32) + grads[1].astype(f32)).astype(bf16)]
    expos, parts = [x for x, _ in owns], [x for _, x in owns]
    queue = [(proto_last, (place, expos, parts, scale, protos_own, views_all, total_all))]
    found = []
    grads = [grads[0], exchange(grads[0], "proto", npr, npr // 2, queue, found)]
    grad_proto = lax.all_gather(found[0], "batch", axis=0, tiled=True)
    both = backward(nb, npr, turn_p, *grads, pos, raw, pre, embeddings, hid, w_out)
    for steps in stages(nb):
        count = len(steps) + 1
        share = both.shape[0] // count
        mine = (b // steps[0]) % 2
        if count == 4:
            mine = mine * 2 + (b // steps[1]) % 2
        kept = lax.dynamic_slice_in_dim(both, mine * share, share, 0)
        for flip, step in zip([1] if count == 2 else [2, 1, 3], steps):
            away = lax.dynamic_slice_in_dim(both, (mine ^ flip) * share, share, 0)
            kept = kept + flipped(away.astype(bf16), "batch", nb, step).astype(f32)
        both = kept
    piece = both.astype(bf16)
    order_b = [0]
    for steps in reversed(stages(nb)):
        piece = jnp.concatenate(
            [piece, *[flipped(piece, "batch", nb, step) for step in steps]], axis=0
        )
        order_b = order_b + [i ^ step for step in steps for i in order_b]
    piece = piece[None]
    order = [0]
    step = npr // 2
    while step > 1:
        piece = jnp.concatenate([piece, flipped(piece, "proto", npr, step)], axis=0)
        order = order + [i ^ step for i in order]
        step //= 2
    pieces = [piece, flipped(piece, "proto", npr, 1)]
    order = order + [i ^ 1 for i in order]
    places = jnp.stack([p, b]).astype(jnp.int32)
    grad_in, grad_out = unpack(
        order, order_b, places, pieces, (wide, hidden_n), (hidden_n, depth)
    )
    return (grad_in, grad_out, grad_proto.astype(f32))


def solution(mesh):
    return jax.shard_map(
        functools.partial(body, mesh.shape["batch"], mesh.shape["proto"]),
        mesh=mesh,
        in_specs=(P("batch", None), P("batch"), P(), P(), P("proto", None)),
        out_specs=(P(), P(), P("proto", None)),
        check_vma=False,
    )
```

```python
import functools
import math

import jax
import jax.numpy as jnp
from jax import lax
from jax.experimental import pallas as pl
from jax.experimental.pallas import tpu as pltpu
from jax.sharding import PartitionSpec as P

ITERS = 3
norm_eps = 1e-06
code_temp = 0.05
pred_temp = 0.1
loss_scale = 64.0
GRAD_SCALE = loss_scale / pred_temp
EXP2_SCALE = math.log2(math.e) / pred_temp
GELU_K = math.sqrt(2.0 / math.pi)
GELU_A = 0.044715

f32 = jnp.float32
bf16 = jnp.bfloat16
NN = (((1,), (0,)), ((), ()))
NT = (((1,), (1,)), ((), ()))
TN = (((0,), (0,)), ((), ()))
VMEM_LIMIT = 12 * 1024 * 1024


def dot(a, b, dims=NN):
    return lax.dot_general(a, b, dims, preferred_element_type=f32)


SMALL = pl.CostEstimate(flops=1000, bytes_accessed=1000, transcendentals=0)


def params(*semantics, limit=VMEM_LIMIT):
    return pltpu.CompilerParams(dimension_semantics=semantics or None, vmem_limit_bytes=limit)


def to_column(vec):
    n = vec.shape[1]
    return jnp.broadcast_to(vec, (8, n)).T[:, :1]


def swap_lanes(x):
    half = x.shape[1] // 2
    return jnp.concatenate([x[:, half:], x[:, :half]], axis=1)


def swap_rows(x):
    half = x.shape[0] // 2
    return jnp.concatenate([x[half:], x[:half]], axis=0)


def in_vmem(x):
    return pltpu.with_memory_space_constraint(x, pltpu.VMEM)


def in_hbm(x):
    return pltpu.with_memory_space_constraint(x, pltpu.HBM)


def full(shape):
    return pl.BlockSpec(shape, lambda *_: (0,) * len(shape))


def head_kernel(emb, pairing, w_in, w_out, pre, hid, raw, views, views_t, pos, scratch):
    step = pl.program_id(0)
    rows = emb.shape[0]
    pre_act = dot(emb[...], w_in[...])
    pre[...] = pre_act
    t = jnp.tanh(GELU_K * (pre_act + GELU_A * (pre_act * pre_act * pre_act)))
    hidden = (0.5 * pre_act * (1.0 + t)).astype(bf16)
    hid[...] = hidden
    raw_out = dot(hidden, w_out[...])
    raw[...] = raw_out
    inv = lax.rsqrt(jnp.sum(raw_out * raw_out, axis=1, keepdims=True) + norm_eps)
    scratch[pl.ds(pl.multiple_of(step * rows, rows), rows), :] = (raw_out * inv).astype(bf16)

    @pl.when(step == pl.num_programs(0) - 1)
    def _():
        mate = pairing[...]
        n = mate.shape[1]
        lane = lax.broadcasted_iota(jnp.int32, (1, n), 1)
        first = lane < mate
        low = jnp.minimum(lane, mate)
        sub = lax.broadcasted_iota(jnp.int32, (n, n), 0)
        before = jnp.where(sub < low, 1.0, 0.0).astype(bf16)
        first8 = jnp.broadcast_to(jnp.where(first, 1.0, 0.0), (8, n)).astype(bf16)
        rank = dot(first8, before)[:1].astype(jnp.int32)
        place = jnp.where(first, rank, rank + n // 2)
        pos[...] = place
        move = jnp.where(sub == place, 1.0, 0.0).astype(bf16)
        ordered = dot(move, scratch[...])
        views[...] = ordered.astype(bf16)
        views_t[...] = ordered.T.astype(bf16)


def head(embeddings, pairing, w_in, w_out):
    rows, wide = embeddings.shape
    hidden = w_in.shape[1]
    depth = w_out.shape[1]
    steps = 4
    block = rows // steps
    return pl.pallas_call(
        head_kernel,
        grid=(steps,),
        in_specs=[
            pl.BlockSpec((block, wide), lambda i: (i, 0)),
            full((1, rows)),
            full((wide, hidden)),
            full((hidden, depth)),
        ],
        out_specs=[
            pl.BlockSpec((block, hidden), lambda i: (i, 0)),
            pl.BlockSpec((block, hidden), lambda i: (i, 0)),
            pl.BlockSpec((block, depth), lambda i: (i, 0)),
            full((rows, depth)),
            full((depth, rows)),
            full((1, rows)),
        ],
        out_shape=[
            pltpu.HBM((rows, hidden), f32),
            pltpu.HBM((rows, hidden), bf16),
            pltpu.HBM((rows, depth), f32),
            jax.ShapeDtypeStruct((rows, depth), bf16),
            jax.ShapeDtypeStruct((depth, rows), bf16),
            jax.ShapeDtypeStruct((1, rows), jnp.int32),
        ],
        scratch_shapes=[pltpu.VMEM((rows, depth), bf16)],
        compiler_params=params("arbitrary"),
        name="head",
    )(in_hbm(embeddings), in_hbm(pairing.reshape(1, rows)), in_hbm(w_in), in_hbm(w_out))


def unit_of(protos):
    proto_f = protos.astype(f32)
    inv = lax.rsqrt(jnp.sum(proto_f * proto_f, axis=1, keepdims=True) + norm_eps)
    return proto_f, inv, proto_f * inv


WHOLE = pl.BlockSpec(memory_space=pltpu.VMEM)


def scaled_pair(x, axis):
    wide = x.astype(f32) * EXP2_SCALE
    hi = wide.astype(bf16)
    lo = (wide - hi.astype(f32)).astype(bf16)
    return jnp.concatenate([hi, lo], axis=axis)


def first_kernel(block, chunk, tile, views, protos, expo, col, tot, pair, stage, tot_acc):
    rows, depth = views.shape
    width = protos.shape[0]
    tot_acc[...] = jnp.zeros_like(tot_acc)
    pair[...] = scaled_pair(views[...], 1)

    def one(j, carry):
        here = pl.ds(pl.multiple_of(j * block, block), block)
        _, _, unit = unit_of(protos[here, :])
        unit16 = unit.astype(bf16)
        twice = jnp.concatenate([unit16, unit16], axis=1)
        running = jnp.zeros((8, block), f32)
        for c in range(rows // chunk):
            stage[c % 2] = dot(pair[c * chunk : (c + 1) * chunk, :], twice, NT)
            for start in range(0, chunk, tile):
                part = slice(c * chunk + start, c * chunk + start + tile)
                soft = jnp.exp2(stage[c % 2, start : start + tile, :])
                hard = soft * soft
                expo[part, here] = hard.astype(bf16)
                lanes = soft[:, :128]
                for k in range(1, block // 128):
                    lanes = lanes + soft[:, k * 128 : (k + 1) * 128]
                tot_acc[part, :] += lanes
                for k in range(0, tile, 8):
                    running = running + hard[k : k + 8]
        col[:, here] = jnp.sum(running, axis=0, keepdims=True)
        return carry

    lax.fori_loop(0, width // block, one, 0)
    tot[...] = jnp.sum(tot_acc[...].T, axis=0, keepdims=True)


def first_pass(views, protos):
    rows, depth = views.shape
    width = protos.shape[0]
    block = min(512, width)
    chunk = min(256, rows)
    tile = min(32, chunk)
    return pl.pallas_call(
        functools.partial(first_kernel, block, chunk, tile),
        in_specs=[WHOLE] * 2,
        out_specs=[WHOLE] * 3,
        out_shape=[
            pltpu.VMEM((rows, width), bf16),
            jax.ShapeDtypeStruct((1, width), f32),
            jax.ShapeDtypeStruct((1, rows), f32),
        ],
        scratch_shapes=[
            pltpu.VMEM((rows, 2 * depth), bf16),
            pltpu.VMEM((2, chunk, block), f32),
            pltpu.VMEM((rows, 128), f32),
        ],
        compiler_params=params(),
        cost_estimate=SMALL,
        name="first_pass",
    )(views, protos)


def sum_parts(parts, width):
    if len(parts[0].shape) == 3:
        parts = [parts[0].at[k] for k in range(parts[0].shape[0])]
    total = parts[0][:, :width]
    for other in parts[1:]:
        total = total + other[:, :width]
    return total


def add_fours(terms):
    total = None
    for k in range(0, len(terms), 4):
        four = terms[k : k + 4]
        while len(four) > 1:
            four = [x + y for x, y in zip(four[::2], four[1::2])]
        part = four[0].astype(f32)
        total = part if total is None else total + part
    return total


def rowsum_tile(expo, here, spread, tall, width):
    terms = []
    total = None
    for k in range(width // 128):
        lanes = slice(k * 128, (k + 1) * 128)
        weight = jnp.concatenate([spread[:, lanes]] * (tall // 16), axis=0)
        terms.append(expo[here, lanes] * weight)
        if len(terms) == 4 or k == width // 128 - 1:
            part = add_fours(terms)
            total = part if total is None else total + part
            terms = []
    return total


def rowsum_kernel(count, expo, *refs):
    parts = refs[:count]
    scale, out, spread, acc = refs[count:]
    rows, width = expo.shape
    inverse = 1.0 / sum_parts(parts, width)
    scale[...] = inverse
    spread[...] = jnp.broadcast_to(inverse, spread.shape).astype(bf16)
    tall = 64

    def one(i, carry):
        here = pl.ds(pl.multiple_of(i * tall, tall), tall)
        acc[here, :] = rowsum_tile(expo, here, spread, tall, width)
        return carry

    lax.fori_loop(0, rows // tall, one, 0)
    out[...] = jnp.sum(acc[...].T, axis=0, keepdims=True)


def rowsum(expo, parts):
    rows, width = expo.shape
    return pl.pallas_call(
        functools.partial(rowsum_kernel, len(parts)),
        in_specs=[WHOLE] * (1 + len(parts)),
        out_specs=[WHOLE] * 2,
        out_shape=[
            jax.ShapeDtypeStruct((1, width), f32),
            jax.ShapeDtypeStruct((1, rows), f32),
        ],
        scratch_shapes=[pltpu.VMEM((16, width), bf16), pltpu.VMEM((rows, 128), f32)],
        compiler_params=params(),
        cost_estimate=SMALL,
        name="rowsum",
    )(in_vmem(expo), *parts)


def split_rows(vec):
    hi = vec.astype(bf16).astype(f32)
    n = vec.shape[1]
    row = lax.broadcasted_iota(jnp.int32, (8, n), 0)
    hi8 = jnp.broadcast_to(hi, (8, n))
    lo8 = jnp.broadcast_to(vec - hi, (8, n))
    return jnp.where(row == 0, hi8, jnp.where(row == 1, lo8, 0.0))


def rowsum_last_kernel(pieces, count, *refs):
    expos = refs[:pieces]
    parts = refs[pieces : pieces + count]
    unit_t, scale, out, code, acc = refs[pieces + count :]
    step = pl.program_id(0)
    depth, block = unit_t.shape
    deep = expos[0].shape[1]
    inverse = 1.0 / sum_parts(parts, block)
    scale[...] = inverse

    @pl.when(step == 0)
    def _():
        acc[...] = jnp.zeros_like(acc)

    for k in range(pieces):
        here = slice(k * deep, (k + 1) * deep)
        scaled = unit_t[:, here].astype(f32) * inverse[:, here]
        pad = jnp.zeros((depth - 8, deep), f32)
        weights = jnp.concatenate([scaled, split_rows(inverse[:, here]), pad], axis=0)
        acc[...] += dot(expos[k][...], weights.astype(bf16), NT)

    @pl.when(step == pl.num_programs(0) - 1)
    def _():
        sums = acc[:, depth:].T
        out[...] = sums[0:1] + sums[1:2]
        code[...] = acc[:, :depth]


def rowsum_last(expo, parts, unit_t):
    rows, width = expo.shape
    depth = unit_t.shape[0]
    block = min(2048, width)
    pieces = 4
    deep = block // pieces
    vec = pl.BlockSpec((1, block), lambda j: (0, j))
    return pl.pallas_call(
        functools.partial(rowsum_last_kernel, pieces, len(parts)),
        grid=(width // block,),
        in_specs=[
            pl.BlockSpec((rows, deep), lambda j, k=k: (0, j * pieces + k)) for k in range(pieces)
        ]
        + [vec] * len(parts)
        + [pl.BlockSpec((depth, block), lambda j: (0, j))],
        out_specs=[vec, full((1, rows)), full((rows, depth))],
        out_shape=[
            jax.ShapeDtypeStruct((1, width), f32),
            jax.ShapeDtypeStruct((1, rows), f32),
            jax.ShapeDtypeStruct((rows, depth), f32),
        ],
        scratch_shapes=[pltpu.VMEM((rows, 2 * depth), f32)],
        compiler_params=params("arbitrary", limit=VMEM_LIMIT + 4 * 1024 * 1024),
        cost_estimate=SMALL,
        name="rowsum_last",
    )(*[in_hbm(expo)] * pieces, *parts, in_hbm(unit_t))


def unit_t_kernel(block, lead, protos, *refs):
    out = refs[-1]

    def one(j, carry):
        here = pl.ds(pl.multiple_of(lead + j * block, block), block)
        _, _, unit = unit_of(protos[here, :])
        out[:, here] = unit.astype(bf16).astype(f32).T.astype(bf16)
        return carry

    lax.fori_loop(0, protos.shape[0] // 2 // block, one, 0)


def unit_transposed(protos, *before):
    width, depth = protos.shape
    lead = width // 2 if before else 0
    return pl.pallas_call(
        functools.partial(unit_t_kernel, min(512, width // 2), lead),
        in_specs=[WHOLE] * (1 + len(before)),
        out_specs=WHOLE,
        out_shape=jax.ShapeDtypeStruct((depth, width), bf16),
        input_output_aliases={1: 0} if before else {},
        compiler_params=params(),
        cost_estimate=SMALL,
        name="unit_t",
    )(protos, *before)


def colsum_kernel(count, expo, *refs):
    parts = refs[:count]
    rest = refs[count:]
    out, spread = rest[-2:]
    rows, width = expo.shape
    inverse = 1.0 / sum_parts(parts, rows)
    spread[...] = jnp.broadcast_to(inverse, (128, rows)).T.astype(bf16)
    block = min(512, width)

    def one(j, carry):
        here = pl.ds(pl.multiple_of(j * block, block), block)
        running = jnp.zeros((16, block), f32)
        for i in range(0, rows // 16, 4):
            terms = []
            for k in range(i, min(i + 4, rows // 16)):
                part = slice(k * 16, (k + 1) * 16)
                weight = jnp.concatenate([spread[part, :]] * (block // 128), axis=1)
                terms.append(expo[part, here] * weight)
            running = running + add_fours(terms)
        total = jnp.sum(running, axis=0, keepdims=True)
        for k in range(out.shape[0]):
            out[k, :, here] = total
        return carry

    lax.fori_loop(0, width // block, one, 0)
    if len(rest) > 2:
        for k in range(out.shape[0]):
            out[k, :, width:] = rest[0][...]


def colsum(expo, parts, copies=1, behind=()):
    rows, width = expo.shape
    long = width + sum(x.shape[1] for x in behind)
    return pl.pallas_call(
        functools.partial(colsum_kernel, len(parts)),
        in_specs=[WHOLE] * (1 + len(parts) + len(behind)),
        out_specs=WHOLE,
        out_shape=jax.ShapeDtypeStruct((copies, 1, long), f32),
        scratch_shapes=[pltpu.VMEM((rows, 128), bf16)],
        compiler_params=params(),
        cost_estimate=SMALL,
        name="colsum",
    )(in_vmem(expo), *parts, *behind)


def proto_first_kernel(chunk, tile, lead, place, protos, views, totals, expo, grad, *scratch):
    weights, twice, pair, stage, soft16, acc = scratch
    count = expo.shape[1] // views.shape[2]
    _, depth, rows = views.shape
    width = protos.shape[0]
    _, _, unit = unit_of(protos[...])
    pair[...] = scaled_pair(unit.astype(bf16), 1)
    for n in range(count):
        k = lead + n
        weights[...] = (views[k].astype(f32) * (GRAD_SCALE / totals[place[0] ^ k])).astype(bf16)
        twice[:depth, :] = views[k]
        twice[depth:, :] = views[k]
        for c in range(width // chunk):
            stage[c % 2] = dot(pair[c * chunk : (c + 1) * chunk, :], twice[...])
            for start in range(0, chunk, tile):
                part = slice(c * chunk + start, c * chunk + start + tile)
                soft = jnp.exp2(stage[c % 2, start : start + tile, :])
                soft16[part, :] = soft.astype(bf16)
                expo[part, n * rows : (n + 1) * rows] = (soft * soft).astype(bf16)
        found = dot(soft16[...], weights[...], NT)
        if n == 0:
            acc[...] = found
        else:
            acc[...] += found
    grad[...] = acc[...]


def proto_first(place, protos, views, totals, lead, count):
    width, depth = protos.shape
    rows = views.shape[2]
    chunk = min(256, width)
    tile = min(16, chunk)
    return pl.pallas_call(
        functools.partial(proto_first_kernel, chunk, tile, lead),
        in_specs=[pl.BlockSpec(memory_space=pltpu.SMEM)] + [WHOLE] * 3,
        out_specs=[WHOLE] * 2,
        out_shape=[
            pltpu.VMEM((width, count * rows), bf16),
            jax.ShapeDtypeStruct((width, depth), f32),
        ],
        scratch_shapes=[
            pltpu.VMEM((depth, rows), bf16),
            pltpu.VMEM((2 * depth, rows), bf16),
            pltpu.VMEM((width, 2 * depth), bf16),
            pltpu.VMEM((2, chunk, rows), f32),
            pltpu.VMEM((width, rows), bf16),
            pltpu.VMEM((width, depth), f32),
        ],
        compiler_params=params(),
        cost_estimate=SMALL,
        name="proto_first",
    )(place, protos, views, totals)


def proto_last_kernel(groups, place, *refs):
    expos, grads = refs[:groups], refs[groups : 2 * groups]
    scale, protos, views, totals, out, weights, acc = refs[2 * groups :]
    count, depth, rows = views.shape
    each = count // groups
    for k in range(count):
        mates = swap_lanes(views[k])
        weights[...] = (mates.astype(f32) * (GRAD_SCALE / totals[place[0] ^ k])).astype(bf16)
        found = dot(expos[k // each][:, (k % each) * rows : (k % each + 1) * rows], weights[...], NT)
        if k == 0:
            acc[...] = found
        else:
            acc[...] += found
    width = protos.shape[0]
    there = pl.ds(pl.multiple_of(place[0] * width, width), width)
    unit_grad = grads[0][...]
    for other in grads[1:]:
        unit_grad = unit_grad + other[...]
    unit_grad = unit_grad - to_column(scale[:, there]) * acc[...]
    proto_f, inv, _ = unit_of(protos[...])
    inner = jnp.sum(proto_f * unit_grad, axis=1, keepdims=True)
    out[...] = (inv * unit_grad - proto_f * (inv * inv * inv) * inner).astype(bf16)


def proto_last(place, expos, grads, scale, protos, views, totals):
    width, depth = protos.shape
    rows = views.shape[2]
    groups = len(expos)
    return pl.pallas_call(
        functools.partial(proto_last_kernel, groups),
        in_specs=[pl.BlockSpec(memory_space=pltpu.SMEM)] + [WHOLE] * (2 * groups + 4),
        out_specs=WHOLE,
        out_shape=jax.ShapeDtypeStruct((width, depth), bf16),
        scratch_shapes=[pltpu.VMEM((depth, rows), bf16), pltpu.VMEM((width, depth), f32)],
        compiler_params=params(),
        name="proto_last",
    )(place, *[in_vmem(x) for x in expos], *grads, scale, protos, views, totals)


def view_soft_kernel(block, tile, lead, views, protos, out, pair, stage, soft16):
    rows, depth = views.shape
    pair[...] = scaled_pair(views[...], 1)
    out[...] = jnp.zeros_like(out)
    chunk = stage.shape[1]

    def one(j, carry):
        here = pl.ds(pl.multiple_of(lead + j * block, block), block)
        _, _, unit = unit_of(protos[here, :])
        unit16 = unit.astype(bf16)
        twice = jnp.concatenate([unit16, unit16], axis=1)
        for c in range(rows // chunk):
            stage[c % 2] = dot(pair[c * chunk : (c + 1) * chunk, :], twice, NT)
            for start in range(0, chunk, tile):
                part = slice(c * chunk + start, c * chunk + start + tile)
                soft16[part, :] = jnp.exp2(stage[c % 2, start : start + tile, :]).astype(bf16)
        out[...] += dot(soft16[...], unit16)
        return carry

    return one


def view_soft_body(block, tile, lead, count, *refs):
    lax.fori_loop(0, count // block, view_soft_kernel(block, tile, lead, *refs), 0)


def view_soft(views, protos, lead, count):
    rows, depth = views.shape
    block = min(512, count)
    chunk = min(256, rows)
    return pl.pallas_call(
        functools.partial(view_soft_body, block, min(32, chunk), lead, count),
        in_specs=[WHOLE] * 2,
        out_specs=WHOLE,
        out_shape=jax.ShapeDtypeStruct((rows, depth), f32),
        scratch_shapes=[
            pltpu.VMEM((rows, 2 * depth), bf16),
            pltpu.VMEM((2, chunk, block), f32),
            pltpu.VMEM((rows, block), bf16),
        ],
        compiler_params=params(),
        cost_estimate=SMALL,
        name="view_soft",
    )(views, protos)


def view_grad_kernel(code, tot, total, *refs):
    softs, out = refs[:-1], refs[-1]
    soft = softs[0][...]
    for other in softs[1:]:
        soft = soft + other[...]
    soft = soft * to_column(GRAD_SCALE / tot[...])
    hard = swap_rows(code[...] * to_column(GRAD_SCALE / total[...]))
    out[...] = (soft - hard).astype(out.dtype)


def view_grad_part(code, tot, total, *softs):
    operands = [code, tot, total, *softs]
    return pl.pallas_call(
        view_grad_kernel,
        grid=(1,),
        in_specs=[full(x.shape) for x in operands],
        out_specs=full(code.shape),
        out_shape=jax.ShapeDtypeStruct(code.shape, bf16),
        compiler_params=params("arbitrary"),
        cost_estimate=SMALL,
        name="view_grad",
    )(code, tot, total, *[in_hbm(x) for x in softs])


def backward_kernel(share, turn, grad_a, grad_b, pos, raw, pre, emb, hid, w_out, out, g_all):
    total = grad_a[...].astype(f32) + grad_b[...].astype(f32)
    n, depth = raw.shape
    place = jnp.broadcast_to(pos[...].astype(f32), (8, n)).T[:, :1].astype(jnp.int32)
    lane = lax.broadcasted_iota(jnp.int32, (n, n), 1)
    move = jnp.where(lane == place, 1.0, 0.0).astype(bf16)
    hi = total.astype(bf16)
    lo = (total - hi.astype(f32)).astype(bf16)
    moved = dot(move, jnp.concatenate([hi, lo], axis=1))
    grad = moved[:, :depth] + moved[:, depth:]
    raw_out = raw[...]
    inv = lax.rsqrt(jnp.sum(raw_out * raw_out, axis=1, keepdims=True) + norm_eps)
    inner = jnp.sum(raw_out * grad, axis=1, keepdims=True)
    d_raw = (inv * grad - raw_out * (inv * inv * inv) * inner).astype(bf16)
    g_all[...] = dot(hid[...], d_raw, TN)
    d_hidden = dot(d_raw, w_out[...], NT)
    v = pre[...]
    t = jnp.tanh(GELU_K * (v + GELU_A * (v * v * v)))
    slope = 0.5 * (1.0 + t) + (0.5 * GELU_K) * v * (1.0 - t * t) * (1.0 + (3.0 * GELU_A) * (v * v))
    d_pre = (slope * d_hidden).astype(bf16)
    g_in = dot(emb[...], d_pre, TN)
    count = out.shape[0]
    tall, wide = g_in.shape[0] // count, g_in.shape[1]
    base, short = tall * (wide // 128), share // count
    for k in range(count):
        n = mirrored(k, count)
        for q in range(wide // 128):
            out[n, q * tall : (q + 1) * tall, :] = g_in[
                k * tall : (k + 1) * tall, q * 128 : (q + 1) * 128
            ]
        low = pl.multiple_of(turn[0] * share + k * short, short)
        out[n, base : base + short, :] = g_all[pl.ds(low, short), :]


def mirrored(k, count):
    found = 0
    while count > 1:
        found = found * 2 + k % 2
        k //= 2
        count //= 2
    return found


def backward(nb, npr, turn, grad_a, grad_b, pos, raw, pre, emb, hid, w_out):
    rows, wide = emb.shape
    hidden, depth = w_out.shape
    part = wide // npr
    share = hidden // npr
    lines = (part * hidden + share * depth) // (nb * 128)
    operands = [grad_a, grad_b, pos, raw, pre, emb, hid, w_out]
    specs = [full(x.shape) for x in operands]
    specs[5] = pl.BlockSpec((rows, part), lambda i, turn: (0, turn[0]))
    return pl.pallas_call(
        functools.partial(backward_kernel, share),
        grid_spec=pltpu.PrefetchScalarGridSpec(
            num_scalar_prefetch=1,
            grid=(1,),
            in_specs=specs,
            out_specs=full((nb, lines, 128)),
            scratch_shapes=[pltpu.VMEM((hidden, depth), f32)],
        ),
        out_shape=jax.ShapeDtypeStruct((nb, lines, 128), f32),
        compiler_params=params("arbitrary"),
        name="backward",
    )(turn, grad_a, grad_b, pos, *[in_hbm(x) for x in operands[3:]])


def unpack_kernel(order, order_b, place, *refs):
    pieces, (g_in, g_out) = refs[:-2], refs[-2:]
    nb = len(order_b)
    npr = len(order)
    tall, wide = g_in.shape[0] // (nb * npr), g_in.shape[1]
    base, short = tall * (wide // 128), g_out.shape[0] // (nb * npr)
    half = pieces[0].shape[0]
    for n, flip in enumerate(order):
        for k, flip_b in enumerate(order_b):
            owner = (place[0] ^ flip) * nb + (place[1] ^ flip_b)
            x = pieces[n // half][n % half, k].astype(f32)
            low = pl.multiple_of(owner * tall, tall)
            for q in range(wide // 128):
                g_in[pl.ds(low, tall), q * 128 : (q + 1) * 128] = x[q * tall : (q + 1) * tall]
            low = pl.multiple_of(owner * short, short)
            g_out[pl.ds(low, short), :] = x[base : base + short]


def unpack(order, order_b, place, pieces, shape_in, shape_out):
    return pl.pallas_call(
        functools.partial(unpack_kernel, order, order_b),
        in_specs=[pl.BlockSpec(memory_space=pltpu.SMEM)] + [WHOLE] * len(pieces),
        out_specs=[WHOLE] * 2,
        out_shape=[jax.ShapeDtypeStruct(shape_in, f32), jax.ShapeDtypeStruct(shape_out, f32)],
        compiler_params=params(),
        name="unpack",
    )(place, *pieces)


def stages(size, first=1):
    found, step = ([[1]], 2) if first == 1 else ([], 1)
    while step < size:
        if step * 2 < size:
            found.append([step, step * 2, step * 3])
            step *= 4
        else:
            found.append([step])
            step *= 2
    return found


def body(nb, npr, embeddings, pairing, w_in, w_out, prototypes):
    b = lax.axis_index("batch")
    p = lax.axis_index("proto")
    rows, wide = embeddings.shape
    width, depth = prototypes.shape
    hidden_n = w_in.shape[1]
    own = width // nb

    def flipped(x, axis, size, step):
        return lax.ppermute(x, axis, [(i, i ^ step) for i in range(size)])

    def trade(x, axis, size, steps, queue=(), results=None):
        others = [flipped(x, axis, size, step) for step in steps]
        work = queue.pop(0) if queue else None
        if work:
            operands, _ = lax.optimization_barrier((work[1], x))
            others, found = lax.optimization_barrier((others, work[0](*operands)))
            results.append(found)
        return others

    def summed(x, axis, size, queue=(), results=None):
        rounds = stages(size, 1 if axis == "batch" else 2)
        for n, steps in enumerate(rounds):
            others = trade(x, axis, size, steps, queue, results)
            if n == len(rounds) - 1:
                return [x, *others]
            for other in others:
                x = x + other

    pre, hid, raw, views, views_t, pos = head(embeddings, pairing, w_in, w_out)
    views_all = lax.all_gather(views_t, "batch", axis=0)
    protos_own = lax.dynamic_slice_in_dim(prototypes, b * own, own, 0)
    place = b.astype(jnp.int32).reshape(1)
    turn_p = p.astype(jnp.int32).reshape(1)
    views, protos_own, place, turn_p = lax.optimization_barrier(
        (views, protos_own, place, turn_p)
    )
    expo, col, tot = first_pass(views, prototypes)

    groups = 4
    cols = width // groups
    softs = []
    queue = [
        (functools.partial(view_soft, lead=k * cols, count=cols), (views, prototypes))
        for k in range(groups)
    ]
    scale, row = rowsum(expo, summed(col, "batch", nb, queue, softs))
    rest = len(stages(npr, 2)) - 1
    queue = [None] * rest + queue
    both = sum(summed(jnp.concatenate([row, tot], axis=0), "proto", npr, queue, softs))
    totals, tot = [both[:1]], both[1:]

    def unit_half(protos):
        return unit_transposed(protos, *taken)

    taken = []
    halves = [(unit_half, (prototypes,))] * 2
    col = colsum(expo, totals)[0]
    tot_all = tot[None]
    rounds = stages(nb)
    for n, steps in enumerate(rounds):
        others = [flipped(tot_all, "batch", nb, step) for step in steps]
        if queue:
            parts = trade(col, "batch", nb, steps, queue, softs)
        else:
            parts = trade(col, "batch", nb, steps, halves, taken)
        others, parts = lax.optimization_barrier((others, parts))
        tot_all = jnp.concatenate([tot_all, *others], axis=0)
        if n < len(rounds) - 1:
            for part in parts:
                col = col + part
    scale, row = rowsum(expo, [col, *parts])
    halves = [None] * rest + halves
    col = colsum(expo, summed(row, "proto", npr, halves, taken))[0]
    unit_t = taken[-1]

    col, views_all = lax.optimization_barrier((col, views_all))
    each = nb // groups
    owns = []
    queue = [
        (
            functools.partial(proto_first, lead=k * each, count=each),
            (place, protos_own, views_all, tot_all),
        )
        for k in range(groups)
    ]
    scale, row, code = rowsum_last(expo, summed(col, "batch", nb, queue, owns), unit_t)
    queue = [None] * rest + queue
    total = sum(summed(row, "proto", npr, queue, owns))
    total_all = total[None]
    grads = []
    queue = [(view_grad_part, (code, tot, total, *softs))] + queue
    turn = 1
    for steps in stages(nb):
        others = trade(total_all, "batch", nb, steps, queue, grads if not grads else owns)
        if len(grads) > 1:
            grads = [(grads[0].astype(f32) + grads[1].astype(f32)).astype(bf16)]
            others[0], grads[0] = lax.optimization_barrier((others[0], grads[0]))
        if turn * 2 < npr:
            grads = [grads[0], flipped(grads[0], "proto", npr, turn)]
            turn *= 2
        total_all = jnp.concatenate([total_all, *others], axis=0)

    while turn * 2 < npr:
        if len(grads) > 1:
            grads = [(grads[0].astype(f32) + grads[1].astype(f32)).astype(bf16)]
        grads = [grads[0], flipped(grads[0], "proto", npr, turn)]
        turn *= 2
    if len(grads) > 1:
        grads = [(grads[0].astype(f32) + grads[1].astype(f32)).astype(bf16)]
    expos, parts = [x for x, _ in owns], [x for _, x in owns]
    queue = [(proto_last, (place, expos, parts, scale, protos_own, views_all, total_all))]
    found = []
    grads = [grads[0], *trade(grads[0], "proto", npr, [npr // 2], queue, found)]
    grad_proto = lax.all_gather(found[0], "batch", axis=0, tiled=True)
    both = backward(nb, npr, turn_p, *grads, pos, raw, pre, embeddings, hid, w_out)
    for steps in stages(nb):
        count = len(steps) + 1
        share = both.shape[0] // count
        mine = (b // steps[0]) % 2
        if count == 4:
            mine = mine * 2 + (b // steps[1]) % 2
        kept = lax.dynamic_slice_in_dim(both, mine * share, share, 0)
        for flip, step in zip([1] if count == 2 else [2, 1, 3], steps):
            away = lax.dynamic_slice_in_dim(both, (mine ^ flip) * share, share, 0)
            kept = kept + flipped(away.astype(bf16), "batch", nb, step).astype(f32)
        both = kept
    piece = both.astype(bf16)
    order_b = [0]
    for steps in reversed(stages(nb)):
        piece = jnp.concatenate(
            [piece, *[flipped(piece, "batch", nb, step) for step in steps]], axis=0
        )
        order_b = order_b + [i ^ step for step in steps for i in order_b]
    piece = piece[None]
    order = [0]
    step = npr // 2
    while step > 1:
        piece = jnp.concatenate([piece, flipped(piece, "proto", npr, step)], axis=0)
        order = order + [i ^ step for i in order]
        step //= 2
    pieces = [piece, flipped(piece, "proto", npr, 1)]
    order = order + [i ^ 1 for i in order]
    places = jnp.stack([p, b]).astype(jnp.int32)
    grad_in, grad_out = unpack(
        order, order_b, places, pieces, (wide, hidden_n), (hidden_n, depth)
    )
    return (grad_in, grad_out, grad_proto.astype(f32))


def solution(mesh):
    return jax.shard_map(
        functools.partial(body, mesh.shape["batch"], mesh.shape["proto"]),
        mesh=mesh,
        in_specs=(P("batch", None), P("batch"), P(), P(), P("proto", None)),
        out_specs=(P(), P(), P("proto", None)),
        check_vma=False,
    )
```

```python
import functools
import math

import jax
import jax.numpy as jnp
from jax import lax
from jax.experimental import pallas as pl
from jax.experimental.pallas import tpu as pltpu
from jax.sharding import PartitionSpec as P

ITERS = 3
norm_eps = 1e-06
code_temp = 0.05
pred_temp = 0.1
loss_scale = 64.0
GRAD_SCALE = loss_scale / pred_temp
EXP2_SCALE = math.log2(math.e) / pred_temp
GELU_K = math.sqrt(2.0 / math.pi)
GELU_A = 0.044715

f32 = jnp.float32
bf16 = jnp.bfloat16
NN = (((1,), (0,)), ((), ()))
NT = (((1,), (1,)), ((), ()))
TN = (((0,), (0,)), ((), ()))
VMEM_LIMIT = 12 * 1024 * 1024


def dot(a, b, dims=NN):
    return lax.dot_general(a, b, dims, preferred_element_type=f32)


SMALL = pl.CostEstimate(flops=1000, bytes_accessed=1000, transcendentals=0)


def params(*semantics, limit=VMEM_LIMIT):
    return pltpu.CompilerParams(dimension_semantics=semantics or None, vmem_limit_bytes=limit)


def to_column(vec):
    n = vec.shape[1]
    return jnp.broadcast_to(vec, (8, n)).T[:, :1]


def swap_lanes(x):
    half = x.shape[1] // 2
    return jnp.concatenate([x[:, half:], x[:, :half]], axis=1)


def swap_rows(x):
    half = x.shape[0] // 2
    return jnp.concatenate([x[half:], x[:half]], axis=0)


def in_vmem(x):
    return pltpu.with_memory_space_constraint(x, pltpu.VMEM)


def in_hbm(x):
    return pltpu.with_memory_space_constraint(x, pltpu.HBM)


def full(shape):
    return pl.BlockSpec(shape, lambda *_: (0,) * len(shape))


def head_kernel(emb, pairing, w_in, w_out, pre, hid, raw, views, views_t, pos, scratch):
    step = pl.program_id(0)
    rows = emb.shape[0]
    pre_act = dot(emb[...], w_in[...])
    pre[...] = pre_act
    t = jnp.tanh(GELU_K * (pre_act + GELU_A * (pre_act * pre_act * pre_act)))
    hidden = (0.5 * pre_act * (1.0 + t)).astype(bf16)
    hid[...] = hidden
    raw_out = dot(hidden, w_out[...])
    raw[...] = raw_out
    inv = lax.rsqrt(jnp.sum(raw_out * raw_out, axis=1, keepdims=True) + norm_eps)
    scratch[pl.ds(pl.multiple_of(step * rows, rows), rows), :] = (raw_out * inv).astype(bf16)

    @pl.when(step == pl.num_programs(0) - 1)
    def _():
        mate = pairing[...]
        n = mate.shape[1]
        lane = lax.broadcasted_iota(jnp.int32, (1, n), 1)
        first = lane < mate
        low = jnp.minimum(lane, mate)
        sub = lax.broadcasted_iota(jnp.int32, (n, n), 0)
        before = jnp.where(sub < low, 1.0, 0.0).astype(bf16)
        first8 = jnp.broadcast_to(jnp.where(first, 1.0, 0.0), (8, n)).astype(bf16)
        rank = dot(first8, before)[:1].astype(jnp.int32)
        place = jnp.where(first, rank, rank + n // 2)
        pos[...] = place
        move = jnp.where(sub == place, 1.0, 0.0).astype(bf16)
        ordered = dot(move, scratch[...])
        views[...] = ordered.astype(bf16)
        views_t[...] = ordered.T.astype(bf16)


def head(embeddings, pairing, w_in, w_out):
    rows, wide = embeddings.shape
    hidden = w_in.shape[1]
    depth = w_out.shape[1]
    steps = 4
    block = rows // steps
    return pl.pallas_call(
        head_kernel,
        grid=(steps,),
        in_specs=[
            pl.BlockSpec((block, wide), lambda i: (i, 0)),
            full((1, rows)),
            full((wide, hidden)),
            full((hidden, depth)),
        ],
        out_specs=[
            pl.BlockSpec((block, hidden), lambda i: (i, 0)),
            pl.BlockSpec((block, hidden), lambda i: (i, 0)),
            pl.BlockSpec((block, depth), lambda i: (i, 0)),
            full((rows, depth)),
            full((depth, rows)),
            full((1, rows)),
        ],
        out_shape=[
            pltpu.HBM((rows, hidden), f32),
            pltpu.HBM((rows, hidden), bf16),
            pltpu.HBM((rows, depth), f32),
            jax.ShapeDtypeStruct((rows, depth), bf16),
            jax.ShapeDtypeStruct((depth, rows), bf16),
            jax.ShapeDtypeStruct((1, rows), jnp.int32),
        ],
        scratch_shapes=[pltpu.VMEM((rows, depth), bf16)],
        compiler_params=params("arbitrary"),
        name="head",
    )(in_hbm(embeddings), in_hbm(pairing.reshape(1, rows)), in_hbm(w_in), in_hbm(w_out))


def unit_of(protos):
    proto_f = protos.astype(f32)
    inv = lax.rsqrt(jnp.sum(proto_f * proto_f, axis=1, keepdims=True) + norm_eps)
    return proto_f, inv, proto_f * inv


WHOLE = pl.BlockSpec(memory_space=pltpu.VMEM)


def scaled_pair(x, axis):
    wide = x.astype(f32) * EXP2_SCALE
    hi = wide.astype(bf16)
    lo = (wide - hi.astype(f32)).astype(bf16)
    return jnp.concatenate([hi, lo], axis=axis)


def first_kernel(block, chunk, tile, views, protos, expo, col, tot, pair, stage, tot_acc):
    rows, depth = views.shape
    width = protos.shape[0]
    tot_acc[...] = jnp.zeros_like(tot_acc)
    pair[...] = scaled_pair(views[...], 1)

    def one(j, carry):
        here = pl.ds(pl.multiple_of(j * block, block), block)
        _, _, unit = unit_of(protos[here, :])
        unit16 = unit.astype(bf16)
        twice = jnp.concatenate([unit16, unit16], axis=1)
        running = jnp.zeros((8, block), f32)
        for c in range(rows // chunk):
            stage[c % 2] = dot(pair[c * chunk : (c + 1) * chunk, :], twice, NT)
            for start in range(0, chunk, tile):
                part = slice(c * chunk + start, c * chunk + start + tile)
                soft = jnp.exp2(stage[c % 2, start : start + tile, :])
                hard = soft * soft
                expo[part, here] = hard.astype(bf16)
                lanes = soft[:, :128]
                for k in range(1, block // 128):
                    lanes = lanes + soft[:, k * 128 : (k + 1) * 128]
                tot_acc[part, :] += lanes
                for k in range(0, tile, 8):
                    running = running + hard[k : k + 8]
        col[:, here] = jnp.sum(running, axis=0, keepdims=True)
        return carry

    lax.fori_loop(0, width // block, one, 0)
    tot[...] = jnp.sum(tot_acc[...].T, axis=0, keepdims=True)


def first_pass(views, protos):
    rows, depth = views.shape
    width = protos.shape[0]
    block = min(512, width)
    chunk = min(256, rows)
    tile = min(32, chunk)
    return pl.pallas_call(
        functools.partial(first_kernel, block, chunk, tile),
        in_specs=[WHOLE] * 2,
        out_specs=[WHOLE] * 3,
        out_shape=[
            pltpu.VMEM((rows, width), bf16),
            jax.ShapeDtypeStruct((1, width), f32),
            jax.ShapeDtypeStruct((1, rows), f32),
        ],
        scratch_shapes=[
            pltpu.VMEM((rows, 2 * depth), bf16),
            pltpu.VMEM((2, chunk, block), f32),
            pltpu.VMEM((rows, 128), f32),
        ],
        compiler_params=params(),
        cost_estimate=SMALL,
        name="first_pass",
    )(views, protos)


def sum_parts(parts, width):
    if len(parts[0].shape) == 3:
        parts = [parts[0].at[k] for k in range(parts[0].shape[0])]
    total = parts[0][:, :width]
    for other in parts[1:]:
        total = total + other[:, :width]
    return total


def add_fours(terms):
    total = None
    for k in range(0, len(terms), 4):
        four = terms[k : k + 4]
        while len(four) > 1:
            four = [x + y for x, y in zip(four[::2], four[1::2])]
        part = four[0].astype(f32)
        total = part if total is None else total + part
    return total


def rowsum_tile(expo, here, spread, tall, width):
    terms = []
    total = None
    for k in range(width // 128):
        lanes = slice(k * 128, (k + 1) * 128)
        weight = jnp.concatenate([spread[:, lanes]] * (tall // 16), axis=0)
        terms.append(expo[here, lanes] * weight)
        if len(terms) == 4 or k == width // 128 - 1:
            part = add_fours(terms)
            total = part if total is None else total + part
            terms = []
    return total


def rowsum_kernel(count, expo, *refs):
    parts = refs[:count]
    scale, out, spread, acc = refs[count:]
    rows, width = expo.shape
    inverse = 1.0 / sum_parts(parts, width)
    scale[...] = inverse
    spread[...] = jnp.broadcast_to(inverse, spread.shape).astype(bf16)
    tall = 64

    def one(i, carry):
        here = pl.ds(pl.multiple_of(i * tall, tall), tall)
        acc[here, :] = rowsum_tile(expo, here, spread, tall, width)
        return carry

    lax.fori_loop(0, rows // tall, one, 0)
    out[...] = jnp.sum(acc[...].T, axis=0, keepdims=True)


def rowsum(expo, parts):
    rows, width = expo.shape
    return pl.pallas_call(
        functools.partial(rowsum_kernel, len(parts)),
        in_specs=[WHOLE] * (1 + len(parts)),
        out_specs=[WHOLE] * 2,
        out_shape=[
            jax.ShapeDtypeStruct((1, width), f32),
            jax.ShapeDtypeStruct((1, rows), f32),
        ],
        scratch_shapes=[pltpu.VMEM((16, width), bf16), pltpu.VMEM((rows, 128), f32)],
        compiler_params=params(),
        cost_estimate=SMALL,
        name="rowsum",
    )(in_vmem(expo), *parts)


def split_rows(vec):
    hi = vec.astype(bf16).astype(f32)
    n = vec.shape[1]
    row = lax.broadcasted_iota(jnp.int32, (8, n), 0)
    hi8 = jnp.broadcast_to(hi, (8, n))
    lo8 = jnp.broadcast_to(vec - hi, (8, n))
    return jnp.where(row == 0, hi8, jnp.where(row == 1, lo8, 0.0))


def rowsum_last_kernel(pieces, count, *refs):
    expos = refs[:pieces]
    parts = refs[pieces : pieces + count]
    unit_t, scale, out, code, acc = refs[pieces + count :]
    step = pl.program_id(0)
    depth, block = unit_t.shape
    deep = expos[0].shape[1]
    inverse = 1.0 / sum_parts(parts, block)
    scale[...] = inverse

    @pl.when(step == 0)
    def _():
        acc[...] = jnp.zeros_like(acc)

    for k in range(pieces):
        here = slice(k * deep, (k + 1) * deep)
        scaled = unit_t[:, here].astype(f32) * inverse[:, here]
        pad = jnp.zeros((depth - 8, deep), f32)
        weights = jnp.concatenate([scaled, split_rows(inverse[:, here]), pad], axis=0)
        acc[...] += dot(expos[k][...], weights.astype(bf16), NT)

    @pl.when(step == pl.num_programs(0) - 1)
    def _():
        sums = acc[:, depth:].T
        out[...] = sums[0:1] + sums[1:2]
        code[...] = acc[:, :depth]


def rowsum_last(expo, parts, unit_t):
    rows, width = expo.shape
    depth = unit_t.shape[0]
    block = min(2048, width)
    pieces = 4
    deep = block // pieces
    vec = pl.BlockSpec((1, block), lambda j: (0, j))
    return pl.pallas_call(
        functools.partial(rowsum_last_kernel, pieces, len(parts)),
        grid=(width // block,),
        in_specs=[
            pl.BlockSpec((rows, deep), lambda j, k=k: (0, j * pieces + k)) for k in range(pieces)
        ]
        + [vec] * len(parts)
        + [pl.BlockSpec((depth, block), lambda j: (0, j))],
        out_specs=[vec, full((1, rows)), full((rows, depth))],
        out_shape=[
            jax.ShapeDtypeStruct((1, width), f32),
            jax.ShapeDtypeStruct((1, rows), f32),
            jax.ShapeDtypeStruct((rows, depth), f32),
        ],
        scratch_shapes=[pltpu.VMEM((rows, 2 * depth), f32)],
        compiler_params=params("arbitrary", limit=VMEM_LIMIT + 4 * 1024 * 1024),
        cost_estimate=SMALL,
        name="rowsum_last",
    )(*[in_hbm(expo)] * pieces, *parts, in_hbm(unit_t))


def unit_t_kernel(block, lead, protos, *refs):
    out = refs[-1]

    def one(j, carry):
        here = pl.ds(pl.multiple_of(lead + j * block, block), block)
        _, _, unit = unit_of(protos[here, :])
        out[:, here] = unit.astype(bf16).astype(f32).T.astype(bf16)
        return carry

    lax.fori_loop(0, protos.shape[0] // 2 // block, one, 0)


def unit_transposed(protos, *before):
    width, depth = protos.shape
    lead = width // 2 if before else 0
    return pl.pallas_call(
        functools.partial(unit_t_kernel, min(512, width // 2), lead),
        in_specs=[WHOLE] * (1 + len(before)),
        out_specs=WHOLE,
        out_shape=jax.ShapeDtypeStruct((depth, width), bf16),
        input_output_aliases={1: 0} if before else {},
        compiler_params=params(),
        cost_estimate=SMALL,
        name="unit_t",
    )(protos, *before)


def colsum_kernel(count, expo, *refs):
    parts = refs[:count]
    rest = refs[count:]
    out, spread = rest[-2:]
    rows, width = expo.shape
    inverse = 1.0 / sum_parts(parts, rows)
    spread[...] = jnp.broadcast_to(inverse, (128, rows)).T.astype(bf16)
    block = min(512, width)

    def one(j, carry):
        here = pl.ds(pl.multiple_of(j * block, block), block)
        running = jnp.zeros((16, block), f32)
        for i in range(0, rows // 16, 4):
            terms = []
            for k in range(i, min(i + 4, rows // 16)):
                part = slice(k * 16, (k + 1) * 16)
                weight = jnp.concatenate([spread[part, :]] * (block // 128), axis=1)
                terms.append(expo[part, here] * weight)
            running = running + add_fours(terms)
        total = jnp.sum(running, axis=0, keepdims=True)
        for k in range(out.shape[0]):
            out[k, :, here] = total
        return carry

    lax.fori_loop(0, width // block, one, 0)
    if len(rest) > 2:
        for k in range(out.shape[0]):
            out[k, :, width:] = rest[0][...]


def colsum(expo, parts, copies=1, behind=()):
    rows, width = expo.shape
    long = width + sum(x.shape[1] for x in behind)
    return pl.pallas_call(
        functools.partial(colsum_kernel, len(parts)),
        in_specs=[WHOLE] * (1 + len(parts) + len(behind)),
        out_specs=WHOLE,
        out_shape=jax.ShapeDtypeStruct((copies, 1, long), f32),
        scratch_shapes=[pltpu.VMEM((rows, 128), bf16)],
        compiler_params=params(),
        cost_estimate=SMALL,
        name="colsum",
    )(in_vmem(expo), *parts, *behind)


def proto_first_kernel(chunk, tile, lead, place, protos, views, totals, expo, grad, *scratch):
    weights, twice, pair, stage, soft16, acc, near, arrived = scratch
    count = expo.shape[1] // views.shape[2]
    _, depth, rows = views.shape
    width = protos.shape[0]
    copies = [
        pltpu.make_async_copy(views.at[lead + n], near.at[n], arrived.at[n]) for n in range(count)
    ]
    for copy in copies:
        copy.start()
    _, _, unit = unit_of(protos[...])
    pair[...] = scaled_pair(unit.astype(bf16), 1)
    for n in range(count):
        copies[n].wait()
        total = totals[place[0] ^ (lead + n)]
        weights[...] = (near[n].astype(f32) * (GRAD_SCALE / total)).astype(bf16)
        twice[:depth, :] = near[n]
        twice[depth:, :] = near[n]
        for c in range(width // chunk):
            stage[c % 2] = dot(pair[c * chunk : (c + 1) * chunk, :], twice[...])
            for start in range(0, chunk, tile):
                part = slice(c * chunk + start, c * chunk + start + tile)
                soft = jnp.exp2(stage[c % 2, start : start + tile, :])
                soft16[part, :] = soft.astype(bf16)
                expo[part, n * rows : (n + 1) * rows] = (soft * soft).astype(bf16)
        found = dot(soft16[...], weights[...], NT)
        if n == 0:
            acc[...] = found
        else:
            acc[...] += found
    grad[...] = acc[...]


def proto_first(place, protos, views, totals, lead, count):
    width, depth = protos.shape
    rows = views.shape[2]
    chunk = min(256, width)
    tile = min(16, chunk)
    return pl.pallas_call(
        functools.partial(proto_first_kernel, chunk, tile, lead),
        in_specs=[
            pl.BlockSpec(memory_space=pltpu.SMEM),
            WHOLE,
            pl.BlockSpec(memory_space=pl.ANY),
            WHOLE,
        ],
        out_specs=[WHOLE] * 2,
        out_shape=[
            pltpu.VMEM((width, count * rows), bf16),
            jax.ShapeDtypeStruct((width, depth), f32),
        ],
        scratch_shapes=[
            pltpu.VMEM((depth, rows), bf16),
            pltpu.VMEM((2 * depth, rows), bf16),
            pltpu.VMEM((width, 2 * depth), bf16),
            pltpu.VMEM((2, chunk, rows), f32),
            pltpu.VMEM((width, rows), bf16),
            pltpu.VMEM((width, depth), f32),
            pltpu.VMEM((count, depth, rows), bf16),
            pltpu.SemaphoreType.DMA((count,)),
        ],
        compiler_params=params(),
        cost_estimate=SMALL,
        name="proto_first",
    )(place, protos, in_hbm(views), totals)


def proto_last_kernel(groups, place, *refs):
    expos, grads = refs[:groups], refs[groups : 2 * groups]
    scale, protos, views, totals, out, weights, acc = refs[2 * groups :]
    count, depth, rows = views.shape
    each = count // groups
    for k in range(count):
        mates = swap_lanes(views[k])
        weights[...] = (mates.astype(f32) * (GRAD_SCALE / totals[place[0] ^ k])).astype(bf16)
        found = dot(expos[k // each][:, (k % each) * rows : (k % each + 1) * rows], weights[...], NT)
        if k == 0:
            acc[...] = found
        else:
            acc[...] += found
    width = protos.shape[0]
    there = pl.ds(pl.multiple_of(place[0] * width, width), width)
    unit_grad = grads[0][...]
    for other in grads[1:]:
        unit_grad = unit_grad + other[...]
    unit_grad = unit_grad - to_column(scale[:, there]) * acc[...]
    proto_f, inv, _ = unit_of(protos[...])
    inner = jnp.sum(proto_f * unit_grad, axis=1, keepdims=True)
    out[...] = (inv * unit_grad - proto_f * (inv * inv * inv) * inner).astype(bf16)


def proto_last(place, expos, grads, scale, protos, views, totals):
    width, depth = protos.shape
    rows = views.shape[2]
    groups = len(expos)
    return pl.pallas_call(
        functools.partial(proto_last_kernel, groups),
        in_specs=[pl.BlockSpec(memory_space=pltpu.SMEM)] + [WHOLE] * (2 * groups + 4),
        out_specs=WHOLE,
        out_shape=jax.ShapeDtypeStruct((width, depth), bf16),
        scratch_shapes=[pltpu.VMEM((depth, rows), bf16), pltpu.VMEM((width, depth), f32)],
        compiler_params=params(),
        name="proto_last",
    )(place, *[in_vmem(x) for x in expos], *grads, scale, protos, views, totals)


def view_soft_kernel(block, tile, lead, views, protos, out, pair, stage, soft16):
    rows, depth = views.shape
    pair[...] = scaled_pair(views[...], 1)
    out[...] = jnp.zeros_like(out)
    chunk = stage.shape[1]

    def one(j, carry):
        here = pl.ds(pl.multiple_of(lead + j * block, block), block)
        _, _, unit = unit_of(protos[here, :])
        unit16 = unit.astype(bf16)
        twice = jnp.concatenate([unit16, unit16], axis=1)
        for c in range(rows // chunk):
            stage[c % 2] = dot(pair[c * chunk : (c + 1) * chunk, :], twice, NT)
            for start in range(0, chunk, tile):
                part = slice(c * chunk + start, c * chunk + start + tile)
                soft16[part, :] = jnp.exp2(stage[c % 2, start : start + tile, :]).astype(bf16)
        out[...] += dot(soft16[...], unit16)
        return carry

    return one


def view_soft_body(block, tile, lead, count, *refs):
    lax.fori_loop(0, count // block, view_soft_kernel(block, tile, lead, *refs), 0)


def view_soft(views, protos, lead, count):
    rows, depth = views.shape
    block = min(512, count)
    chunk = min(256, rows)
    return pl.pallas_call(
        functools.partial(view_soft_body, block, min(32, chunk), lead, count),
        in_specs=[WHOLE] * 2,
        out_specs=WHOLE,
        out_shape=jax.ShapeDtypeStruct((rows, depth), f32),
        scratch_shapes=[
            pltpu.VMEM((rows, 2 * depth), bf16),
            pltpu.VMEM((2, chunk, block), f32),
            pltpu.VMEM((rows, block), bf16),
        ],
        compiler_params=params(),
        cost_estimate=SMALL,
        name="view_soft",
    )(views, protos)


def view_grad_kernel(code, tot, total, *refs):
    softs, out = refs[:-1], refs[-1]
    soft = softs[0][...]
    for other in softs[1:]:
        soft = soft + other[...]
    soft = soft * to_column(GRAD_SCALE / tot[...])
    hard = swap_rows(code[...] * to_column(GRAD_SCALE / total[...]))
    out[...] = (soft - hard).astype(out.dtype)


def view_grad_part(code, tot, total, *softs):
    operands = [code, tot, total, *softs]
    return pl.pallas_call(
        view_grad_kernel,
        grid=(1,),
        in_specs=[full(x.shape) for x in operands],
        out_specs=full(code.shape),
        out_shape=jax.ShapeDtypeStruct(code.shape, bf16),
        compiler_params=params("arbitrary"),
        cost_estimate=SMALL,
        name="view_grad",
    )(code, tot, total, *[in_hbm(x) for x in softs])


def backward_kernel(share, turn, grad_a, grad_b, pos, raw, pre, emb, hid, w_out, out, g_all):
    total = grad_a[...].astype(f32) + grad_b[...].astype(f32)
    n, depth = raw.shape
    place = jnp.broadcast_to(pos[...].astype(f32), (8, n)).T[:, :1].astype(jnp.int32)
    lane = lax.broadcasted_iota(jnp.int32, (n, n), 1)
    move = jnp.where(lane == place, 1.0, 0.0).astype(bf16)
    hi = total.astype(bf16)
    lo = (total - hi.astype(f32)).astype(bf16)
    moved = dot(move, jnp.concatenate([hi, lo], axis=1))
    grad = moved[:, :depth] + moved[:, depth:]
    raw_out = raw[...]
    inv = lax.rsqrt(jnp.sum(raw_out * raw_out, axis=1, keepdims=True) + norm_eps)
    inner = jnp.sum(raw_out * grad, axis=1, keepdims=True)
    d_raw = (inv * grad - raw_out * (inv * inv * inv) * inner).astype(bf16)
    g_all[...] = dot(hid[...], d_raw, TN)
    d_hidden = dot(d_raw, w_out[...], NT)
    v = pre[...]
    t = jnp.tanh(GELU_K * (v + GELU_A * (v * v * v)))
    slope = 0.5 * (1.0 + t) + (0.5 * GELU_K) * v * (1.0 - t * t) * (1.0 + (3.0 * GELU_A) * (v * v))
    d_pre = (slope * d_hidden).astype(bf16)
    g_in = dot(emb[...], d_pre, TN)
    count = out.shape[0]
    tall, wide = g_in.shape[0] // count, g_in.shape[1]
    base, short = tall * (wide // 128), share // count
    for k in range(count):
        n = mirrored(k, count)
        for q in range(wide // 128):
            out[n, q * tall : (q + 1) * tall, :] = g_in[
                k * tall : (k + 1) * tall, q * 128 : (q + 1) * 128
            ]
        low = pl.multiple_of(turn[0] * share + k * short, short)
        out[n, base : base + short, :] = g_all[pl.ds(low, short), :]


def mirrored(k, count):
    found = 0
    while count > 1:
        found = found * 2 + k % 2
        k //= 2
        count //= 2
    return found


def backward(nb, npr, turn, grad_a, grad_b, pos, raw, pre, emb, hid, w_out):
    rows, wide = emb.shape
    hidden, depth = w_out.shape
    part = wide // npr
    share = hidden // npr
    lines = (part * hidden + share * depth) // (nb * 128)
    operands = [grad_a, grad_b, pos, raw, pre, emb, hid, w_out]
    specs = [full(x.shape) for x in operands]
    specs[5] = pl.BlockSpec((rows, part), lambda i, turn: (0, turn[0]))
    return pl.pallas_call(
        functools.partial(backward_kernel, share),
        grid_spec=pltpu.PrefetchScalarGridSpec(
            num_scalar_prefetch=1,
            grid=(1,),
            in_specs=specs,
            out_specs=full((nb, lines, 128)),
            scratch_shapes=[pltpu.VMEM((hidden, depth), f32)],
        ),
        out_shape=jax.ShapeDtypeStruct((nb, lines, 128), f32),
        compiler_params=params("arbitrary"),
        name="backward",
    )(turn, grad_a, grad_b, pos, *[in_hbm(x) for x in operands[3:]])


def unpack_kernel(order, order_b, place, *refs):
    pieces, (g_in, g_out) = refs[:-2], refs[-2:]
    nb = len(order_b)
    npr = len(order)
    tall, wide = g_in.shape[0] // (nb * npr), g_in.shape[1]
    base, short = tall * (wide // 128), g_out.shape[0] // (nb * npr)
    half = pieces[0].shape[0]
    for n, flip in enumerate(order):
        for k, flip_b in enumerate(order_b):
            owner = (place[0] ^ flip) * nb + (place[1] ^ flip_b)
            x = pieces[n // half][n % half, k].astype(f32)
            low = pl.multiple_of(owner * tall, tall)
            for q in range(wide // 128):
                g_in[pl.ds(low, tall), q * 128 : (q + 1) * 128] = x[q * tall : (q + 1) * tall]
            low = pl.multiple_of(owner * short, short)
            g_out[pl.ds(low, short), :] = x[base : base + short]


def unpack(order, order_b, place, pieces, shape_in, shape_out):
    return pl.pallas_call(
        functools.partial(unpack_kernel, order, order_b),
        in_specs=[pl.BlockSpec(memory_space=pltpu.SMEM)] + [WHOLE] * len(pieces),
        out_specs=[WHOLE] * 2,
        out_shape=[jax.ShapeDtypeStruct(shape_in, f32), jax.ShapeDtypeStruct(shape_out, f32)],
        compiler_params=params(),
        name="unpack",
    )(place, *pieces)


def widen_kernel(x, out, narrow, wide, came, went):
    count, rows, _ = narrow.shape
    ins = [
        pltpu.make_async_copy(x.at[pl.ds(k * rows, rows)], narrow.at[k], came.at[k])
        for k in range(count)
    ]
    outs = [
        pltpu.make_async_copy(wide.at[k], out.at[pl.ds(k * rows, rows)], went.at[k])
        for k in range(count)
    ]
    for copy in ins:
        copy.start()
    for k in range(count):
        ins[k].wait()
        wide[k] = narrow[k].astype(f32)
        outs[k].start()
    for copy in outs:
        copy.wait()


def widen(x):
    rows, depth = x.shape
    count = 8
    block = rows // count
    return pl.pallas_call(
        widen_kernel,
        in_specs=[pl.BlockSpec(memory_space=pl.ANY)],
        out_specs=pl.BlockSpec(memory_space=pl.ANY),
        out_shape=jax.ShapeDtypeStruct((rows, depth), f32),
        scratch_shapes=[
            pltpu.VMEM((count, block, depth), bf16),
            pltpu.VMEM((count, block, depth), f32),
            pltpu.SemaphoreType.DMA((count,)),
            pltpu.SemaphoreType.DMA((count,)),
        ],
        compiler_params=params(),
        name="widen",
    )(in_hbm(x))


def stages(size, first=1):
    found, step = ([[1]], 2) if first == 1 else ([], 1)
    while step < size:
        if step * 2 < size:
            found.append([step, step * 2, step * 3])
            step *= 4
        else:
            found.append([step])
            step *= 2
    return found


def body(nb, npr, embeddings, pairing, w_in, w_out, prototypes):
    b = lax.axis_index("batch")
    p = lax.axis_index("proto")
    rows, wide = embeddings.shape
    width, depth = prototypes.shape
    hidden_n = w_in.shape[1]
    own = width // nb

    def flipped(x, axis, size, step):
        return lax.ppermute(x, axis, [(i, i ^ step) for i in range(size)])

    def trade(x, axis, size, steps, queue=(), results=None):
        others = [flipped(x, axis, size, step) for step in steps]
        work = queue.pop(0) if queue else None
        if work:
            operands, _ = lax.optimization_barrier((work[1], x))
            others, found = lax.optimization_barrier((others, work[0](*operands)))
            results.append(found)
        return others

    def summed(x, axis, size, queue=(), results=None):
        rounds = stages(size, 1 if axis == "batch" else 2)
        for n, steps in enumerate(rounds):
            others = trade(x, axis, size, steps, queue, results)
            if n == len(rounds) - 1:
                return [x, *others]
            for other in others:
                x = x + other

    pre, hid, raw, views, views_t, pos = head(embeddings, pairing, w_in, w_out)
    views_all = lax.all_gather(views_t, "batch", axis=0)
    protos_own = lax.dynamic_slice_in_dim(prototypes, b * own, own, 0)
    place = b.astype(jnp.int32).reshape(1)
    turn_p = p.astype(jnp.int32).reshape(1)
    views, protos_own, place, turn_p = lax.optimization_barrier(
        (views, protos_own, place, turn_p)
    )
    expo, col, tot = first_pass(views, prototypes)

    groups = 4
    cols = width // groups
    softs = []
    queue = [
        (functools.partial(view_soft, lead=k * cols, count=cols), (views, prototypes))
        for k in range(groups)
    ]
    scale, row = rowsum(expo, summed(col, "batch", nb, queue, softs))
    rest = len(stages(npr, 2)) - 1
    queue = [None] * rest + queue
    both = sum(summed(jnp.concatenate([row, tot], axis=0), "proto", npr, queue, softs))
    totals, tot = [both[:1]], both[1:]

    def unit_half(protos):
        return unit_transposed(protos, *taken)

    taken = []
    halves = [(unit_half, (prototypes,))] * 2
    col = colsum(expo, totals)[0]
    tot_all = tot[None]
    rounds = stages(nb)
    for n, steps in enumerate(rounds):
        others = [flipped(tot_all, "batch", nb, step) for step in steps]
        if queue:
            parts = trade(col, "batch", nb, steps, queue, softs)
        else:
            parts = trade(col, "batch", nb, steps, halves, taken)
        others, parts = lax.optimization_barrier((others, parts))
        tot_all = jnp.concatenate([tot_all, *others], axis=0)
        if n < len(rounds) - 1:
            for part in parts:
                col = col + part
    scale, row = rowsum(expo, [col, *parts])
    halves = [None] * rest + halves
    col = colsum(expo, summed(row, "proto", npr, halves, taken))[0]
    unit_t = taken[-1]

    col, views_all = lax.optimization_barrier((col, views_all))
    each = nb // groups
    owns = []
    queue = [
        (
            functools.partial(proto_first, lead=k * each, count=each),
            (place, protos_own, views_all, tot_all),
        )
        for k in range(groups)
    ]
    scale, row, code = rowsum_last(expo, summed(col, "batch", nb, queue, owns), unit_t)
    queue = [None] * rest + queue
    total = sum(summed(row, "proto", npr, queue, owns))
    total_all = total[None]
    grads = []
    queue = [(view_grad_part, (code, tot, total, *softs))] + queue
    turn = 1
    for steps in stages(nb):
        others = trade(total_all, "batch", nb, steps, queue, grads if not grads else owns)
        if len(grads) > 1:
            grads = [(grads[0].astype(f32) + grads[1].astype(f32)).astype(bf16)]
            others[0], grads[0] = lax.optimization_barrier((others[0], grads[0]))
        if turn * 2 < npr:
            grads = [grads[0], flipped(grads[0], "proto", npr, turn)]
            turn *= 2
        total_all = jnp.concatenate([total_all, *others], axis=0)

    while turn * 2 < npr:
        if len(grads) > 1:
            grads = [(grads[0].astype(f32) + grads[1].astype(f32)).astype(bf16)]
        grads = [grads[0], flipped(grads[0], "proto", npr, turn)]
        turn *= 2
    if len(grads) > 1:
        grads = [(grads[0].astype(f32) + grads[1].astype(f32)).astype(bf16)]
    expos, parts = [x for x, _ in owns], [x for _, x in owns]
    queue = [(proto_last, (place, expos, parts, scale, protos_own, views_all, total_all))]
    found = []
    grads = [grads[0], *trade(grads[0], "proto", npr, [npr // 2], queue, found)]
    grad_proto = lax.all_gather(found[0], "batch", axis=0, tiled=True)
    both = backward(nb, npr, turn_p, *grads, pos, raw, pre, embeddings, hid, w_out)
    for steps in stages(nb):
        count = len(steps) + 1
        share = both.shape[0] // count
        mine = (b // steps[0]) % 2
        if count == 4:
            mine = mine * 2 + (b // steps[1]) % 2
        kept = lax.dynamic_slice_in_dim(both, mine * share, share, 0)
        for flip, step in zip([1] if count == 2 else [2, 1, 3], steps):
            away = lax.dynamic_slice_in_dim(both, (mine ^ flip) * share, share, 0)
            kept = kept + flipped(away.astype(bf16), "batch", nb, step).astype(f32)
        both = kept
    piece = both.astype(bf16)
    order_b = [0]
    for steps in reversed(stages(nb)):
        piece = jnp.concatenate(
            [piece, *[flipped(piece, "batch", nb, step) for step in steps]], axis=0
        )
        order_b = order_b + [i ^ step for step in steps for i in order_b]
    piece = piece[None]
    order = [0]
    step = npr // 2
    while step > 1:
        piece = jnp.concatenate([piece, flipped(piece, "proto", npr, step)], axis=0)
        order = order + [i ^ step for i in order]
        step //= 2
    pieces = [piece, flipped(piece, "proto", npr, 1)]
    order = order + [i ^ 1 for i in order]
    places = jnp.stack([p, b]).astype(jnp.int32)
    grad_in, grad_out = unpack(
        order, order_b, places, pieces, (wide, hidden_n), (hidden_n, depth)
    )
    return (grad_in, grad_out, widen(grad_proto))


def solution(mesh):
    return jax.shard_map(
        functools.partial(body, mesh.shape["batch"], mesh.shape["proto"]),
        mesh=mesh,
        in_specs=(P("batch", None), P("batch"), P(), P(), P("proto", None)),
        out_specs=(P(), P(), P("proto", None)),
        check_vma=False,
    )
```

```python
import functools
import math

import jax
import jax.numpy as jnp
from jax import lax
from jax.experimental import pallas as pl
from jax.experimental.pallas import tpu as pltpu
from jax.sharding import PartitionSpec as P

ITERS = 3
norm_eps = 1e-06
code_temp = 0.05
pred_temp = 0.1
loss_scale = 64.0
GRAD_SCALE = loss_scale / pred_temp
EXP2_SCALE = math.log2(math.e) / pred_temp
GELU_K = math.sqrt(2.0 / math.pi)
GELU_A = 0.044715

f32 = jnp.float32
bf16 = jnp.bfloat16
NN = (((1,), (0,)), ((), ()))
NT = (((1,), (1,)), ((), ()))
TN = (((0,), (0,)), ((), ()))
VMEM_LIMIT = 12 * 1024 * 1024


def dot(a, b, dims=NN):
    return lax.dot_general(a, b, dims, preferred_element_type=f32)


SMALL = pl.CostEstimate(flops=1000, bytes_accessed=1000, transcendentals=0)


def params(*semantics, limit=VMEM_LIMIT):
    return pltpu.CompilerParams(dimension_semantics=semantics or None, vmem_limit_bytes=limit)


def to_column(vec):
    n = vec.shape[1]
    return jnp.broadcast_to(vec, (8, n)).T[:, :1]


def swap_lanes(x):
    half = x.shape[1] // 2
    return jnp.concatenate([x[:, half:], x[:, :half]], axis=1)


def swap_rows(x):
    half = x.shape[0] // 2
    return jnp.concatenate([x[half:], x[:half]], axis=0)


def in_vmem(x):
    return pltpu.with_memory_space_constraint(x, pltpu.VMEM)


def in_hbm(x):
    return pltpu.with_memory_space_constraint(x, pltpu.HBM)


def full(shape):
    return pl.BlockSpec(shape, lambda *_: (0,) * len(shape))


def head_kernel(emb, pairing, w_in, w_out, pre, hid, raw, views, views_t, pos, scratch):
    step = pl.program_id(0)
    rows = emb.shape[0]
    pre_act = dot(emb[...], w_in[...])
    pre[...] = pre_act
    t = jnp.tanh(GELU_K * (pre_act + GELU_A * (pre_act * pre_act * pre_act)))
    hidden = (0.5 * pre_act * (1.0 + t)).astype(bf16)
    hid[...] = hidden
    raw_out = dot(hidden, w_out[...])
    raw[...] = raw_out
    inv = lax.rsqrt(jnp.sum(raw_out * raw_out, axis=1, keepdims=True) + norm_eps)
    scratch[pl.ds(pl.multiple_of(step * rows, rows), rows), :] = (raw_out * inv).astype(bf16)

    @pl.when(step == pl.num_programs(0) - 1)
    def _():
        mate = pairing[...]
        n = mate.shape[1]
        lane = lax.broadcasted_iota(jnp.int32, (1, n), 1)
        first = lane < mate
        low = jnp.minimum(lane, mate)
        sub = lax.broadcasted_iota(jnp.int32, (n, n), 0)
        before = jnp.where(sub < low, 1.0, 0.0).astype(bf16)
        first8 = jnp.broadcast_to(jnp.where(first, 1.0, 0.0), (8, n)).astype(bf16)
        rank = dot(first8, before)[:1].astype(jnp.int32)
        place = jnp.where(first, rank, rank + n // 2)
        pos[...] = place
        move = jnp.where(sub == place, 1.0, 0.0).astype(bf16)
        ordered = dot(move, scratch[...])
        views[...] = ordered.astype(bf16)
        views_t[...] = ordered.T.astype(bf16)


def head(embeddings, pairing, w_in, w_out):
    rows, wide = embeddings.shape
    hidden = w_in.shape[1]
    depth = w_out.shape[1]
    steps = 4
    block = rows // steps
    return pl.pallas_call(
        head_kernel,
        grid=(steps,),
        in_specs=[
            pl.BlockSpec((block, wide), lambda i: (i, 0)),
            full((1, rows)),
            full((wide, hidden)),
            full((hidden, depth)),
        ],
        out_specs=[
            pl.BlockSpec((block, hidden), lambda i: (i, 0)),
            pl.BlockSpec((block, hidden), lambda i: (i, 0)),
            pl.BlockSpec((block, depth), lambda i: (i, 0)),
            full((rows, depth)),
            full((depth, rows)),
            full((1, rows)),
        ],
        out_shape=[
            pltpu.HBM((rows, hidden), f32),
            pltpu.HBM((rows, hidden), bf16),
            pltpu.HBM((rows, depth), f32),
            jax.ShapeDtypeStruct((rows, depth), bf16),
            jax.ShapeDtypeStruct((depth, rows), bf16),
            jax.ShapeDtypeStruct((1, rows), jnp.int32),
        ],
        scratch_shapes=[pltpu.VMEM((rows, depth), bf16)],
        compiler_params=params("arbitrary"),
        name="head",
    )(in_hbm(embeddings), in_hbm(pairing.reshape(1, rows)), in_hbm(w_in), in_hbm(w_out))


def unit_of(protos):
    proto_f = protos.astype(f32)
    inv = lax.rsqrt(jnp.sum(proto_f * proto_f, axis=1, keepdims=True) + norm_eps)
    return proto_f, inv, proto_f * inv


WHOLE = pl.BlockSpec(memory_space=pltpu.VMEM)


def scaled_pair(x, axis):
    wide = x.astype(f32) * EXP2_SCALE
    hi = wide.astype(bf16)
    lo = (wide - hi.astype(f32)).astype(bf16)
    return jnp.concatenate([hi, lo], axis=axis)


def first_kernel(block, chunk, tile, views, protos, expo, col, tot, pair, stage, tot_acc):
    rows, depth = views.shape
    width = protos.shape[0]
    tot_acc[...] = jnp.zeros_like(tot_acc)
    pair[...] = scaled_pair(views[...], 1)

    def one(j, carry):
        here = pl.ds(pl.multiple_of(j * block, block), block)
        _, _, unit = unit_of(protos[here, :])
        unit16 = unit.astype(bf16)
        twice = jnp.concatenate([unit16, unit16], axis=1)
        running = jnp.zeros((8, block), f32)
        for c in range(rows // chunk):
            stage[c % 2] = dot(pair[c * chunk : (c + 1) * chunk, :], twice, NT)
            for start in range(0, chunk, tile):
                part = slice(c * chunk + start, c * chunk + start + tile)
                soft = jnp.exp2(stage[c % 2, start : start + tile, :])
                hard = soft * soft
                expo[part, here] = hard.astype(bf16)
                lanes = soft[:, :128]
                for k in range(1, block // 128):
                    lanes = lanes + soft[:, k * 128 : (k + 1) * 128]
                tot_acc[part, :] += lanes
                for k in range(0, tile, 8):
                    running = running + hard[k : k + 8]
        col[:, here] = jnp.sum(running, axis=0, keepdims=True)
        return carry

    lax.fori_loop(0, width // block, one, 0)
    tot[...] = jnp.sum(tot_acc[...].T, axis=0, keepdims=True)


def first_pass(views, protos):
    rows, depth = views.shape
    width = protos.shape[0]
    block = min(512, width)
    chunk = min(256, rows)
    tile = min(32, chunk)
    return pl.pallas_call(
        functools.partial(first_kernel, block, chunk, tile),
        in_specs=[WHOLE] * 2,
        out_specs=[WHOLE] * 3,
        out_shape=[
            pltpu.VMEM((rows, width), bf16),
            jax.ShapeDtypeStruct((1, width), f32),
            jax.ShapeDtypeStruct((1, rows), f32),
        ],
        scratch_shapes=[
            pltpu.VMEM((rows, 2 * depth), bf16),
            pltpu.VMEM((2, chunk, block), f32),
            pltpu.VMEM((rows, 128), f32),
        ],
        compiler_params=params(),
        cost_estimate=SMALL,
        name="first_pass",
    )(views, protos)


def sum_parts(parts, width):
    if len(parts[0].shape) == 3:
        parts = [parts[0].at[k] for k in range(parts[0].shape[0])]
    total = parts[0][:, :width]
    for other in parts[1:]:
        total = total + other[:, :width]
    return total


def add_fours(terms):
    total = None
    for k in range(0, len(terms), 4):
        four = terms[k : k + 4]
        while len(four) > 1:
            four = [x + y for x, y in zip(four[::2], four[1::2])]
        part = four[0].astype(f32)
        total = part if total is None else total + part
    return total


def rowsum_tile(expo, here, spread, tall, width):
    terms = []
    total = None
    for k in range(width // 128):
        lanes = slice(k * 128, (k + 1) * 128)
        weight = jnp.concatenate([spread[:, lanes]] * (tall // 16), axis=0)
        terms.append(expo[here, lanes] * weight)
        if len(terms) == 4 or k == width // 128 - 1:
            part = add_fours(terms)
            total = part if total is None else total + part
            terms = []
    return total


def rowsum_kernel(count, expo, *refs):
    parts = refs[:count]
    scale, out, spread, acc = refs[count:]
    rows, width = expo.shape
    inverse = 1.0 / sum_parts(parts, width)
    scale[...] = inverse
    spread[...] = jnp.broadcast_to(inverse, spread.shape).astype(bf16)
    tall = 64

    def one(i, carry):
        here = pl.ds(pl.multiple_of(i * tall, tall), tall)
        acc[here, :] = rowsum_tile(expo, here, spread, tall, width)
        return carry

    lax.fori_loop(0, rows // tall, one, 0)
    out[...] = jnp.sum(acc[...].T, axis=0, keepdims=True)


def rowsum(expo, parts):
    rows, width = expo.shape
    return pl.pallas_call(
        functools.partial(rowsum_kernel, len(parts)),
        in_specs=[WHOLE] * (1 + len(parts)),
        out_specs=[WHOLE] * 2,
        out_shape=[
            jax.ShapeDtypeStruct((1, width), f32),
            jax.ShapeDtypeStruct((1, rows), f32),
        ],
        scratch_shapes=[pltpu.VMEM((16, width), bf16), pltpu.VMEM((rows, 128), f32)],
        compiler_params=params(),
        cost_estimate=SMALL,
        name="rowsum",
    )(in_vmem(expo), *parts)


def split_rows(vec):
    hi = vec.astype(bf16).astype(f32)
    n = vec.shape[1]
    row = lax.broadcasted_iota(jnp.int32, (8, n), 0)
    hi8 = jnp.broadcast_to(hi, (8, n))
    lo8 = jnp.broadcast_to(vec - hi, (8, n))
    return jnp.where(row == 0, hi8, jnp.where(row == 1, lo8, 0.0))


def rowsum_last_kernel(pieces, count, *refs):
    expos = refs[:pieces]
    parts = refs[pieces : pieces + count]
    unit_t, scale, out, code, acc = refs[pieces + count :]
    step = pl.program_id(0)
    depth, block = unit_t.shape
    deep = expos[0].shape[1]
    inverse = 1.0 / sum_parts(parts, block)
    scale[...] = inverse

    @pl.when(step == 0)
    def _():
        acc[...] = jnp.zeros_like(acc)

    for k in range(pieces):
        here = slice(k * deep, (k + 1) * deep)
        scaled = unit_t[:, here].astype(f32) * inverse[:, here]
        pad = jnp.zeros((depth - 8, deep), f32)
        weights = jnp.concatenate([scaled, split_rows(inverse[:, here]), pad], axis=0)
        acc[...] += dot(expos[k][...], weights.astype(bf16), NT)

    @pl.when(step == pl.num_programs(0) - 1)
    def _():
        sums = acc[:, depth:].T
        out[...] = sums[0:1] + sums[1:2]
        code[...] = acc[:, :depth]


def rowsum_last(expo, parts, unit_t):
    rows, width = expo.shape
    depth = unit_t.shape[0]
    block = min(2048, width)
    pieces = 4
    deep = block // pieces
    vec = pl.BlockSpec((1, block), lambda j: (0, j))
    return pl.pallas_call(
        functools.partial(rowsum_last_kernel, pieces, len(parts)),
        grid=(width // block,),
        in_specs=[
            pl.BlockSpec((rows, deep), lambda j, k=k: (0, j * pieces + k)) for k in range(pieces)
        ]
        + [vec] * len(parts)
        + [pl.BlockSpec((depth, block), lambda j: (0, j))],
        out_specs=[vec, full((1, rows)), full((rows, depth))],
        out_shape=[
            jax.ShapeDtypeStruct((1, width), f32),
            jax.ShapeDtypeStruct((1, rows), f32),
            jax.ShapeDtypeStruct((rows, depth), f32),
        ],
        scratch_shapes=[pltpu.VMEM((rows, 2 * depth), f32)],
        compiler_params=params("arbitrary", limit=VMEM_LIMIT + 4 * 1024 * 1024),
        cost_estimate=SMALL,
        name="rowsum_last",
    )(*[in_hbm(expo)] * pieces, *parts, in_hbm(unit_t))


def unit_t_kernel(block, lead, protos, *refs):
    out = refs[-1]

    def one(j, carry):
        here = pl.ds(pl.multiple_of(lead + j * block, block), block)
        _, _, unit = unit_of(protos[here, :])
        out[:, here] = unit.astype(bf16).astype(f32).T.astype(bf16)
        return carry

    lax.fori_loop(0, protos.shape[0] // 2 // block, one, 0)


def unit_transposed(protos, *before):
    width, depth = protos.shape
    lead = width // 2 if before else 0
    return pl.pallas_call(
        functools.partial(unit_t_kernel, min(512, width // 2), lead),
        in_specs=[WHOLE] * (1 + len(before)),
        out_specs=WHOLE,
        out_shape=jax.ShapeDtypeStruct((depth, width), bf16),
        input_output_aliases={1: 0} if before else {},
        compiler_params=params(),
        cost_estimate=SMALL,
        name="unit_t",
    )(protos, *before)


def colsum_kernel(count, expo, *refs):
    parts = refs[:count]
    rest = refs[count:]
    out, spread = rest[-2:]
    rows, width = expo.shape
    inverse = 1.0 / sum_parts(parts, rows)
    spread[...] = jnp.broadcast_to(inverse, (128, rows)).T.astype(bf16)
    block = min(512, width)

    def one(j, carry):
        here = pl.ds(pl.multiple_of(j * block, block), block)
        running = jnp.zeros((16, block), f32)
        for i in range(0, rows // 16, 4):
            terms = []
            for k in range(i, min(i + 4, rows // 16)):
                part = slice(k * 16, (k + 1) * 16)
                weight = jnp.concatenate([spread[part, :]] * (block // 128), axis=1)
                terms.append(expo[part, here] * weight)
            running = running + add_fours(terms)
        total = jnp.sum(running, axis=0, keepdims=True)
        for k in range(out.shape[0]):
            out[k, :, here] = total
        return carry

    lax.fori_loop(0, width // block, one, 0)
    if len(rest) > 2:
        for k in range(out.shape[0]):
            out[k, :, width:] = rest[0][...]


def colsum(expo, parts, copies=1, behind=()):
    rows, width = expo.shape
    long = width + sum(x.shape[1] for x in behind)
    return pl.pallas_call(
        functools.partial(colsum_kernel, len(parts)),
        in_specs=[WHOLE] * (1 + len(parts) + len(behind)),
        out_specs=WHOLE,
        out_shape=jax.ShapeDtypeStruct((copies, 1, long), f32),
        scratch_shapes=[pltpu.VMEM((rows, 128), bf16)],
        compiler_params=params(),
        cost_estimate=SMALL,
        name="colsum",
    )(in_vmem(expo), *parts, *behind)


def proto_first_kernel(chunk, tile, lead, place, protos, views, totals, expo, grad, *scratch):
    weights, twice, pair, stage, soft16, acc = scratch
    count = expo.shape[1] // views.shape[2]
    _, depth, rows = views.shape
    width = protos.shape[0]
    _, _, unit = unit_of(protos[...])
    pair[...] = scaled_pair(unit.astype(bf16), 1)
    for n in range(count):
        k = lead + n
        weights[...] = (views[k].astype(f32) * (GRAD_SCALE / totals[place[0] ^ k])).astype(bf16)
        twice[:depth, :] = views[k]
        twice[depth:, :] = views[k]
        for c in range(width // chunk):
            stage[c % 2] = dot(pair[c * chunk : (c + 1) * chunk, :], twice[...])
            for start in range(0, chunk, tile):
                part = slice(c * chunk + start, c * chunk + start + tile)
                soft = jnp.exp2(stage[c % 2, start : start + tile, :])
                soft16[part, :] = soft.astype(bf16)
                expo[part, n * rows : (n + 1) * rows] = (soft * soft).astype(bf16)
        found = dot(soft16[...], weights[...], NT)
        if n == 0:
            acc[...] = found
        else:
            acc[...] += found
    grad[...] = acc[...]


def proto_first(place, protos, views, totals, lead, count):
    width, depth = protos.shape
    rows = views.shape[2]
    chunk = min(256, width)
    tile = min(16, chunk)
    return pl.pallas_call(
        functools.partial(proto_first_kernel, chunk, tile, lead),
        in_specs=[pl.BlockSpec(memory_space=pltpu.SMEM)] + [WHOLE] * 3,
        out_specs=[WHOLE] * 2,
        out_shape=[
            pltpu.VMEM((width, count * rows), bf16),
            jax.ShapeDtypeStruct((width, depth), f32),
        ],
        scratch_shapes=[
            pltpu.VMEM((depth, rows), bf16),
            pltpu.VMEM((2 * depth, rows), bf16),
            pltpu.VMEM((width, 2 * depth), bf16),
            pltpu.VMEM((2, chunk, rows), f32),
            pltpu.VMEM((width, rows), bf16),
            pltpu.VMEM((width, depth), f32),
        ],
        compiler_params=params(),
        cost_estimate=SMALL,
        name="proto_first",
    )(place, protos, views, totals)


def proto_last_kernel(groups, place, *refs):
    expos, grads = refs[:groups], refs[groups : 2 * groups]
    scale, protos, views, totals, out, weights, acc = refs[2 * groups :]
    count, depth, rows = views.shape
    each = count // groups
    for k in range(count):
        mates = swap_lanes(views[k])
        weights[...] = (mates.astype(f32) * (GRAD_SCALE / totals[place[0] ^ k])).astype(bf16)
        found = dot(expos[k // each][:, (k % each) * rows : (k % each + 1) * rows], weights[...], NT)
        if k == 0:
            acc[...] = found
        else:
            acc[...] += found
    width = protos.shape[0]
    there = pl.ds(pl.multiple_of(place[0] * width, width), width)
    unit_grad = grads[0][...]
    for other in grads[1:]:
        unit_grad = unit_grad + other[...]
    unit_grad = unit_grad - to_column(scale[:, there]) * acc[...]
    proto_f, inv, _ = unit_of(protos[...])
    inner = jnp.sum(proto_f * unit_grad, axis=1, keepdims=True)
    out[...] = (inv * unit_grad - proto_f * (inv * inv * inv) * inner).astype(bf16)


def proto_last(place, expos, grads, scale, protos, views, totals):
    width, depth = protos.shape
    rows = views.shape[2]
    groups = len(expos)
    return pl.pallas_call(
        functools.partial(proto_last_kernel, groups),
        in_specs=[pl.BlockSpec(memory_space=pltpu.SMEM)] + [WHOLE] * (2 * groups + 4),
        out_specs=WHOLE,
        out_shape=jax.ShapeDtypeStruct((width, depth), bf16),
        scratch_shapes=[pltpu.VMEM((depth, rows), bf16), pltpu.VMEM((width, depth), f32)],
        compiler_params=params(),
        name="proto_last",
    )(place, *[in_vmem(x) for x in expos], *grads, scale, protos, views, totals)


def view_soft_kernel(block, tile, lead, views, protos, out, pair, stage, soft16):
    rows, depth = views.shape
    pair[...] = scaled_pair(views[...], 1)
    out[...] = jnp.zeros_like(out)
    chunk = stage.shape[1]

    def one(j, carry):
        here = pl.ds(pl.multiple_of(lead + j * block, block), block)
        _, _, unit = unit_of(protos[here, :])
        unit16 = unit.astype(bf16)
        twice = jnp.concatenate([unit16, unit16], axis=1)
        for c in range(rows // chunk):
            stage[c % 2] = dot(pair[c * chunk : (c + 1) * chunk, :], twice, NT)
            for start in range(0, chunk, tile):
                part = slice(c * chunk + start, c * chunk + start + tile)
                soft16[part, :] = jnp.exp2(stage[c % 2, start : start + tile, :]).astype(bf16)
        out[...] += dot(soft16[...], unit16)
        return carry

    return one


def view_soft_body(block, tile, lead, count, *refs):
    lax.fori_loop(0, count // block, view_soft_kernel(block, tile, lead, *refs), 0)


def view_soft(views, protos, lead, count):
    rows, depth = views.shape
    block = min(512, count)
    chunk = min(256, rows)
    return pl.pallas_call(
        functools.partial(view_soft_body, block, min(32, chunk), lead, count),
        in_specs=[WHOLE] * 2,
        out_specs=WHOLE,
        out_shape=jax.ShapeDtypeStruct((rows, depth), f32),
        scratch_shapes=[
            pltpu.VMEM((rows, 2 * depth), bf16),
            pltpu.VMEM((2, chunk, block), f32),
            pltpu.VMEM((rows, block), bf16),
        ],
        compiler_params=params(),
        cost_estimate=SMALL,
        name="view_soft",
    )(views, protos)


def view_grad_kernel(code, tot, total, *refs):
    softs, out = refs[:-1], refs[-1]
    soft = softs[0][...]
    for other in softs[1:]:
        soft = soft + other[...]
    soft = soft * to_column(GRAD_SCALE / tot[...])
    hard = swap_rows(code[...] * to_column(GRAD_SCALE / total[...]))
    out[...] = (soft - hard).astype(out.dtype)


def view_grad_part(code, tot, total, *softs):
    operands = [code, tot, total, *softs]
    return pl.pallas_call(
        view_grad_kernel,
        grid=(1,),
        in_specs=[full(x.shape) for x in operands],
        out_specs=full(code.shape),
        out_shape=jax.ShapeDtypeStruct(code.shape, bf16),
        compiler_params=params("arbitrary"),
        cost_estimate=SMALL,
        name="view_grad",
    )(code, tot, total, *[in_hbm(x) for x in softs])


def backward_kernel(share, turn, grad_a, grad_b, pos, raw, pre, emb, hid, w_out, out, g_all):
    total = grad_a[...].astype(f32) + grad_b[...].astype(f32)
    n, depth = raw.shape
    place = jnp.broadcast_to(pos[...].astype(f32), (8, n)).T[:, :1].astype(jnp.int32)
    lane = lax.broadcasted_iota(jnp.int32, (n, n), 1)
    move = jnp.where(lane == place, 1.0, 0.0).astype(bf16)
    hi = total.astype(bf16)
    lo = (total - hi.astype(f32)).astype(bf16)
    moved = dot(move, jnp.concatenate([hi, lo], axis=1))
    grad = moved[:, :depth] + moved[:, depth:]
    raw_out = raw[...]
    inv = lax.rsqrt(jnp.sum(raw_out * raw_out, axis=1, keepdims=True) + norm_eps)
    inner = jnp.sum(raw_out * grad, axis=1, keepdims=True)
    d_raw = (inv * grad - raw_out * (inv * inv * inv) * inner).astype(bf16)
    g_all[...] = dot(hid[...], d_raw, TN)
    d_hidden = dot(d_raw, w_out[...], NT)
    v = pre[...]
    t = jnp.tanh(GELU_K * (v + GELU_A * (v * v * v)))
    slope = 0.5 * (1.0 + t) + (0.5 * GELU_K) * v * (1.0 - t * t) * (1.0 + (3.0 * GELU_A) * (v * v))
    d_pre = (slope * d_hidden).astype(bf16)
    g_in = dot(emb[...], d_pre, TN)
    count = out.shape[0]
    tall, wide = g_in.shape[0] // count, g_in.shape[1]
    base, short = tall * (wide // 128), share // count
    for k in range(count):
        n = mirrored(k, count)
        for q in range(wide // 128):
            out[n, q * tall : (q + 1) * tall, :] = g_in[
                k * tall : (k + 1) * tall, q * 128 : (q + 1) * 128
            ]
        low = pl.multiple_of(turn[0] * share + k * short, short)
        out[n, base : base + short, :] = g_all[pl.ds(low, short), :]


def mirrored(k, count):
    found = 0
    while count > 1:
        found = found * 2 + k % 2
        k //= 2
        count //= 2
    return found


def backward(nb, npr, turn, grad_a, grad_b, pos, raw, pre, emb, hid, w_out):
    rows, wide = emb.shape
    hidden, depth = w_out.shape
    part = wide // npr
    share = hidden // npr
    lines = (part * hidden + share * depth) // (nb * 128)
    operands = [grad_a, grad_b, pos, raw, pre, emb, hid, w_out]
    specs = [full(x.shape) for x in operands]
    specs[5] = pl.BlockSpec((rows, part), lambda i, turn: (0, turn[0]))
    return pl.pallas_call(
        functools.partial(backward_kernel, share),
        grid_spec=pltpu.PrefetchScalarGridSpec(
            num_scalar_prefetch=1,
            grid=(1,),
            in_specs=specs,
            out_specs=full((nb, lines, 128)),
            scratch_shapes=[pltpu.VMEM((hidden, depth), f32)],
        ),
        out_shape=jax.ShapeDtypeStruct((nb, lines, 128), f32),
        compiler_params=params("arbitrary"),
        name="backward",
    )(turn, grad_a, grad_b, pos, *[in_hbm(x) for x in operands[3:]])


def unpack_kernel(order, order_b, place, *refs):
    pieces, (g_in, g_out) = refs[:-2], refs[-2:]
    nb = len(order_b)
    npr = len(order)
    tall, wide = g_in.shape[0] // (nb * npr), g_in.shape[1]
    base, short = tall * (wide // 128), g_out.shape[0] // (nb * npr)
    half = pieces[0].shape[0]
    for n, flip in enumerate(order):
        for k, flip_b in enumerate(order_b):
            owner = (place[0] ^ flip) * nb + (place[1] ^ flip_b)
            x = pieces[n // half][n % half, k].astype(f32)
            low = pl.multiple_of(owner * tall, tall)
            for q in range(wide // 128):
                g_in[pl.ds(low, tall), q * 128 : (q + 1) * 128] = x[q * tall : (q + 1) * tall]
            low = pl.multiple_of(owner * short, short)
            g_out[pl.ds(low, short), :] = x[base : base + short]


def unpack(order, order_b, place, pieces, shape_in, shape_out):
    return pl.pallas_call(
        functools.partial(unpack_kernel, order, order_b),
        in_specs=[pl.BlockSpec(memory_space=pltpu.SMEM)] + [WHOLE] * len(pieces),
        out_specs=[WHOLE] * 2,
        out_shape=[jax.ShapeDtypeStruct(shape_in, f32), jax.ShapeDtypeStruct(shape_out, f32)],
        compiler_params=params(),
        name="unpack",
    )(place, *pieces)


def widen_kernel(x, out, narrow, wide, came, went):
    count, rows, _ = narrow.shape
    ins = [
        pltpu.make_async_copy(x.at[pl.ds(k * rows, rows)], narrow.at[k], came.at[k])
        for k in range(count)
    ]
    outs = [
        pltpu.make_async_copy(wide.at[k], out.at[pl.ds(k * rows, rows)], went.at[k])
        for k in range(count)
    ]
    for copy in ins:
        copy.start()
    for k in range(count):
        ins[k].wait()
        wide[k] = narrow[k].astype(f32)
        outs[k].start()
    for copy in outs:
        copy.wait()


def widen(x):
    rows, depth = x.shape
    count = 8
    block = rows // count
    return pl.pallas_call(
        widen_kernel,
        in_specs=[pl.BlockSpec(memory_space=pl.ANY)],
        out_specs=pl.BlockSpec(memory_space=pl.ANY),
        out_shape=jax.ShapeDtypeStruct((rows, depth), f32),
        scratch_shapes=[
            pltpu.VMEM((count, block, depth), bf16),
            pltpu.VMEM((count, block, depth), f32),
            pltpu.SemaphoreType.DMA((count,)),
            pltpu.SemaphoreType.DMA((count,)),
        ],
        compiler_params=params(),
        name="widen",
    )(in_hbm(x))


def stages(size, first=1):
    found, step = ([[1]], 2) if first == 1 else ([], 1)
    while step < size:
        if step * 2 < size:
            found.append([step, step * 2, step * 3])
            step *= 4
        else:
            found.append([step])
            step *= 2
    return found


def body(nb, npr, embeddings, pairing, w_in, w_out, prototypes):
    b = lax.axis_index("batch")
    p = lax.axis_index("proto")
    rows, wide = embeddings.shape
    width, depth = prototypes.shape
    hidden_n = w_in.shape[1]
    own = width // nb

    def flipped(x, axis, size, step):
        return lax.ppermute(x, axis, [(i, i ^ step) for i in range(size)])

    def trade(x, axis, size, steps, queue=(), results=None):
        others = [flipped(x, axis, size, step) for step in steps]
        work = queue.pop(0) if queue else None
        if work:
            operands, _ = lax.optimization_barrier((work[1], x))
            others, found = lax.optimization_barrier((others, work[0](*operands)))
            results.append(found)
        return others

    def summed(x, axis, size, queue=(), results=None):
        rounds = stages(size, 1 if axis == "batch" else 2)
        for n, steps in enumerate(rounds):
            others = trade(x, axis, size, steps, queue, results)
            if n == len(rounds) - 1:
                return [x, *others]
            for other in others:
                x = x + other

    pre, hid, raw, views, views_t, pos = head(embeddings, pairing, w_in, w_out)
    views_all = lax.all_gather(views_t, "batch", axis=0)
    protos_own = lax.dynamic_slice_in_dim(prototypes, b * own, own, 0)
    place = b.astype(jnp.int32).reshape(1)
    turn_p = p.astype(jnp.int32).reshape(1)
    views, protos_own, place, turn_p = lax.optimization_barrier(
        (views, protos_own, place, turn_p)
    )
    expo, col, tot = first_pass(views, prototypes)

    groups = 4
    cols = width // groups
    softs = []
    queue = [
        (functools.partial(view_soft, lead=k * cols, count=cols), (views, prototypes))
        for k in range(groups)
    ]
    scale, row = rowsum(expo, summed(col, "batch", nb, queue, softs))
    rest = len(stages(npr, 2)) - 1
    queue = [None] * rest + queue
    both = sum(summed(jnp.concatenate([row, tot], axis=0), "proto", npr, queue, softs))
    totals, tot = [both[:1]], both[1:]

    def unit_half(protos):
        return unit_transposed(protos, *taken)

    taken = []
    halves = [(unit_half, (prototypes,))] * 2
    col = colsum(expo, totals)[0]
    tot_all = tot[None]
    rounds = stages(nb)
    for n, steps in enumerate(rounds):
        others = [flipped(tot_all, "batch", nb, step) for step in steps]
        parts = trade(col, "batch", nb, steps, halves, taken)
        others, parts = lax.optimization_barrier((others, parts))
        tot_all = jnp.concatenate([tot_all, *others], axis=0)
        if n < len(rounds) - 1:
            for part in parts:
                col = col + part
    scale, row = rowsum(expo, [col, *parts])
    queue = [None] * rest + queue
    col = colsum(expo, summed(row, "proto", npr, queue, softs))[0]
    for left, results in ((halves, taken), (queue, softs)):
        results.extend(work[0](*work[1]) for work in left if work)
    unit_t = taken[-1]

    col, views_all = lax.optimization_barrier((col, views_all))
    each = nb // groups
    owns = []
    queue = [
        (
            functools.partial(proto_first, lead=k * each, count=each),
            (place, protos_own, views_all, tot_all),
        )
        for k in range(groups)
    ]
    scale, row, code = rowsum_last(expo, summed(col, "batch", nb, queue, owns), unit_t)
    queue = [None] * rest + queue
    total = sum(summed(row, "proto", npr, queue, owns))
    total_all = total[None]
    grads = []
    queue = [(view_grad_part, (code, tot, total, *softs))] + queue
    turn = 1
    for steps in stages(nb):
        others = trade(total_all, "batch", nb, steps, queue, grads if not grads else owns)
        if len(grads) > 1:
            grads = [(grads[0].astype(f32) + grads[1].astype(f32)).astype(bf16)]
            others[0], grads[0] = lax.optimization_barrier((others[0], grads[0]))
        if turn * 2 < npr:
            turn *= 2
            grads = [grads[0], flipped(grads[0], "proto", npr, npr // turn)]
        total_all = jnp.concatenate([total_all, *others], axis=0)

    while turn * 2 < npr:
        if len(grads) > 1:
            grads = [(grads[0].astype(f32) + grads[1].astype(f32)).astype(bf16)]
        turn *= 2
        grads = [grads[0], flipped(grads[0], "proto", npr, npr // turn)]
    if len(grads) > 1:
        grads = [(grads[0].astype(f32) + grads[1].astype(f32)).astype(bf16)]
    expos, parts = [x for x, _ in owns], [x for _, x in owns]
    queue = [(proto_last, (place, expos, parts, scale, protos_own, views_all, total_all))]
    found = []
    grads = [grads[0], *trade(grads[0], "proto", npr, [1], queue, found)]
    grad_proto = lax.all_gather(found[0], "batch", axis=0, tiled=True)
    both = backward(nb, npr, turn_p, *grads, pos, raw, pre, embeddings, hid, w_out)
    for steps in stages(nb):
        count = len(steps) + 1
        share = both.shape[0] // count
        mine = (b // steps[0]) % 2
        if count == 4:
            mine = mine * 2 + (b // steps[1]) % 2
        kept = lax.dynamic_slice_in_dim(both, mine * share, share, 0)
        for flip, step in zip([1] if count == 2 else [2, 1, 3], steps):
            away = lax.dynamic_slice_in_dim(both, (mine ^ flip) * share, share, 0)
            kept = kept + flipped(away.astype(bf16), "batch", nb, step).astype(f32)
        both = kept
    piece = both.astype(bf16)
    order_b = [0]
    for steps in reversed(stages(nb)):
        piece = jnp.concatenate(
            [piece, *[flipped(piece, "batch", nb, step) for step in steps]], axis=0
        )
        order_b = order_b + [i ^ step for step in steps for i in order_b]
    piece = piece[None]
    order = [0]
    step = npr // 2
    while step > 1:
        piece = jnp.concatenate([piece, flipped(piece, "proto", npr, step)], axis=0)
        order = order + [i ^ step for i in order]
        step //= 2
    pieces = [piece, flipped(piece, "proto", npr, 1)]
    order = order + [i ^ 1 for i in order]
    places = jnp.stack([p, b]).astype(jnp.int32)
    grad_in, grad_out = unpack(
        order, order_b, places, pieces, (wide, hidden_n), (hidden_n, depth)
    )
    return (grad_in, grad_out, widen(grad_proto))


def solution(mesh):
    return jax.shard_map(
        functools.partial(body, mesh.shape["batch"], mesh.shape["proto"]),
        mesh=mesh,
        in_specs=(P("batch", None), P("batch"), P(), P(), P("proto", None)),
        out_specs=(P(), P(), P("proto", None)),
        check_vma=False,
    )
```

```python
import functools
import math

import jax
import jax.numpy as jnp
from jax import lax
from jax.experimental import pallas as pl
from jax.experimental.pallas import tpu as pltpu
from jax.sharding import PartitionSpec as P

ITERS = 3
norm_eps = 1e-06
code_temp = 0.05
pred_temp = 0.1
loss_scale = 64.0
GRAD_SCALE = loss_scale / pred_temp
EXP2_SCALE = math.log2(math.e) / pred_temp
GELU_K = math.sqrt(2.0 / math.pi)
GELU_A = 0.044715

f32 = jnp.float32
bf16 = jnp.bfloat16
NN = (((1,), (0,)), ((), ()))
NT = (((1,), (1,)), ((), ()))
TN = (((0,), (0,)), ((), ()))
VMEM_LIMIT = 12 * 1024 * 1024


def dot(a, b, dims=NN):
    return lax.dot_general(a, b, dims, preferred_element_type=f32)


SMALL = pl.CostEstimate(flops=1000, bytes_accessed=1000, transcendentals=0)


def params(*semantics, limit=VMEM_LIMIT):
    return pltpu.CompilerParams(dimension_semantics=semantics or None, vmem_limit_bytes=limit)


def to_column(vec):
    n = vec.shape[1]
    return jnp.broadcast_to(vec, (8, n)).T[:, :1]


def swap_lanes(x):
    half = x.shape[1] // 2
    return jnp.concatenate([x[:, half:], x[:, :half]], axis=1)


def swap_rows(x):
    half = x.shape[0] // 2
    return jnp.concatenate([x[half:], x[:half]], axis=0)


def in_vmem(x):
    return pltpu.with_memory_space_constraint(x, pltpu.VMEM)


def in_hbm(x):
    return pltpu.with_memory_space_constraint(x, pltpu.HBM)


def full(shape):
    return pl.BlockSpec(shape, lambda *_: (0,) * len(shape))


def head_kernel(emb, pairing, w_in, w_out, pre, hid, raw, views, views_t, pos, scratch):
    step = pl.program_id(0)
    rows = emb.shape[0]
    pre_act = dot(emb[...], w_in[...])
    pre[...] = pre_act
    t = jnp.tanh(GELU_K * (pre_act + GELU_A * (pre_act * pre_act * pre_act)))
    hidden = (0.5 * pre_act * (1.0 + t)).astype(bf16)
    hid[...] = hidden
    raw_out = dot(hidden, w_out[...])
    raw[...] = raw_out
    inv = lax.rsqrt(jnp.sum(raw_out * raw_out, axis=1, keepdims=True) + norm_eps)
    scratch[pl.ds(pl.multiple_of(step * rows, rows), rows), :] = (raw_out * inv).astype(bf16)

    @pl.when(step == pl.num_programs(0) - 1)
    def _():
        mate = pairing[...]
        n = mate.shape[1]
        lane = lax.broadcasted_iota(jnp.int32, (1, n), 1)
        first = lane < mate
        low = jnp.minimum(lane, mate)
        sub = lax.broadcasted_iota(jnp.int32, (n, n), 0)
        before = jnp.where(sub < low, 1.0, 0.0).astype(bf16)
        first8 = jnp.broadcast_to(jnp.where(first, 1.0, 0.0), (8, n)).astype(bf16)
        rank = dot(first8, before)[:1].astype(jnp.int32)
        place = jnp.where(first, rank, rank + n // 2)
        pos[...] = place
        move = jnp.where(sub == place, 1.0, 0.0).astype(bf16)
        ordered = dot(move, scratch[...])
        views[...] = ordered.astype(bf16)
        views_t[...] = ordered.T.astype(bf16)


def head(embeddings, pairing, w_in, w_out):
    rows, wide = embeddings.shape
    hidden = w_in.shape[1]
    depth = w_out.shape[1]
    steps = 4
    block = rows // steps
    return pl.pallas_call(
        head_kernel,
        grid=(steps,),
        in_specs=[
            pl.BlockSpec((block, wide), lambda i: (i, 0)),
            full((1, rows)),
            full((wide, hidden)),
            full((hidden, depth)),
        ],
        out_specs=[
            pl.BlockSpec((block, hidden), lambda i: (i, 0)),
            pl.BlockSpec((block, hidden), lambda i: (i, 0)),
            pl.BlockSpec((block, depth), lambda i: (i, 0)),
            full((rows, depth)),
            full((depth, rows)),
            full((1, rows)),
        ],
        out_shape=[
            pltpu.HBM((rows, hidden), f32),
            pltpu.HBM((rows, hidden), bf16),
            pltpu.HBM((rows, depth), f32),
            jax.ShapeDtypeStruct((rows, depth), bf16),
            jax.ShapeDtypeStruct((depth, rows), bf16),
            jax.ShapeDtypeStruct((1, rows), jnp.int32),
        ],
        scratch_shapes=[pltpu.VMEM((rows, depth), bf16)],
        compiler_params=params("arbitrary"),
        name="head",
    )(in_hbm(embeddings), in_hbm(pairing.reshape(1, rows)), in_hbm(w_in), in_hbm(w_out))


def unit_of(protos):
    proto_f = protos.astype(f32)
    inv = lax.rsqrt(jnp.sum(proto_f * proto_f, axis=1, keepdims=True) + norm_eps)
    return proto_f, inv, proto_f * inv


WHOLE = pl.BlockSpec(memory_space=pltpu.VMEM)


def scaled_pair(x, axis):
    wide = x.astype(f32) * EXP2_SCALE
    hi = wide.astype(bf16)
    lo = (wide - hi.astype(f32)).astype(bf16)
    return jnp.concatenate([hi, lo], axis=axis)


def first_kernel(block, chunk, tile, views, protos, expo, col, tot, pair, stage, tot_acc):
    rows, depth = views.shape
    width = protos.shape[0]
    tot_acc[...] = jnp.zeros_like(tot_acc)
    pair[...] = scaled_pair(views[...], 1)

    def one(j, carry):
        here = pl.ds(pl.multiple_of(j * block, block), block)
        _, _, unit = unit_of(protos[here, :])
        unit16 = unit.astype(bf16)
        twice = jnp.concatenate([unit16, unit16], axis=1)
        running = jnp.zeros((8, block), f32)
        for c in range(rows // chunk):
            stage[c % 2] = dot(pair[c * chunk : (c + 1) * chunk, :], twice, NT)
            for start in range(0, chunk, tile):
                part = slice(c * chunk + start, c * chunk + start + tile)
                soft = jnp.exp2(stage[c % 2, start : start + tile, :])
                hard = soft * soft
                expo[part, here] = hard.astype(bf16)
                lanes = soft[:, :128]
                for k in range(1, block // 128):
                    lanes = lanes + soft[:, k * 128 : (k + 1) * 128]
                tot_acc[part, :] += lanes
                for k in range(0, tile, 8):
                    running = running + hard[k : k + 8]
        col[:, here] = jnp.sum(running, axis=0, keepdims=True)
        return carry

    lax.fori_loop(0, width // block, one, 0)
    tot[...] = jnp.sum(tot_acc[...].T, axis=0, keepdims=True)


def first_pass(views, protos):
    rows, depth = views.shape
    width = protos.shape[0]
    block = min(512, width)
    chunk = min(256, rows)
    tile = min(32, chunk)
    return pl.pallas_call(
        functools.partial(first_kernel, block, chunk, tile),
        in_specs=[WHOLE] * 2,
        out_specs=[WHOLE] * 3,
        out_shape=[
            pltpu.VMEM((rows, width), bf16),
            jax.ShapeDtypeStruct((1, width), f32),
            jax.ShapeDtypeStruct((1, rows), f32),
        ],
        scratch_shapes=[
            pltpu.VMEM((rows, 2 * depth), bf16),
            pltpu.VMEM((2, chunk, block), f32),
            pltpu.VMEM((rows, 128), f32),
        ],
        compiler_params=params(),
        cost_estimate=SMALL,
        name="first_pass",
    )(views, protos)


def sum_parts(parts, width):
    if len(parts[0].shape) == 3:
        parts = [parts[0].at[k] for k in range(parts[0].shape[0])]
    total = parts[0][:, :width]
    for other in parts[1:]:
        total = total + other[:, :width]
    return total


def add_fours(terms):
    total = None
    for k in range(0, len(terms), 4):
        four = terms[k : k + 4]
        while len(four) > 1:
            four = [x + y for x, y in zip(four[::2], four[1::2])]
        part = four[0].astype(f32)
        total = part if total is None else total + part
    return total


def rowsum_tile(expo, here, spread, tall, width):
    terms = []
    total = None
    for k in range(width // 128):
        lanes = slice(k * 128, (k + 1) * 128)
        weight = jnp.concatenate([spread[:, lanes]] * (tall // 16), axis=0)
        terms.append(expo[here, lanes] * weight)
        if len(terms) == 4 or k == width // 128 - 1:
            part = add_fours(terms)
            total = part if total is None else total + part
            terms = []
    return total


def rowsum_kernel(count, expo, *refs):
    parts = refs[:count]
    scale, out, spread, acc = refs[count:]
    rows, width = expo.shape
    inverse = 1.0 / sum_parts(parts, width)
    scale[...] = inverse
    spread[...] = jnp.broadcast_to(inverse, spread.shape).astype(bf16)
    tall = 64

    def one(i, carry):
        here = pl.ds(pl.multiple_of(i * tall, tall), tall)
        acc[here, :] = rowsum_tile(expo, here, spread, tall, width)
        return carry

    lax.fori_loop(0, rows // tall, one, 0)
    out[...] = jnp.sum(acc[...].T, axis=0, keepdims=True)


def rowsum(expo, parts):
    rows, width = expo.shape
    return pl.pallas_call(
        functools.partial(rowsum_kernel, len(parts)),
        in_specs=[WHOLE] * (1 + len(parts)),
        out_specs=[WHOLE] * 2,
        out_shape=[
            jax.ShapeDtypeStruct((1, width), f32),
            jax.ShapeDtypeStruct((1, rows), f32),
        ],
        scratch_shapes=[pltpu.VMEM((16, width), bf16), pltpu.VMEM((rows, 128), f32)],
        compiler_params=params(),
        cost_estimate=SMALL,
        name="rowsum",
    )(in_vmem(expo), *parts)


def split_rows(vec):
    hi = vec.astype(bf16).astype(f32)
    n = vec.shape[1]
    row = lax.broadcasted_iota(jnp.int32, (8, n), 0)
    hi8 = jnp.broadcast_to(hi, (8, n))
    lo8 = jnp.broadcast_to(vec - hi, (8, n))
    return jnp.where(row == 0, hi8, jnp.where(row == 1, lo8, 0.0))


def rowsum_last_kernel(pieces, count, *refs):
    expos = refs[:pieces]
    parts = refs[pieces : pieces + count]
    unit_t, scale, out, code, acc = refs[pieces + count :]
    step = pl.program_id(0)
    depth, block = unit_t.shape
    deep = expos[0].shape[1]
    inverse = 1.0 / sum_parts(parts, block)
    scale[...] = inverse

    @pl.when(step == 0)
    def _():
        acc[...] = jnp.zeros_like(acc)

    for k in range(pieces):
        here = slice(k * deep, (k + 1) * deep)
        scaled = unit_t[:, here].astype(f32) * inverse[:, here]
        pad = jnp.zeros((depth - 8, deep), f32)
        weights = jnp.concatenate([scaled, split_rows(inverse[:, here]), pad], axis=0)
        acc[...] += dot(expos[k][...], weights.astype(bf16), NT)

    @pl.when(step == pl.num_programs(0) - 1)
    def _():
        sums = acc[:, depth:].T
        out[...] = sums[0:1] + sums[1:2]
        code[...] = acc[:, :depth]


def rowsum_last(expo, parts, unit_t):
    rows, width = expo.shape
    depth = unit_t.shape[0]
    block = min(1024, width)
    pieces = 2
    deep = block // pieces
    vec = pl.BlockSpec((1, block), lambda j: (0, j))
    return pl.pallas_call(
        functools.partial(rowsum_last_kernel, pieces, len(parts)),
        grid=(width // block,),
        in_specs=[
            pl.BlockSpec((rows, deep), lambda j, k=k: (0, j * pieces + k)) for k in range(pieces)
        ]
        + [vec] * len(parts)
        + [pl.BlockSpec((depth, block), lambda j: (0, j))],
        out_specs=[vec, full((1, rows)), full((rows, depth))],
        out_shape=[
            jax.ShapeDtypeStruct((1, width), f32),
            jax.ShapeDtypeStruct((1, rows), f32),
            jax.ShapeDtypeStruct((rows, depth), f32),
        ],
        scratch_shapes=[pltpu.VMEM((rows, 2 * depth), f32)],
        compiler_params=params("arbitrary", limit=VMEM_LIMIT + 4 * 1024 * 1024),
        cost_estimate=SMALL,
        name="rowsum_last",
    )(*[in_hbm(expo)] * pieces, *parts, in_hbm(unit_t))


def unit_t_kernel(block, lead, protos, *refs):
    out = refs[-1]

    def one(j, carry):
        here = pl.ds(pl.multiple_of(lead + j * block, block), block)
        _, _, unit = unit_of(protos[here, :])
        out[:, here] = unit.astype(bf16).astype(f32).T.astype(bf16)
        return carry

    lax.fori_loop(0, protos.shape[0] // 2 // block, one, 0)


def unit_transposed(protos, *before):
    width, depth = protos.shape
    lead = width // 2 if before else 0
    return pl.pallas_call(
        functools.partial(unit_t_kernel, min(512, width // 2), lead),
        in_specs=[WHOLE] * (1 + len(before)),
        out_specs=WHOLE,
        out_shape=jax.ShapeDtypeStruct((depth, width), bf16),
        input_output_aliases={1: 0} if before else {},
        compiler_params=params(),
        cost_estimate=SMALL,
        name="unit_t",
    )(protos, *before)


def colsum_kernel(count, expo, *refs):
    parts = refs[:count]
    rest = refs[count:]
    out, spread = rest[-2:]
    rows, width = expo.shape
    inverse = 1.0 / sum_parts(parts, rows)
    spread[...] = jnp.broadcast_to(inverse, (128, rows)).T.astype(bf16)
    block = min(512, width)

    def one(j, carry):
        here = pl.ds(pl.multiple_of(j * block, block), block)
        running = jnp.zeros((16, block), f32)
        for i in range(0, rows // 16, 4):
            terms = []
            for k in range(i, min(i + 4, rows // 16)):
                part = slice(k * 16, (k + 1) * 16)
                weight = jnp.concatenate([spread[part, :]] * (block // 128), axis=1)
                terms.append(expo[part, here] * weight)
            running = running + add_fours(terms)
        total = jnp.sum(running, axis=0, keepdims=True)
        for k in range(out.shape[0]):
            out[k, :, here] = total
        return carry

    lax.fori_loop(0, width // block, one, 0)
    if len(rest) > 2:
        for k in range(out.shape[0]):
            out[k, :, width:] = rest[0][...]


def colsum(expo, parts, copies=1, behind=()):
    rows, width = expo.shape
    long = width + sum(x.shape[1] for x in behind)
    return pl.pallas_call(
        functools.partial(colsum_kernel, len(parts)),
        in_specs=[WHOLE] * (1 + len(parts) + len(behind)),
        out_specs=WHOLE,
        out_shape=jax.ShapeDtypeStruct((copies, 1, long), f32),
        scratch_shapes=[pltpu.VMEM((rows, 128), bf16)],
        compiler_params=params(),
        cost_estimate=SMALL,
        name="colsum",
    )(in_vmem(expo), *parts, *behind)


def proto_first_kernel(chunk, tile, lead, place, protos, views, totals, expo, grad, *scratch):
    weights, twice, pair, stage, soft16, acc = scratch
    count = expo.shape[1] // views.shape[2]
    _, depth, rows = views.shape
    width = protos.shape[0]
    _, _, unit = unit_of(protos[...])
    pair[...] = scaled_pair(unit.astype(bf16), 1)
    for n in range(count):
        k = lead + n
        weights[...] = (views[k].astype(f32) * (GRAD_SCALE / totals[place[0] ^ k])).astype(bf16)
        twice[:depth, :] = views[k]
        twice[depth:, :] = views[k]
        for c in range(width // chunk):
            stage[c % 2] = dot(pair[c * chunk : (c + 1) * chunk, :], twice[...])
            for start in range(0, chunk, tile):
                part = slice(c * chunk + start, c * chunk + start + tile)
                soft = jnp.exp2(stage[c % 2, start : start + tile, :])
                soft16[part, :] = soft.astype(bf16)
                expo[part, n * rows : (n + 1) * rows] = (soft * soft).astype(bf16)
        found = dot(soft16[...], weights[...], NT)
        if n == 0:
            acc[...] = found
        else:
            acc[...] += found
    grad[...] = acc[...]


def proto_first(place, protos, views, totals, lead, count):
    width, depth = protos.shape
    rows = views.shape[2]
    chunk = min(256, width)
    tile = min(16, chunk)
    return pl.pallas_call(
        functools.partial(proto_first_kernel, chunk, tile, lead),
        in_specs=[pl.BlockSpec(memory_space=pltpu.SMEM)] + [WHOLE] * 3,
        out_specs=[WHOLE] * 2,
        out_shape=[
            pltpu.VMEM((width, count * rows), bf16),
            jax.ShapeDtypeStruct((width, depth), f32),
        ],
        scratch_shapes=[
            pltpu.VMEM((depth, rows), bf16),
            pltpu.VMEM((2 * depth, rows), bf16),
            pltpu.VMEM((width, 2 * depth), bf16),
            pltpu.VMEM((2, chunk, rows), f32),
            pltpu.VMEM((width, rows), bf16),
            pltpu.VMEM((width, depth), f32),
        ],
        compiler_params=params(),
        cost_estimate=SMALL,
        name="proto_first",
    )(place, protos, views, totals)


def proto_last_kernel(groups, place, *refs):
    expos, grads = refs[:groups], refs[groups : 2 * groups]
    scale, protos, views, totals, out, weights, acc = refs[2 * groups :]
    count, depth, rows = views.shape
    each = count // groups
    for k in range(count):
        mates = swap_lanes(views[k])
        weights[...] = (mates.astype(f32) * (GRAD_SCALE / totals[place[0] ^ k])).astype(bf16)
        found = dot(expos[k // each][:, (k % each) * rows : (k % each + 1) * rows], weights[...], NT)
        if k == 0:
            acc[...] = found
        else:
            acc[...] += found
    width = protos.shape[0]
    there = pl.ds(pl.multiple_of(place[0] * width, width), width)
    unit_grad = grads[0][...]
    for other in grads[1:]:
        unit_grad = unit_grad + other[...]
    unit_grad = unit_grad - to_column(scale[:, there]) * acc[...]
    proto_f, inv, _ = unit_of(protos[...])
    inner = jnp.sum(proto_f * unit_grad, axis=1, keepdims=True)
    out[...] = (inv * unit_grad - proto_f * (inv * inv * inv) * inner).astype(bf16)


def proto_last(place, expos, grads, scale, protos, views, totals):
    width, depth = protos.shape
    rows = views.shape[2]
    groups = len(expos)
    return pl.pallas_call(
        functools.partial(proto_last_kernel, groups),
        in_specs=[pl.BlockSpec(memory_space=pltpu.SMEM)] + [WHOLE] * (2 * groups + 4),
        out_specs=WHOLE,
        out_shape=jax.ShapeDtypeStruct((width, depth), bf16),
        scratch_shapes=[pltpu.VMEM((depth, rows), bf16), pltpu.VMEM((width, depth), f32)],
        compiler_params=params(),
        name="proto_last",
    )(place, *[in_vmem(x) for x in expos], *grads, scale, protos, views, totals)


def view_soft_kernel(block, tile, lead, views, protos, out, pair, stage, soft16):
    rows, depth = views.shape
    pair[...] = scaled_pair(views[...], 1)
    out[...] = jnp.zeros_like(out)
    chunk = stage.shape[1]

    def one(j, carry):
        here = pl.ds(pl.multiple_of(lead + j * block, block), block)
        _, _, unit = unit_of(protos[here, :])
        unit16 = unit.astype(bf16)
        twice = jnp.concatenate([unit16, unit16], axis=1)
        for c in range(rows // chunk):
            stage[c % 2] = dot(pair[c * chunk : (c + 1) * chunk, :], twice, NT)
            for start in range(0, chunk, tile):
                part = slice(c * chunk + start, c * chunk + start + tile)
                soft16[part, :] = jnp.exp2(stage[c % 2, start : start + tile, :]).astype(bf16)
        out[...] += dot(soft16[...], unit16)
        return carry

    return one


def view_soft_body(block, tile, lead, count, *refs):
    lax.fori_loop(0, count // block, view_soft_kernel(block, tile, lead, *refs), 0)


def view_soft(views, protos, lead, count):
    rows, depth = views.shape
    block = min(512, count)
    chunk = min(256, rows)
    return pl.pallas_call(
        functools.partial(view_soft_body, block, min(32, chunk), lead, count),
        in_specs=[WHOLE] * 2,
        out_specs=WHOLE,
        out_shape=jax.ShapeDtypeStruct((rows, depth), f32),
        scratch_shapes=[
            pltpu.VMEM((rows, 2 * depth), bf16),
            pltpu.VMEM((2, chunk, block), f32),
            pltpu.VMEM((rows, block), bf16),
        ],
        compiler_params=params(),
        cost_estimate=SMALL,
        name="view_soft",
    )(views, protos)


def view_grad_kernel(code, tot, total, *refs):
    softs, out = refs[:-1], refs[-1]
    soft = softs[0][...]
    for other in softs[1:]:
        soft = soft + other[...]
    soft = soft * to_column(GRAD_SCALE / tot[...])
    hard = swap_rows(code[...] * to_column(GRAD_SCALE / total[...]))
    out[...] = (soft - hard).astype(out.dtype)


def view_grad_part(code, tot, total, *softs):
    operands = [code, tot, total, *softs]
    return pl.pallas_call(
        view_grad_kernel,
        grid=(1,),
        in_specs=[full(x.shape) for x in operands],
        out_specs=full(code.shape),
        out_shape=jax.ShapeDtypeStruct(code.shape, bf16),
        compiler_params=params("arbitrary"),
        cost_estimate=SMALL,
        name="view_grad",
    )(code, tot, total, *[in_hbm(x) for x in softs])


def backward_kernel(share, turn, grad_a, grad_b, pos, raw, pre, emb, hid, w_out, out, g_all):
    total = grad_a[...].astype(f32) + grad_b[...].astype(f32)
    n, depth = raw.shape
    place = jnp.broadcast_to(pos[...].astype(f32), (8, n)).T[:, :1].astype(jnp.int32)
    lane = lax.broadcasted_iota(jnp.int32, (n, n), 1)
    move = jnp.where(lane == place, 1.0, 0.0).astype(bf16)
    hi = total.astype(bf16)
    lo = (total - hi.astype(f32)).astype(bf16)
    moved = dot(move, jnp.concatenate([hi, lo], axis=1))
    grad = moved[:, :depth] + moved[:, depth:]
    raw_out = raw[...]
    inv = lax.rsqrt(jnp.sum(raw_out * raw_out, axis=1, keepdims=True) + norm_eps)
    inner = jnp.sum(raw_out * grad, axis=1, keepdims=True)
    d_raw = (inv * grad - raw_out * (inv * inv * inv) * inner).astype(bf16)
    g_all[...] = dot(hid[...], d_raw, TN)
    d_hidden = dot(d_raw, w_out[...], NT)
    v = pre[...]
    t = jnp.tanh(GELU_K * (v + GELU_A * (v * v * v)))
    slope = 0.5 * (1.0 + t) + (0.5 * GELU_K) * v * (1.0 - t * t) * (1.0 + (3.0 * GELU_A) * (v * v))
    d_pre = (slope * d_hidden).astype(bf16)
    g_in = dot(emb[...], d_pre, TN)
    count = out.shape[0]
    tall, wide = g_in.shape[0] // count, g_in.shape[1]
    base, short = tall * (wide // 128), share // count
    for k in range(count):
        n = mirrored(k, count)
        for q in range(wide // 128):
            out[n, q * tall : (q + 1) * tall, :] = g_in[
                k * tall : (k + 1) * tall, q * 128 : (q + 1) * 128
            ]
        low = pl.multiple_of(turn[0] * share + k * short, short)
        out[n, base : base + short, :] = g_all[pl.ds(low, short), :]


def mirrored(k, count):
    found = 0
    while count > 1:
        found = found * 2 + k % 2
        k //= 2
        count //= 2
    return found


def backward(nb, npr, turn, grad_a, grad_b, pos, raw, pre, emb, hid, w_out):
    rows, wide = emb.shape
    hidden, depth = w_out.shape
    part = wide // npr
    share = hidden // npr
    lines = (part * hidden + share * depth) // (nb * 128)
    operands = [grad_a, grad_b, pos, raw, pre, emb, hid, w_out]
    specs = [full(x.shape) for x in operands]
    specs[5] = pl.BlockSpec((rows, part), lambda i, turn: (0, turn[0]))
    return pl.pallas_call(
        functools.partial(backward_kernel, share),
        grid_spec=pltpu.PrefetchScalarGridSpec(
            num_scalar_prefetch=1,
            grid=(1,),
            in_specs=specs,
            out_specs=full((nb, lines, 128)),
            scratch_shapes=[pltpu.VMEM((hidden, depth), f32)],
        ),
        out_shape=jax.ShapeDtypeStruct((nb, lines, 128), f32),
        compiler_params=params("arbitrary"),
        name="backward",
    )(turn, grad_a, grad_b, pos, *[in_hbm(x) for x in operands[3:]])


def unpack_kernel(order, order_b, place, *refs):
    pieces, (g_in, g_out) = refs[:-2], refs[-2:]
    nb = len(order_b)
    npr = len(order)
    tall, wide = g_in.shape[0] // (nb * npr), g_in.shape[1]
    base, short = tall * (wide // 128), g_out.shape[0] // (nb * npr)
    half = pieces[0].shape[0]
    for n, flip in enumerate(order):
        for k, flip_b in enumerate(order_b):
            owner = (place[0] ^ flip) * nb + (place[1] ^ flip_b)
            x = pieces[n // half][n % half, k].astype(f32)
            low = pl.multiple_of(owner * tall, tall)
            for q in range(wide // 128):
                g_in[pl.ds(low, tall), q * 128 : (q + 1) * 128] = x[q * tall : (q + 1) * tall]
            low = pl.multiple_of(owner * short, short)
            g_out[pl.ds(low, short), :] = x[base : base + short]


def unpack(order, order_b, place, pieces, shape_in, shape_out):
    return pl.pallas_call(
        functools.partial(unpack_kernel, order, order_b),
        in_specs=[pl.BlockSpec(memory_space=pltpu.SMEM)] + [WHOLE] * len(pieces),
        out_specs=[WHOLE] * 2,
        out_shape=[jax.ShapeDtypeStruct(shape_in, f32), jax.ShapeDtypeStruct(shape_out, f32)],
        compiler_params=params(),
        name="unpack",
    )(place, *pieces)


def widen_kernel(x, out, narrow, wide, came, went):
    count, rows, _ = narrow.shape
    ins = [
        pltpu.make_async_copy(x.at[pl.ds(k * rows, rows)], narrow.at[k], came.at[k])
        for k in range(count)
    ]
    outs = [
        pltpu.make_async_copy(wide.at[k], out.at[pl.ds(k * rows, rows)], went.at[k])
        for k in range(count)
    ]
    for copy in ins:
        copy.start()
    for k in range(count):
        ins[k].wait()
        wide[k] = narrow[k].astype(f32)
        outs[k].start()
    for copy in outs:
        copy.wait()


def widen(x):
    rows, depth = x.shape
    count = 8
    block = rows // count
    return pl.pallas_call(
        widen_kernel,
        in_specs=[pl.BlockSpec(memory_space=pl.ANY)],
        out_specs=pl.BlockSpec(memory_space=pl.ANY),
        out_shape=jax.ShapeDtypeStruct((rows, depth), f32),
        scratch_shapes=[
            pltpu.VMEM((count, block, depth), bf16),
            pltpu.VMEM((count, block, depth), f32),
            pltpu.SemaphoreType.DMA((count,)),
            pltpu.SemaphoreType.DMA((count,)),
        ],
        compiler_params=params(),
        name="widen",
    )(in_hbm(x))


def stages(size, first=1):
    found, step = ([[1]], 2) if first == 1 else ([], 1)
    while step < size:
        if step * 2 < size:
            found.append([step, step * 2, step * 3])
            step *= 4
        else:
            found.append([step])
            step *= 2
    return found


def body(nb, npr, embeddings, pairing, w_in, w_out, prototypes):
    b = lax.axis_index("batch")
    p = lax.axis_index("proto")
    rows, wide = embeddings.shape
    width, depth = prototypes.shape
    hidden_n = w_in.shape[1]
    own = width // nb

    def flipped(x, axis, size, step):
        return lax.ppermute(x, axis, [(i, i ^ step) for i in range(size)])

    def trade(x, axis, size, steps, queue=(), results=None):
        others = [flipped(x, axis, size, step) for step in steps]
        work = queue.pop(0) if queue else None
        if work:
            operands, _ = lax.optimization_barrier((work[1], x))
            others, found = lax.optimization_barrier((others, work[0](*operands)))
            results.append(found)
        return others

    def summed(x, axis, size, queue=(), results=None):
        rounds = stages(size, 1 if axis == "batch" else 2)
        for n, steps in enumerate(rounds):
            others = trade(x, axis, size, steps, queue, results)
            if n == len(rounds) - 1:
                return [x, *others]
            for other in others:
                x = x + other

    pre, hid, raw, views, views_t, pos = head(embeddings, pairing, w_in, w_out)
    views_all = lax.all_gather(views_t, "batch", axis=0)
    protos_own = lax.dynamic_slice_in_dim(prototypes, b * own, own, 0)
    place = b.astype(jnp.int32).reshape(1)
    turn_p = p.astype(jnp.int32).reshape(1)
    views, protos_own, place, turn_p = lax.optimization_barrier(
        (views, protos_own, place, turn_p)
    )
    expo, col, tot = first_pass(views, prototypes)

    groups = 4
    cols = width // groups
    softs = []
    queue = [
        (functools.partial(view_soft, lead=k * cols, count=cols), (views, prototypes))
        for k in range(groups)
    ]
    scale, row = rowsum(expo, summed(col, "batch", nb, queue, softs))
    rest = len(stages(npr, 2)) - 1
    queue = [None] * rest + queue
    both = sum(summed(jnp.concatenate([row, tot], axis=0), "proto", npr, queue, softs))
    totals, tot = [both[:1]], both[1:]

    def unit_half(protos):
        return unit_transposed(protos, *taken)

    taken = []
    halves = [(unit_half, (prototypes,))] * 2
    col = colsum(expo, totals)[0]
    tot_all = tot[None]
    rounds = stages(nb)
    for n, steps in enumerate(rounds):
        others = [flipped(tot_all, "batch", nb, step) for step in steps]
        parts = trade(col, "batch", nb, steps, halves, taken)
        others, parts = lax.optimization_barrier((others, parts))
        tot_all = jnp.concatenate([tot_all, *others], axis=0)
        if n < len(rounds) - 1:
            for part in parts:
                col = col + part
    scale, row = rowsum(expo, [col, *parts])
    queue = [None] * rest + queue
    col = colsum(expo, summed(row, "proto", npr, queue, softs))[0]
    for left, results in ((halves, taken), (queue, softs)):
        results.extend(work[0](*work[1]) for work in left if work)
    unit_t = taken[-1]

    col, views_all = lax.optimization_barrier((col, views_all))
    each = nb // groups
    owns = []
    queue = [
        (
            functools.partial(proto_first, lead=k * each, count=each),
            (place, protos_own, views_all, tot_all),
        )
        for k in range(groups)
    ]
    scale, row, code = rowsum_last(expo, summed(col, "batch", nb, queue, owns), unit_t)
    queue = [None] * rest + queue
    total = sum(summed(row, "proto", npr, queue, owns))
    total_all = total[None]
    grads = []
    queue = [(view_grad_part, (code, tot, total, *softs))] + queue
    turn = 1
    for steps in stages(nb):
        others = trade(total_all, "batch", nb, steps, queue, grads if not grads else owns)
        if len(grads) > 1:
            grads = [(grads[0].astype(f32) + grads[1].astype(f32)).astype(bf16)]
            others[0], grads[0] = lax.optimization_barrier((others[0], grads[0]))
        if turn * 2 < npr:
            turn *= 2
            grads = [grads[0], flipped(grads[0], "proto", npr, npr // turn)]
        total_all = jnp.concatenate([total_all, *others], axis=0)

    while turn * 2 < npr:
        if len(grads) > 1:
            grads = [(grads[0].astype(f32) + grads[1].astype(f32)).astype(bf16)]
        turn *= 2
        grads = [grads[0], flipped(grads[0], "proto", npr, npr // turn)]
    if len(grads) > 1:
        grads = [(grads[0].astype(f32) + grads[1].astype(f32)).astype(bf16)]
    expos, parts = [x for x, _ in owns], [x for _, x in owns]
    queue = [(proto_last, (place, expos, parts, scale, protos_own, views_all, total_all))]
    found = []
    grads = [grads[0], *trade(grads[0], "proto", npr, [1], queue, found)]
    grad_proto = lax.all_gather(found[0], "batch", axis=0, tiled=True)
    both = backward(nb, npr, turn_p, *grads, pos, raw, pre, embeddings, hid, w_out)
    for steps in stages(nb):
        count = len(steps) + 1
        share = both.shape[0] // count
        mine = (b // steps[0]) % 2
        if count == 4:
            mine = mine * 2 + (b // steps[1]) % 2
        kept = lax.dynamic_slice_in_dim(both, mine * share, share, 0)
        for flip, step in zip([1] if count == 2 else [2, 1, 3], steps):
            away = lax.dynamic_slice_in_dim(both, (mine ^ flip) * share, share, 0)
            kept = kept + flipped(away.astype(bf16), "batch", nb, step).astype(f32)
        both = kept
    piece = both.astype(bf16)
    order_b = [0]
    for steps in reversed(stages(nb)):
        piece = jnp.concatenate(
            [piece, *[flipped(piece, "batch", nb, step) for step in steps]], axis=0
        )
        order_b = order_b + [i ^ step for step in steps for i in order_b]
    piece = piece[None]
    order = [0]
    step = npr // 2
    while step > 1:
        piece = jnp.concatenate([piece, flipped(piece, "proto", npr, step)], axis=0)
        order = order + [i ^ step for i in order]
        step //= 2
    pieces = [piece, flipped(piece, "proto", npr, 1)]
    order = order + [i ^ 1 for i in order]
    places = jnp.stack([p, b]).astype(jnp.int32)
    grad_in, grad_out = unpack(
        order, order_b, places, pieces, (wide, hidden_n), (hidden_n, depth)
    )
    return (grad_in, grad_out, widen(grad_proto))


def solution(mesh):
    return jax.shard_map(
        functools.partial(body, mesh.shape["batch"], mesh.shape["proto"]),
        mesh=mesh,
        in_specs=(P("batch", None), P("batch"), P(), P(), P("proto", None)),
        out_specs=(P(), P(), P("proto", None)),
        check_vma=False,
    )
```
